32 devices in a mesh: stream: 2 (over x), dp: 16 (over z, y, core).
Axes of the slice: x: 2, y: 2, z: 4, core: 2. Of those that a mesh axis runs over, the one named last changes fastest.
Arguments:
- tokens_in: bfloat16 [32, 1024, 768], P('dp', 'stream'), may hold values from -6 to 6
- char_ids: int32 [32, 4096], P('dp'), may hold values from 0 to 255
- char_lengths: int32 [32, 1024], P('dp'), may hold values from 1 to 8, 4096 in all within a row
- out_grad: bfloat16 [32, 1024, 768], P('dp', 'stream'), may hold values from -6 to 6
- w_qkv: float32 [768, 2304], P(('stream', 'dp')), may hold values from -0.21875 to 0.21875
- first_qkv: float32 [768, 2304], P(('stream', 'dp')), may hold values from -640 to 640
- second_qkv: float32 [768, 2304], P(('stream', 'dp')), may hold values from 5898.24 to 95027.2
- w_out: float32 [768, 768], P(('stream', 'dp')), may hold values from -4 to 4
- first_out: float32 [768, 768], P(('stream', 'dp')), may hold values from -32 to 32
- second_out: float32 [768, 768], P(('stream', 'dp')), may hold values from 12.8 to 208
- w_up: float32 [768, 3072], P(('stream', 'dp')), may hold values from -0.21875 to 0.21875
- first_up: float32 [768, 3072], P(('stream', 'dp')), may hold values from -224 to 224
- second_up: float32 [768, 3072], P(('stream', 'dp')), may hold values from 655.36 to 10485.76
- w_down: float32 [3072, 768], P(('stream', 'dp')), may hold values from -0.109375 to 0.109375
- first_down: float32 [3072, 768], P(('stream', 'dp')), may hold values from -448 to 448
- second_down: float32 [3072, 768], P(('stream', 'dp')), may hold values from 2621.44 to 41943.04
- w_gru: float32 [768, 1536], P(('stream', 'dp')), may hold values from -0.21875 to 0.21875
- first_gru: float32 [768, 1536], P(('stream', 'dp')), may hold values from -112 to 112
- second_gru: float32 [768, 1536], P(('stream', 'dp')), may hold values from 163.84 to 2621.44
- w_blend: float32 [4608, 768], P(('stream', 'dp')), may hold values from -0.09375 to 0.09375
- first_blend: float32 [4608, 768], P(('stream', 'dp')), may hold values from -384 to 384
- second_blend: float32 [4608, 768], P(('stream', 'dp')), may hold values from 1966.08 to 32112.64
- char_table: float32 [256, 768], P(('stream', 'dp')), may hold values from -5 to 5
- first_table: float32 [256, 768], P(('stream', 'dp')), may hold values from -10 to 10
- second_table: float32 [256, 768], P(('stream', 'dp')), may hold values from 1.28 to 20.48
- gains: float32 [3, 768], P(None, ('stream', 'dp')), may hold values from 0.5 to 1.5
- first_gains: float32 [3, 768], P(None, ('stream', 'dp')), may hold values from -896 to 896
- second_gains: float32 [3, 768], P(None, ('stream', 'dp')), may hold values from 10485.76 to 167116.8
Outputs:
- block_out: bfloat16 [32, 1024, 768], P('dp', 'stream')
- tokens_grad: bfloat16 [32, 1024, 768], P('dp', 'stream')
- fresh_qkv: float32 [768, 2304], P(('stream', 'dp'))
- mean_qkv: float32 [768, 2304], P(('stream', 'dp'))
- power_qkv: float32 [768, 2304], P(('stream', 'dp'))
- fresh_out: float32 [768, 768], P(('stream', 'dp'))
- mean_out: float32 [768, 768], P(('stream', 'dp'))
- power_out: float32 [768, 768], P(('stream', 'dp'))
- fresh_up: float32 [768, 3072], P(('stream', 'dp'))
- mean_up: float32 [768, 3072], P(('stream', 'dp'))
- power_up: float32 [768, 3072], P(('stream', 'dp'))
- fresh_down: float32 [3072, 768], P(('stream', 'dp'))
- mean_down: float32 [3072, 768], P(('stream', 'dp'))
- power_down: float32 [3072, 768], P(('stream', 'dp'))
- fresh_gru: float32 [768, 1536], P(('stream', 'dp'))
- mean_gru: float32 [768, 1536], P(('stream', 'dp'))
- power_gru: float32 [768, 1536], P(('stream', 'dp'))
- fresh_blend: float32 [4608, 768], P(('stream', 'dp'))
- mean_blend: float32 [4608, 768], P(('stream', 'dp'))
- power_blend: float32 [4608, 768], P(('stream', 'dp'))
- fresh_table: float32 [256, 768], P(('stream', 'dp'))
- mean_table: float32 [256, 768], P(('stream', 'dp'))
- power_table: float32 [256, 768], P(('stream', 'dp'))
- fresh_gains: float32 [3, 768], P(None, ('stream', 'dp'))
- mean_gains: float32 [3, 768], P(None, ('stream', 'dp'))
- power_gains: float32 [3, 768], P(None, ('stream', 'dp'))
The draws below stay inside these ranges and needn't reach their ends.
Inputs may be any that keep to these rules, and one draw needn't show every extreme that they name: `char_lengths`: the 1024 lengths of a sequence sum to 4096, and one of them is 8.
All inputs are finite; a program needn't handle non-finite values.
Results may differ from the reference program's by a relative error of at most 0.017.
The reference program's roundings to bfloat16 on the way count: a program that leaves them out, or rounds other values in their place, can miss the bound.
Values may be sent and summed in bfloat16 or wider, within the bound.
No kernel may reach another device: no remote copies, remote signals or barrier semaphores. Data moves between devices by JAX's collectives and lax.ppermute only.
A program may use at most 320 MiB of HBM per device.

```python
import math
import jax
import jax.numpy as jnp
import numpy as np
from jax import lax

D = 768
HEADS = 12
FF = 3072
HID = 384
CV = 256
LEN = 1024
MOSTC = 8
STEP = 5
CHARS = 4096
SEQS = 32


def set_ends(entries, key, low, high):
    index_at = [jax.random.randint(jax.random.fold_in(key, axis), (), 0, length) for axis, length in enumerate(entries.shape)]
    longest = entries.shape.index(max(entries.shape))
    next_to = index_at[:longest] + [(index_at[longest] + 1) % entries.shape[longest]] + index_at[longest + 1:]
    return entries.at[tuple(index_at)].set(low).at[tuple(next_to)].set(high)


def with_spikes(values, rng, source, target, shards_of, factor):
    owner, partner = [(jnp.arange(values.shape[position]) // (values.shape[position] // shards_of)).reshape([-1 if axis == position else 1 for axis in range(values.ndim)]) for position in (source, target)]
    chosen = jax.random.permutation(rng, shards_of)[partner]
    strong = (owner == chosen) | (owner == (partner + shards_of // 2) % shards_of)
    return jnp.where(strong, factor * values, values)


def block_scale(stream_key, extent, split, smallest, high):
    gain, own = 1.0, jax.random.fold_in(stream_key, 6)
    for dim, parts in split:
        steps = jnp.exp(jax.random.uniform(jax.random.fold_in(own, dim), (parts,), jnp.float32, smallest / len(split), high / len(split)))
        gain = gain * jnp.repeat(steps, extent[dim] // parts).reshape([-1 if axis == dim else 1 for axis in range(len(extent))])
    return gain


def cumulative_ranks(amount, lean):
    weights = [(1 << 20) // math.isqrt(grade ** lean) + 1 for grade in range(1, amount + 1)]
    scale = 1 + sum(weights) // (1 << 30)
    return np.cumsum(np.array([max(1, weight // scale) for weight in weights]))


def ranked(own_key, dims, amount, skew):
    grid = cumulative_ranks(amount, skew)
    lot = jax.random.randint(jax.random.fold_in(own_key, 1), dims, 0, int(grid[amount - 1]))
    rank = jnp.searchsorted(jnp.asarray(grid, jnp.int32), lot, side="right")
    return jax.random.permutation(jax.random.fold_in(own_key, 2), amount)[rank].astype(jnp.int32)


def profile(number_of, total, reach, skew):
    portions = [(1 << 20) // math.isqrt(rank ** skew) + 1 for rank in range(2, number_of + 1)]
    spare, counts = total - reach - (number_of - 1), [1] * (number_of - 1)
    while spare > 0:
        candidates = [i for i in range(number_of - 1) if counts[i] < reach]
        pool, remaining = sum([portions[i] for i in candidates]), spare
        for i in candidates:
            extra = min(reach - counts[i], max(1, remaining * portions[i] // pool), spare)
            counts[i] = counts[i] + extra
            spare = spare - extra
    return np.array([reach] + counts)


def uneven(key, count, total, limit, skew):
    if count == 2:
        one = jax.random.randint(key, (), max(1, total - limit), min(limit, total - 1) + 1)
        return jnp.stack([one, total - one])
    sizes = jnp.asarray(profile(count, total, limit, skew), jnp.int32)
    pairs = (count - 1) // 2
    source_of, receiver = sizes[1:1 + 2 * pairs:2], sizes[2:2 + 2 * pairs:2]
    margin = jnp.minimum(source_of - 1, limit - receiver)
    passed = jax.random.randint(jax.random.fold_in(key, 1), (pairs,), 0, 1 << 20) % (margin + 1)
    sizes = sizes.at[1:1 + 2 * pairs:2].set(source_of - passed).at[2:2 + 2 * pairs:2].set(receiver + passed)
    return sizes[jax.random.permutation(jax.random.fold_in(key, 2), count)]


def gaussian(stream_key, extent, scale, reach, cuts=(), dtype=jnp.bfloat16):
    result = scale * jax.random.normal(stream_key, extent, jnp.float32)
    if cuts:
        result = result * block_scale(stream_key, extent, cuts, -0.22, 0.18)
    return jnp.clip(result, -reach, reach).astype(dtype)


def noise_with(rng, extent, scale, most, split, heavy, kind=jnp.bfloat16):
    drawn = scale * jax.random.normal(rng, extent, jnp.float32)
    if split:
        drawn = drawn * block_scale(rng, extent, split, -0.22, 0.18)
    return jnp.clip(with_spikes(drawn, jax.random.fold_in(rng, 3), *heavy), -most, most).astype(kind)


def setup_inputs(seed: int = 0) -> dict:
    splits = jax.random.split(jax.random.key(seed), 29)
    tokens_in = gaussian(splits[0], (SEQS, LEN, D), 1.0, 6.0, ((0, 16), (1, 2)))
    char_ids = set_ends(ranked(splits[1], (SEQS, CHARS), CV, 2), jax.random.fold_in(splits[1], 3), 0, CV - 1).astype(jnp.int32)
    char_lengths = jax.vmap(lambda own: uneven(own, LEN, CHARS, MOSTC, 1))(jax.random.split(splits[2], SEQS)).reshape((SEQS, LEN)).astype(jnp.int32)
    out_grad = noise_with(splits[3], (SEQS, LEN, D), 1.0, 6.0, ((0, 16), (1, 2)), (0, 2, 16, 2.0))
    w_qkv = gaussian(splits[4], (D, 3 * D), D ** -0.5, 0.21875, ((0, 32),), jnp.float32)
    first_qkv = gaussian(splits[5], (D, 3 * D), (0.6 * (SEQS * LEN) ** 0.5), 640.0, ((0, 32),), jnp.float32)
    second_qkv = jnp.clip(jnp.exp(math.log(95027.2) - 2.779509 * jax.random.uniform(splits[6], (D, 3 * D), jnp.float32) ** block_scale(splits[6], (D, 3 * D), ((0, 32),), -0.2, 0.2)), 5898.24, 95027.2)
    w_out = gaussian(splits[7], (D, D), (3 * D // LEN) ** -0.5, 4.0, ((0, 32),), jnp.float32)
    first_out = gaussian(splits[8], (D, D), (0.9 * SEQS ** 0.5), 32.0, ((0, 32),), jnp.float32)
    second_out = jnp.clip(jnp.exp(math.log(208.0) - 2.7880929 * jax.random.uniform(splits[9], (D, D), jnp.float32) ** block_scale(splits[9], (D, D), ((0, 32),), -0.2, 0.2)), 12.8, 208.0)
    w_up = gaussian(splits[10], (D, FF), D ** -0.5, 0.21875, ((0, 32),), jnp.float32)
    first_up = gaussian(splits[11], (D, FF), (0.2 * (SEQS * LEN) ** 0.5), 224.0, ((0, 32),), jnp.float32)
    second_up = jnp.clip(jnp.exp(math.log(10485.76) - 2.7725887 * jax.random.uniform(splits[12], (D, FF), jnp.float32) ** block_scale(splits[12], (D, FF), ((0, 32),), -0.2, 0.2)), 655.36, 10485.76)
    w_down = gaussian(splits[13], (FF, D), FF ** -0.5, 0.109375, ((0, 32),), jnp.float32)
    first_down = gaussian(splits[14], (FF, D), (0.4 * (SEQS * LEN) ** 0.5), 448.0, ((0, 32),), jnp.float32)
    second_down = jnp.clip(jnp.exp(math.log(41943.04) - 2.7725887 * jax.random.uniform(splits[15], (FF, D), jnp.float32) ** block_scale(splits[15], (FF, D), ((0, 32),), -0.2, 0.2)), 2621.44, 41943.04)
    w_gru = gaussian(splits[16], (D, 4 * HID), D ** -0.5, 0.21875, ((0, 32),), jnp.float32)
    first_gru = gaussian(splits[17], (D, 4 * HID), (0.1 * (SEQS * LEN) ** 0.5), 112.0, ((0, 32),), jnp.float32)
    second_gru = jnp.clip(jnp.exp(math.log(2621.44) - 2.7725887 * jax.random.uniform(splits[18], (D, 4 * HID), jnp.float32) ** block_scale(splits[18], (D, 4 * HID), ((0, 32),), -0.2, 0.2)), 163.84, 2621.44)
    w_blend = gaussian(splits[19], (6 * D, D), (6 * D) ** -0.5, 0.09375, ((0, 32),), jnp.float32)
    first_blend = gaussian(splits[20], (6 * D, D), (0.35 * (SEQS * LEN) ** 0.5), 384.0, ((0, 32),), jnp.float32)
    second_blend = jnp.clip(jnp.exp(math.log(32112.64) - 2.7932081 * jax.random.uniform(splits[21], (6 * D, D), jnp.float32) ** block_scale(splits[21], (6 * D, D), ((0, 32),), -0.2, 0.2)), 1966.08, 32112.64)
    char_table = gaussian(splits[22], (CV, D), 1.0, 5.0, ((0, 32),), jnp.float32)
    first_table = gaussian(splits[23], (CV, D), (0.14 * (SEQS * LEN / CV) ** 0.5), 10.0, ((0, 32),), jnp.float32)
    second_table = jnp.clip(jnp.exp(math.log(20.48) - 2.7725887 * jax.random.uniform(splits[24], (CV, D), jnp.float32) ** block_scale(splits[24], (CV, D), ((0, 32),), -0.2, 0.2)), 1.28, 20.48)
    gains = jnp.clip(1.0 + 0.1 * jax.random.normal(splits[25], (3, D), jnp.float32), 0.5, 1.5)
    first_gains = gaussian(splits[26], (3, D), (0.8 * (SEQS * LEN) ** 0.5), 896.0, ((1, 32),), jnp.float32)
    second_gains = jnp.clip(jnp.exp(math.log(167116.8) - 2.7686748 * jax.random.uniform(splits[27], (3, D), jnp.float32) ** block_scale(splits[27], (3, D), ((1, 32),), -0.2, 0.2)), 10485.76, 167116.8)
    return dict(tokens_in=tokens_in, char_ids=char_ids, char_lengths=char_lengths, out_grad=out_grad, w_qkv=w_qkv, first_qkv=first_qkv, second_qkv=second_qkv, w_out=w_out, first_out=first_out, second_out=second_out, w_up=w_up, first_up=first_up, second_up=second_up, w_down=w_down, first_down=first_down, second_down=second_down, w_gru=w_gru, first_gru=first_gru, second_gru=second_gru, w_blend=w_blend, first_blend=first_blend, second_blend=second_blend, char_table=char_table, first_table=first_table, second_table=second_table, gains=gains, first_gains=first_gains, second_gains=second_gains)


@jax.custom_vjp
def low(v):
    return lax.optimization_barrier(v.astype(jnp.bfloat16)).astype(jnp.float32)

@jax.custom_vjp
def low_back(v):
    return v

def low_keep(v):
    return (low(v), None)

def low_pass(kept, grad):
    return (grad,)

def back_keep(v):
    return (v, None)

def back_low(kept, grad):
    return (low(grad),)
low.defvjp(low_keep, low_pass)
low_back.defvjp(back_keep, back_low)
highest = lax.Precision.HIGHEST

def product(former, latter):
    return jnp.dot(former, latter, precision=highest)

def norm_gain(values, scales):
    center = lax.optimization_barrier(jnp.mean(values, axis=-1, keepdims=True))
    shifted = values - center
    spread = lax.optimization_barrier(jnp.mean(shifted * shifted, axis=-1, keepdims=True))
    return shifted * lax.rsqrt(spread + 1e-05) * scales

def combine(earlier, latter):
    return (earlier[0] * latter[0], latter[0] * earlier[1] + latter[1])

def linear_chain(factor, inject):
    return lax.associative_scan(combine, (factor, inject), axis=0)[1]

def chain_states(logits, candidate):
    update = jax.nn.sigmoid(logits)
    return linear_chain(1.0 - update, update * candidate)

def rows_before(matrix):
    return jnp.concatenate([jnp.zeros_like(matrix[:1]), matrix[:-1]], 0)

def rows_after(matrix):
    return jnp.concatenate([matrix[1:], jnp.zeros_like(matrix[:1])], 0)

def char_segments(lengths, char_count):
    starts = (jnp.cumsum(lengths) - lengths).astype(jnp.int32)
    markers = jnp.zeros((char_count,), jnp.int32).at[starts].add(1)
    return (jnp.cumsum(markers) - 1).astype(jnp.int32)

def step_rates():
    return (0.5 * D ** (-0.5), 0.5 * (3 * D // LEN) ** (-0.5), 0.5 * D ** (-0.5), 0.5 * FF ** (-0.5), 0.5 * D ** (-0.5), 0.5 * (6 * D) ** (-0.5), 0.5, 0.2)

def adamw(master, first_m, second_m, grad_sum, step_rate):
    mean_new = 0.5 * first_m + 0.5 * grad_sum
    power = 0.5 * second_m + 0.5 * grad_sum * grad_sum
    correct = 1.0 - 0.5 ** STEP
    fresh_w = master - step_rate * (mean_new / correct / (jnp.sqrt(power / correct) + 1e-08) + 0.01 * master)
    return (fresh_w, mean_new, power)

def layer(params, tokens, char_ids, lengths):
    w_qkv, w_out, w_up, w_down, w_gru, w_blend, char_table, gains = [low(master) for master in params]
    head_size = D // HEADS
    qkv = low_back(low(product(tokens, w_qkv)))
    queries = qkv[:, :D].reshape(LEN, HEADS, head_size)
    key_rows = qkv[:, D:2 * D].reshape(LEN, HEADS, head_size)
    value_rows = qkv[:, 2 * D:].reshape(LEN, HEADS, head_size)
    scores = low_back(jnp.einsum('qhd,khd->hqk', queries, key_rows, precision=highest) * head_size ** (-0.5))
    attn_probs = low(jax.nn.softmax(scores, axis=-1))
    context = low_back(low(jnp.einsum('hqk,khd->qhd', attn_probs, value_rows, precision=highest).reshape(LEN, D)))
    attended = low_back(product(context, w_out))
    normed = norm_gain(tokens + attended, gains[0])
    hidden = low_back(product(low(normed), w_up))
    active = low(jax.nn.gelu(hidden))
    summed = normed + low_back(product(active, w_down))
    feature = low_back(low(norm_gain(summed, gains[1])))
    embedded = char_table[char_ids]
    gate_logits = low_back(product(embedded, w_gru))
    forward_states = chain_states(gate_logits[:, :HID], gate_logits[:, HID:2 * HID])
    reversed_logits = jnp.flip(gate_logits[:, 2 * HID:], 0)
    backward_states = jnp.flip(chain_states(reversed_logits[:, :HID], reversed_logits[:, HID:]), 0)
    states = jnp.concatenate([forward_states, backward_states], 1)
    segment = char_segments(lengths, CHARS)
    span_len = lengths.astype(jnp.float32)[:, None]
    pooled = low(jax.ops.segment_sum(states, segment, num_segments=LEN, indices_are_sorted=True) / span_len)
    joined = jnp.concatenate([feature, pooled], 1)
    stacked = jnp.concatenate([rows_before(joined), joined, rows_after(joined)], 1)
    blend_in = low_back(product(stacked, w_blend))
    return norm_gain(feature + jax.nn.gelu(blend_in), gains[2])

def reference(tokens_in, char_ids, char_lengths, out_grad, w_qkv, first_qkv, second_qkv, w_out, first_out, second_out, w_up, first_up, second_up, w_down, first_down, second_down, w_gru, first_gru, second_gru, w_blend, first_blend, second_blend, char_table, first_table, second_table, gains, first_gains, second_gains):
    params = (w_qkv, w_out, w_up, w_down, w_gru, w_blend, char_table, gains)
    firsts = (first_qkv, first_out, first_up, first_down, first_gru, first_blend, first_table, first_gains)
    seconds = (second_qkv, second_out, second_up, second_down, second_gru, second_blend, second_table, second_gains)

    def one_sequence(running, pieces):
        tokens, ids_row, lengths_row, cotangent = pieces

        def apply_layer(weights, inputs):
            return layer(weights, inputs, ids_row, lengths_row)
        output, pullback = jax.vjp(apply_layer, params, tokens.astype(jnp.float32))
        grad_params, grad_tokens = pullback(cotangent.astype(jnp.float32))
        running = jax.tree.map(lambda so_far, adding: so_far + adding, running, grad_params)
        return (running, (output.astype(jnp.bfloat16), grad_tokens.astype(jnp.bfloat16)))
    zero_grads = jax.tree.map(jnp.zeros_like, params)
    totals, outputs = lax.scan(one_sequence, zero_grads, (tokens_in, char_ids, char_lengths, out_grad))
    block_out, tokens_grad = outputs
    rates = step_rates()
    results = [adamw(params[number], firsts[number], seconds[number], totals[number], rates[number]) for number in range(8)]
    return (block_out, tokens_grad, results[0][0], results[0][1], results[0][2], results[1][0], results[1][1], results[1][2], results[2][0], results[2][1], results[2][2], results[3][0], results[3][1], results[3][2], results[4][0], results[4][1], results[4][2], results[5][0], results[5][1], results[5][2], results[6][0], results[6][1], results[6][2], results[7][0], results[7][1], results[7][2])
```

```python
import jax
import jax.numpy as jnp
from jax import lax
from jax.experimental import pallas as pl
from jax.experimental.pallas import tpu as pltpu
from jax.sharding import PartitionSpec as P

D = 768
HEADS = 12
FF = 3072
LEN = 1024
STEP = 5


def partner(block, axis, apart):
    count = lax.axis_size(axis)
    route = []
    for low in range(count):
        high = low | 1 << apart
        if high != low and high < count:
            route += [(low, high), (high, low)]
    return lax.ppermute(block, axis, route)


def to_rows(matrix, parts):
    side = matrix.shape[1] // D
    own = matrix.shape[0] // parts
    blocks = matrix.astype(jnp.bfloat16).reshape(parts, own, side, D)
    return blocks.transpose(0, 2, 1, 3).reshape(parts, side * own, D)


def from_rows(rows, offset, own, side):
    parts = rows.shape[0]
    blocks = rows[:, offset : offset + own * side].reshape(parts, side, own, D)
    return blocks.transpose(0, 2, 1, 3).reshape(parts * own, side * D)


def gains_row(gains):
    return jnp.pad(gains.reshape(1, -1), ((0, 7), (0, D - gains.size)))


def gather_rows(shards, axes):
    packed = jnp.concatenate([to_rows(shard, 1)[0] for shard in shards], 0)
    rows = lax.all_gather(packed, axes, axis=0, tiled=False)
    pieces = []
    offset = 0
    for shard in shards:
        own, side = shard.shape[0], shard.shape[1] // D
        pieces.append(from_rows(rows, offset, own, side))
        offset += own * side
    return pieces


def scatter_rows(grads, axes):
    parts = lax.axis_size(axes)
    packed = jnp.concatenate([to_rows(grad, parts) for grad in grads], 1)
    high = packed.shape[1]
    total = lax.psum_scatter(packed.reshape(parts * high, D), axes, scatter_dimension=0, tiled=True)
    pieces = []
    offset = 0
    for grad in grads:
        own, side = grad.shape[0] // parts, grad.shape[1] // D
        pieces.append(from_rows(total[None], offset, own, side).astype(jnp.float32))
        offset += own * side
    return pieces


def product(former, latter):
    return jnp.dot(former, latter, preferred_element_type=jnp.float32)


def inner_rows(former, latter):
    return lax.dot_general(
        former, latter, (((0,), (0,)), ((), ())), preferred_element_type=jnp.float32
    )


def inner_cols(former, latter):
    return lax.dot_general(
        former, latter, (((1,), (1,)), ((), ())), preferred_element_type=jnp.float32
    )


def norm_gain(values, scales):
    center = jnp.mean(values, axis=-1, keepdims=True)
    shifted = values - center
    spread = jnp.mean(shifted * shifted, axis=-1, keepdims=True)
    return shifted * lax.rsqrt(spread + 1e-05) * scales


def rows_before(matrix):
    return jnp.concatenate([jnp.zeros_like(matrix[:1]), matrix[:-1]], 0)


def rows_after(matrix):
    return jnp.concatenate([matrix[1:], jnp.zeros_like(matrix[:1])], 0)


def char_segments(lengths, char_count):
    starts = jnp.cumsum(lengths) - lengths
    markers = jnp.zeros((char_count,), jnp.int32).at[starts].add(1)
    return jnp.cumsum(markers) - 1


def step_rates():
    return (
        0.5 * D ** (-0.5),
        0.5 * (3 * D // LEN) ** (-0.5),
        0.5 * D ** (-0.5),
        0.5 * FF ** (-0.5),
        0.5 * D ** (-0.5),
        0.5 * (6 * D) ** (-0.5),
        0.5,
        0.2,
    )


def adamw(master, first_m, second_m, grad_sum, step_rate):
    mean_new = 0.5 * first_m + 0.5 * grad_sum
    power = 0.5 * second_m + 0.5 * grad_sum * grad_sum
    correct = 1.0 - 0.5**STEP
    fresh_w = master - step_rate * (
        mean_new / correct / (jnp.sqrt(power / correct) + 1e-08) + 0.01 * master
    )
    return (fresh_w, mean_new, power)


STEP_ROWS = 512
UNROLL = 8


def lane_blocks(count):
    half = count // 2
    return [(number, number if number < half else number - half + 4) for number in range(count)]


def chars_ahead(ids, owners, table, w_gru, shares, keep, inject, before, pooled, sums, carry):
    block = pl.program_id(0)
    total = ids.shape[0]
    width = w_gru.shape[1] // 4

    @pl.when(block == 0)
    def start():
        logits = jnp.dot(table[...], w_gru[...], preferred_element_type=jnp.float32)
        keep[...] = jnp.zeros_like(keep)
        inject[...] = jnp.zeros_like(inject)
        carry[...] = jnp.zeros_like(carry)
        for number, place in lane_blocks(6):
            left = number * 128 if number < 3 else 2 * width + (number - 3) * 128
            update = jax.nn.sigmoid(logits[:, left : left + 128])
            keep[:, place, :] = 1.0 - update
            inject[:, place, :] = update * logits[:, left + width : left + width + 128]

    leading = lax.broadcasted_iota(jnp.int32, (8, 128), 0) < 4

    def one(step, state, running, owner_f, owner_b):
        place = block * STEP_ROWS + step
        mirror = total - 1 - place
        id_f, id_b = ids[place], ids[mirror]
        now_f, now_b = owners[place], owners[mirror]
        before[step] = state
        state = jnp.where(leading, keep[id_f], keep[id_b]) * state + jnp.where(
            leading, inject[id_f], inject[id_b]
        )
        stay_f = jnp.where(now_f == owner_f, 1.0, 0.0)
        stay_b = jnp.where(now_b == owner_b, 1.0, 0.0)
        running = running * jnp.where(leading, stay_f, stay_b) + state
        sums[now_f, 0:4] = running[0:4]
        sums[now_b, 4:8] = running[4:8]
        return state, running, now_f, now_b

    def several(group, held):
        for inner in range(UNROLL):
            held = one(group * UNROLL + inner, *held)
        return held

    first = block * STEP_ROWS
    last_f = jnp.where(block == 0, -1, owners[jnp.maximum(first - 1, 0)])
    last_b = jnp.where(block == 0, -1, owners[jnp.minimum(total - first, total - 1)])
    state, running, _, _ = lax.fori_loop(
        0, STEP_ROWS // UNROLL, several, (carry[0], carry[1], last_f, last_b)
    )
    carry[0] = state
    carry[1] = running

    @pl.when(block == pl.num_programs(0) - 1)
    def finish():
        for number, place in lane_blocks(6):
            pooled[:, number * 128 : number * 128 + 128] = (
                sums[:, place, :] * shares[...]
            ).astype(pooled.dtype)


def chars_back(
    ids, owners, upstream, shares, table, w_gru, keep, inject, before, grad_gru, grad_table, spread, zs, cs, full, carry
):
    block = pl.num_programs(0) - 1 - pl.program_id(0)
    total = ids.shape[0]

    @pl.when(pl.program_id(0) == 0)
    def start():
        zs[...] = jnp.zeros_like(zs)
        cs[...] = jnp.zeros_like(cs)
        carry[...] = jnp.zeros_like(carry)
        for number, place in lane_blocks(6):
            spread[:, place, :] = upstream[:, number * 128 : number * 128 + 128] * shares[...]
        for place in (3, 7):
            spread[:, place, :] = jnp.zeros((spread.shape[0], 128), jnp.float32)

    leading = lax.broadcasted_iota(jnp.int32, (8, 128), 0) < 4

    def one(step, passed):
        place = block * STEP_ROWS + step
        mirror = total - 1 - place
        id_f, id_b = ids[place], ids[mirror]
        now_f, now_b = owners[place], owners[mirror]
        kept = jnp.where(leading, keep[id_f], keep[id_b])
        came = jnp.where(leading, inject[id_f], inject[id_b])
        carried = jnp.where(leading, spread[now_f], spread[now_b]) + passed
        passed = kept * carried
        update = 1.0 - kept
        cand_grad = carried * update
        gate_grad = passed * (came - before[step] * update)
        cand_grad = cand_grad.astype(jnp.bfloat16).astype(jnp.float32)
        gate_grad = gate_grad.astype(jnp.bfloat16).astype(jnp.float32)
        zs[id_f, 0:4] += gate_grad[0:4]
        zs[id_b, 4:8] += gate_grad[4:8]
        cs[id_f, 0:4] += cand_grad[0:4]
        cs[id_b, 4:8] += cand_grad[4:8]
        return passed

    def several(group, held):
        for inner in range(UNROLL):
            held = one(STEP_ROWS - 1 - group * UNROLL - inner, held)
        return held

    carry[...] = lax.fori_loop(0, STEP_ROWS // UNROLL, several, carry[...])

    @pl.when(block == 0)
    def finish():
        width = full.shape[1] // 4
        for number, place in lane_blocks(6):
            left = number * 128 if number < 3 else 2 * width + (number - 3) * 128
            full[:, left : left + 128] = zs[:, place, :]
            full[:, left + width : left + width + 128] = cs[:, place, :]
        upper = full[...].astype(jnp.bfloat16)
        lower = (full[...] - upper.astype(jnp.float32)).astype(jnp.bfloat16)
        grad_gru[...] = (
            contract(table[...], upper, 0, 0) + contract(table[...], lower, 0, 0)
        ).astype(grad_gru.dtype)
        grad_table[...] = (
            contract(upper, w_gru[...], 1, 1) + contract(lower, w_gru[...], 1, 1)
        ).astype(grad_table.dtype)


def whole(array):
    return pl.BlockSpec(array.shape, lambda block: (0,) * len(array.shape))


def scalars():
    return pl.BlockSpec(memory_space=pltpu.SMEM)


def run_chars(ids, owners, table, w_gru, shares):
    total, count = ids.shape[0], shares.shape[0]
    letters = table.shape[0]
    f32 = jnp.float32
    tile = jax.ShapeDtypeStruct((letters, 8, 128), f32)
    outs = (
        tile,
        tile,
        jax.ShapeDtypeStruct((total, 8, 128), f32),
        jax.ShapeDtypeStruct((count, w_gru.shape[1] // 2), jnp.bfloat16),
    )
    return pl.pallas_call(
        chars_ahead,
        grid=(total // STEP_ROWS,),
        in_specs=[scalars(), scalars(), whole(table), whole(w_gru), whole(shares)],
        out_specs=[
            whole(tile),
            whole(tile),
            pl.BlockSpec((STEP_ROWS, 8, 128), lambda block: (block, 0, 0)),
            whole(outs[3]),
        ],
        out_shape=outs,
        scratch_shapes=[pltpu.VMEM((count, 8, 128), f32), pltpu.VMEM((2, 8, 128), f32)],
        compiler_params=pltpu.CompilerParams(vmem_limit_bytes=40 << 20),
        cost_estimate=pl.CostEstimate(flops=2 * 256 * 768 * 1536, bytes_accessed=40 << 20, transcendentals=0),
    )(ids, owners, table, w_gru, shares)


def run_chars_back(ids, owners, upstream, shares, table, w_gru, keep, inject, before):
    total, count = ids.shape[0], shares.shape[0]
    letters = keep.shape[0]
    f32 = jnp.float32
    blocks = total // STEP_ROWS
    outs = (
        jax.ShapeDtypeStruct(w_gru.shape, jnp.bfloat16),
        jax.ShapeDtypeStruct(table.shape, jnp.bfloat16),
    )
    return pl.pallas_call(
        chars_back,
        grid=(blocks,),
        in_specs=[
            scalars(),
            scalars(),
            whole(upstream),
            whole(shares),
            whole(table),
            whole(w_gru),
            whole(keep),
            whole(inject),
            pl.BlockSpec((STEP_ROWS, 8, 128), lambda block: (blocks - 1 - block, 0, 0)),
        ],
        out_specs=[whole(outs[0]), whole(outs[1])],
        out_shape=outs,
        scratch_shapes=[
            pltpu.VMEM((count, 8, 128), f32),
            pltpu.VMEM((letters, 8, 128), f32),
            pltpu.VMEM((letters, 8, 128), f32),
            pltpu.VMEM((letters, w_gru.shape[1]), f32),
            pltpu.VMEM((8, 128), f32),
        ],
        compiler_params=pltpu.CompilerParams(vmem_limit_bytes=48 << 20),
        cost_estimate=pl.CostEstimate(
            flops=20_000_000_000, bytes_accessed=40 << 20, transcendentals=0
        ),
    )(ids, owners, upstream, shares, table, w_gru, keep, inject, before)


ROWS = 256


def contract(former, latter, left, right):
    return lax.dot_general(
        former, latter, (((left,), (right,)), ((), ())), preferred_element_type=jnp.float32
    )


def attend(queries, key_rows, value_rows, context, logsum):
    size = key_rows.shape[1] // 2
    lanes = lax.broadcasted_iota(jnp.int32, (1, 2 * size), 1)
    scale = size ** (-0.5)

    def some_rows(number, _):
        at = pl.ds(pl.multiple_of(number * ROWS, ROWS), ROWS)
        row_block = queries[at, :]
        parts = []
        sums = []
        for head in range(2):
            own = (lanes < size) if head == 0 else (lanes >= size)
            scores = contract(jnp.where(own, row_block, 0) * scale, key_rows[...], 1, 1)
            row_max = jnp.max(scores, axis=-1, keepdims=True)
            exponent = jnp.exp(scores - row_max)
            row_total = jnp.sum(exponent, axis=-1, keepdims=True)
            probs = (exponent * (1.0 / row_total)).astype(jnp.bfloat16)
            parts.append(contract(probs, value_rows[...], 1, 0))
            sums.append(row_max + jnp.log(row_total))
        context[at, :] = jnp.where(lanes < size, parts[0], parts[1]).astype(context.dtype)
        both = jnp.where(lanes < size, sums[0], sums[1])
        turned = jnp.transpose(both)
        logsum[0:8, at] = turned[0:8]
        logsum[8:16, at] = turned[size : size + 8]
        return 0

    lax.fori_loop(0, queries.shape[0] // ROWS, some_rows, 0)


def attend_back(queries, key_rows, value_rows, logsum, grads, query_grad, key_grad, value_grad, key_sum, value_sum):
    size = key_rows.shape[1] // 2
    lanes = lax.broadcasted_iota(jnp.int32, (1, 2 * size), 1)
    scale = size ** (-0.5)
    key_sum[...] = jnp.zeros_like(key_sum)
    value_sum[...] = jnp.zeros_like(value_sum)

    def some_rows(number, _):
        at = pl.ds(pl.multiple_of(number * ROWS, ROWS), ROWS)
        row_block = queries[at, :]
        grad_block = grads[at, :]
        parts = []
        for head in range(2):
            own = (lanes < size) if head == 0 else (lanes >= size)
            own_rows = jnp.where(own, row_block, 0) * scale
            own_grads = jnp.where(own, grad_block, 0)
            scores = contract(key_rows[...], own_rows, 1, 1)
            probs = jnp.exp(scores - logsum[8 * head : 8 * head + 1, at])
            value_sum[...] += contract(probs.astype(jnp.bfloat16), own_grads, 1, 0)
            prob_grad = contract(value_rows[...], own_grads, 1, 1)
            center = jnp.sum(prob_grad * probs, axis=0, keepdims=True)
            score_grad = (probs * (prob_grad - center)).astype(jnp.bfloat16)
            key_sum[...] += contract(score_grad, own_rows, 1, 0)
            parts.append(contract(score_grad, key_rows[...], 0, 0))
        query_grad[at, :] = (
            jnp.where(lanes < size, parts[0], parts[1]) * scale
        ).astype(query_grad.dtype)
        return 0

    lax.fori_loop(0, queries.shape[0] // ROWS, some_rows, 0)
    key_grad[...] = key_sum[...].astype(key_grad.dtype)
    value_grad[...] = value_sum[...].astype(value_grad.dtype)


def column(rows, width, offset):
    return pl.BlockSpec((rows, width), lambda pair: (0, offset + pair))


def run_attend(qkv):
    length, across = qkv.shape
    model = across // 3
    pairs = model // 128
    return pl.pallas_call(
        attend,
        grid=(pairs,),
        in_specs=[column(length, 128, pairs * part) for part in range(3)],
        out_specs=[column(length, 128, 0), pl.BlockSpec((16, length), lambda pair: (pair, 0))],
        out_shape=(
            jax.ShapeDtypeStruct((length, model), jnp.bfloat16),
            jax.ShapeDtypeStruct((16 * pairs, length), jnp.float32),
        ),
        compiler_params=pltpu.CompilerParams(vmem_limit_bytes=40 << 20),
        cost_estimate=pl.CostEstimate(flops=4 * length * length * model, bytes_accessed=8 * length * model, transcendentals=length * length * 12),
    )(qkv, qkv, qkv)


def run_attend_back(qkv, logsum, grads):
    length, across = qkv.shape
    model = across // 3
    pairs = model // 128
    part = jax.ShapeDtypeStruct((length, model), jnp.bfloat16)
    return pl.pallas_call(
        attend_back,
        grid=(pairs,),
        in_specs=[column(length, 128, pairs * part) for part in range(3)]
        + [pl.BlockSpec((16, length), lambda pair: (pair, 0)), column(length, 128, 0)],
        out_specs=[column(length, 128, 0)] * 3,
        out_shape=(part, part, part),
        scratch_shapes=[pltpu.VMEM((length, 128), jnp.float32)] * 2,
        compiler_params=pltpu.CompilerParams(vmem_limit_bytes=40 << 20),
        cost_estimate=pl.CostEstimate(flops=10 * length * length * model, bytes_accessed=16 * length * model, transcendentals=length * length * 12),
    )(qkv, qkv, qkv, logsum, grads)


def token_forward(tokens, weights):
    qkv = product(tokens, weights[0]).astype(jnp.bfloat16)
    context, logsum = run_attend(qkv)
    mixed_sum = tokens.astype(jnp.float32) + product(context, weights[1])
    normed = norm_gain(mixed_sum, weights[7][0].astype(jnp.float32))
    hidden = product(normed.astype(jnp.bfloat16), weights[2])
    summed = normed + product(jax.nn.gelu(hidden).astype(jnp.bfloat16), weights[3])
    feature = norm_gain(summed, weights[7][1].astype(jnp.float32)).astype(jnp.bfloat16)
    return (feature, (qkv, logsum, context, mixed_sum, normed, hidden, summed))


def token_backward(tokens, stored, feature_grad, weights):
    qkv, logsum, context, mixed_sum, normed, kept_hidden, summed = stored
    summed_grad, gain_ffn = jax.vjp(norm_gain, summed, weights[7][1].astype(jnp.float32))[1](
        feature_grad.astype(jnp.float32)
    )
    ffn_grad = summed_grad.astype(jnp.bfloat16)
    active = jax.nn.gelu(kept_hidden).astype(jnp.bfloat16)
    grad_down = inner_rows(active, ffn_grad)
    hidden_grad = jax.vjp(jax.nn.gelu, kept_hidden)[1](inner_cols(ffn_grad, weights[3]))[0].astype(
        jnp.bfloat16
    )
    grad_up = inner_rows(normed.astype(jnp.bfloat16), hidden_grad)
    normed_grad = summed_grad + inner_cols(hidden_grad, weights[2])
    mixed_grad, gain_attn = jax.vjp(norm_gain, mixed_sum, weights[7][0].astype(jnp.float32))[1](
        normed_grad
    )
    attended_grad = mixed_grad.astype(jnp.bfloat16)
    grad_out = inner_rows(context, attended_grad)
    context_grad = inner_cols(attended_grad, weights[1]).astype(jnp.bfloat16)
    qkv_grad = jnp.concatenate(run_attend_back(qkv, logsum, context_grad), 1)
    grad_qkv = inner_rows(tokens, qkv_grad)
    tokens_grad = (mixed_grad + inner_cols(qkv_grad, weights[0])).astype(jnp.bfloat16)
    return (tokens_grad, (grad_qkv, grad_out, grad_up, grad_down, gain_attn, gain_ffn))


def char_section(feature, pooled, kept, out_rows, weights):
    ids_row, segment, shares, keep, inject, before = kept
    w_gru, w_blend, table_copy = (weights[4], weights[5], weights[6])
    joined = jnp.concatenate([feature, pooled], 1)
    stacked = jnp.concatenate([rows_before(joined), joined, rows_after(joined)], 1)
    blend_in = product(stacked, w_blend)
    blended, gelu_pull = jax.vjp(jax.nn.gelu, blend_in)
    result, norm_pull = jax.vjp(
        norm_gain, feature.astype(jnp.float32) + blended, weights[7][2].astype(jnp.float32)
    )
    total_grad, gain_blend = norm_pull(out_rows.astype(jnp.float32))
    blend_grad = gelu_pull(total_grad)[0].astype(jnp.bfloat16)
    grad_blend = inner_rows(stacked, blend_grad)
    stacked_grad = inner_cols(blend_grad, w_blend)
    pair_width = joined.shape[1]
    model_width = pair_width // 2
    joined_grad = (
        stacked_grad[:, pair_width : 2 * pair_width]
        + rows_after(stacked_grad[:, :pair_width])
        + rows_before(stacked_grad[:, 2 * pair_width :])
    )
    feature_grad = (total_grad + joined_grad[:, :model_width]).astype(jnp.bfloat16)
    grad_gru, grad_table = run_chars_back(
        ids_row, segment, joined_grad[:, model_width:], shares, table_copy, w_gru, keep, inject, before
    )
    return (
        result.astype(jnp.bfloat16),
        feature_grad,
        (grad_gru, grad_blend, grad_table, gain_blend),
    )


def on_device(
    tokens_in,
    char_ids,
    char_lengths,
    out_grad,
    w_qkv,
    first_qkv,
    second_qkv,
    w_out,
    first_out,
    second_out,
    w_up,
    first_up,
    second_up,
    w_down,
    first_down,
    second_down,
    w_gru,
    first_gru,
    second_gru,
    w_blend,
    first_blend,
    second_blend,
    char_table,
    first_table,
    second_table,
    gains,
    first_gains,
    second_gains,
):
    masters = (w_qkv, w_out, w_up, w_down, w_gru, w_blend, char_table, gains)
    firsts = (
        first_qkv,
        first_out,
        first_up,
        first_down,
        first_gru,
        first_blend,
        first_table,
        first_gains,
    )
    seconds = (
        second_qkv,
        second_out,
        second_up,
        second_down,
        second_gru,
        second_blend,
        second_table,
        second_gains,
    )
    on_first = lax.axis_index("stream") == 0
    half_len = tokens_in.shape[1]
    everyone = ("stream", "dp")
    early = gather_rows((char_table, w_gru, w_qkv), everyone)
    late = gather_rows((w_out, w_up, w_down, w_blend, gains_row(gains)), everyone)
    count = late[4].shape[0] // 8
    all_gains = late[4][::8, : gains.size].reshape(count, 3, -1).transpose(1, 0, 2).reshape(3, -1)
    current = (early[2], late[0], late[1], late[2], early[1], late[3], early[0], all_gains)
    block_parts = []
    grad_parts = []
    other_tokens = jnp.where(on_first, tokens_in[1], tokens_in[0])
    other_grad = jnp.where(on_first, out_grad[1], out_grad[0])
    keep_tokens = jnp.where(on_first, tokens_in[0], tokens_in[1])
    keep_grad = jnp.where(on_first, out_grad[0], out_grad[1])
    got_tokens, got_grad = partner((other_tokens, other_grad), "stream", 0)
    whole_tokens = jnp.where(
        on_first,
        jnp.concatenate([keep_tokens, got_tokens], 0),
        jnp.concatenate([got_tokens, keep_tokens], 0),
    )
    whole_grad = jnp.where(
        on_first,
        jnp.concatenate([keep_grad, got_grad], 0),
        jnp.concatenate([got_grad, keep_grad], 0),
    )
    ids_row = jnp.where(on_first, char_ids[0], char_ids[1])
    lengths_row = jnp.where(on_first, char_lengths[0], char_lengths[1])
    segment = char_segments(lengths_row, ids_row.shape[0])
    shares = 1.0 / lengths_row.astype(jnp.float32)[:, None]
    keep, inject, before, pooled = run_chars(ids_row, segment, current[6], current[4], shares)
    feature, stored = token_forward(whole_tokens, current)
    result, feature_grad, char_grads = char_section(
        feature, pooled, (ids_row, segment, shares, keep, inject, before), whole_grad, current
    )
    tokens_grad, token_grads = token_backward(whole_tokens, stored, feature_grad, current)
    send_result = jnp.where(on_first, result[half_len:], result[:half_len])
    send_grad = jnp.where(on_first, tokens_grad[half_len:], tokens_grad[:half_len])
    back_result, back_grad = partner((send_result, send_grad), "stream", 0)
    block_parts.append(jnp.where(on_first, result[:half_len], back_result))
    block_parts.append(jnp.where(on_first, back_result, result[half_len:]))
    grad_parts.append(jnp.where(on_first, tokens_grad[:half_len], back_grad))
    grad_parts.append(jnp.where(on_first, back_grad, tokens_grad[half_len:]))
    gain_grads = jnp.stack([token_grads[4], token_grads[5], char_grads[3]])
    gain_rows = gain_grads.reshape(3, count, -1).transpose(1, 0, 2).reshape(count, -1)
    gain_rows = jnp.pad(gain_rows[:, None], ((0, 0), (0, 7), (0, D - gain_rows.shape[1])))
    gain_rows = gain_rows.reshape(8 * count, D)
    blend_sum = scatter_rows((char_grads[1],), everyone)
    middle = scatter_rows((token_grads[3], token_grads[2], char_grads[0], char_grads[2]), everyone)
    final = scatter_rows((token_grads[0], token_grads[1], gain_rows), everyone)
    gain_sum = final[2][0, : gains.size].reshape(gains.shape)
    sums = (final[0], final[1], middle[1], middle[0], middle[2], blend_sum[0], middle[3], gain_sum)
    rates = step_rates()
    results = [
        adamw(masters[number], firsts[number], seconds[number], sums[number], rates[number])
        for number in range(8)
    ]
    return (
        jnp.stack(block_parts),
        jnp.stack(grad_parts),
        results[0][0],
        results[0][1],
        results[0][2],
        results[1][0],
        results[1][1],
        results[1][2],
        results[2][0],
        results[2][1],
        results[2][2],
        results[3][0],
        results[3][1],
        results[3][2],
        results[4][0],
        results[4][1],
        results[4][2],
        results[5][0],
        results[5][1],
        results[5][2],
        results[6][0],
        results[6][1],
        results[6][2],
        results[7][0],
        results[7][1],
        results[7][2],
    )


def solution(mesh):
    in_specs = (
        P("dp", "stream", None),
        P("dp", None),
        P("dp", None),
        P("dp", "stream", None),
        P(("stream", "dp"), None),
        P(("stream", "dp"), None),
        P(("stream", "dp"), None),
        P(("stream", "dp"), None),
        P(("stream", "dp"), None),
        P(("stream", "dp"), None),
        P(("stream", "dp"), None),
        P(("stream", "dp"), None),
        P(("stream", "dp"), None),
        P(("stream", "dp"), None),
        P(("stream", "dp"), None),
        P(("stream", "dp"), None),
        P(("stream", "dp"), None),
        P(("stream", "dp"), None),
        P(("stream", "dp"), None),
        P(("stream", "dp"), None),
        P(("stream", "dp"), None),
        P(("stream", "dp"), None),
        P(("stream", "dp"), None),
        P(("stream", "dp"), None),
        P(("stream", "dp"), None),
        P(None, ("stream", "dp")),
        P(None, ("stream", "dp")),
        P(None, ("stream", "dp")),
    )
    out_specs = (
        P("dp", "stream", None),
        P("dp", "stream", None),
        P(("stream", "dp"), None),
        P(("stream", "dp"), None),
        P(("stream", "dp"), None),
        P(("stream", "dp"), None),
        P(("stream", "dp"), None),
        P(("stream", "dp"), None),
        P(("stream", "dp"), None),
        P(("stream", "dp"), None),
        P(("stream", "dp"), None),
        P(("stream", "dp"), None),
        P(("stream", "dp"), None),
        P(("stream", "dp"), None),
        P(("stream", "dp"), None),
        P(("stream", "dp"), None),
        P(("stream", "dp"), None),
        P(("stream", "dp"), None),
        P(("stream", "dp"), None),
        P(("stream", "dp"), None),
        P(("stream", "dp"), None),
        P(("stream", "dp"), None),
        P(("stream", "dp"), None),
        P(None, ("stream", "dp")),
        P(None, ("stream", "dp")),
        P(None, ("stream", "dp")),
    )
    return jax.shard_map(
        on_device, mesh=mesh, in_specs=in_specs, out_specs=out_specs, check_vma=False
    )
```

```python
import functools

import jax
import jax.numpy as jnp
from jax import lax
from jax.experimental import pallas as pl
from jax.experimental.pallas import tpu as pltpu
from jax.sharding import PartitionSpec as P

D = 768
HEADS = 12
FF = 3072
LEN = 1024
STEP = 5


def partner(block, axis, apart):
    count = lax.axis_size(axis)
    route = []
    for low in range(count):
        high = low | 1 << apart
        if high != low and high < count:
            route += [(low, high), (high, low)]
    return lax.ppermute(block, axis, route)


def to_rows(matrix, parts):
    side = matrix.shape[1] // D
    own = matrix.shape[0] // parts
    blocks = matrix.astype(jnp.bfloat16).reshape(parts, own, side, D)
    return blocks.transpose(0, 2, 1, 3).reshape(parts, side * own, D)


def from_rows(rows, offset, own, side):
    parts = rows.shape[0]
    blocks = rows[:, offset : offset + own * side].reshape(parts, side, own, D)
    return blocks.transpose(0, 2, 1, 3).reshape(parts * own, side * D)


def gains_row(gains):
    return jnp.pad(gains.reshape(1, -1), ((0, 7), (0, D - gains.size)))


def swap_bit(block, bit):
    inner = lax.axis_size("dp").bit_length() - 1
    if bit < inner:
        return partner(block, "dp", bit)
    return partner(block, "stream", bit - inner)


def pair_bits():
    return (lax.axis_size("dp") * lax.axis_size("stream")).bit_length() - 2


def hop_order(turned):
    top = pair_bits()
    order = list(range(2, top)) + ([1, top] if turned else [top, 1])
    return order


def in_pairs(shapes):
    parts = lax.axis_size("dp") * lax.axis_size("stream")
    return parts >= 8 and parts & (parts - 1) == 0 and all(rows % 8 == 0 for rows, _ in shapes)


def my_place():
    return (lax.axis_index("stream") * lax.axis_size("dp") + lax.axis_index("dp")).reshape(1)


def shapes_of(matrices, parts):
    return [(matrix.shape[0] // parts, matrix.shape[1] // D) for matrix in matrices]


def assemble(shapes, place, mine, theirs, *weights):
    core = place[0] & 1
    low = (place[0] >> 1) & 3
    pieces = []
    for pair in range(4):
        own = mine[pair ^ low].astype(jnp.float32)
        other = theirs[pair ^ low].astype(jnp.float32)
        pieces.append(jnp.where(core == 0, own, other))
        pieces.append(jnp.where(core == 0, other, own))
    offset = 0
    for (rows, side), weight in zip(shapes, weights):
        for number in range(side):
            block = jnp.concatenate([piece[offset : offset + rows] for piece in pieces], 0)
            weight[:, number * D : number * D + D] = block.astype(weight.dtype)
            offset += rows


def apart(shapes, place, *refs):
    grads, keep, send = refs[: len(shapes)], refs[-2], refs[-1]
    core = place[0] & 1
    low = (place[0] >> 1) & 3
    for pair in range(4):
        halves = []
        for side in range(2):
            pieces = []
            for (rows, across), grad in zip(shapes, grads):
                first = (2 * pair + side) * rows
                for number in range(across):
                    pieces.append(
                        grad[first : first + rows, number * D : number * D + D].astype(jnp.float32)
                    )
            halves.append(jnp.concatenate(pieces, 0))
        keep[pair ^ low] = jnp.where(core == 0, halves[0], halves[1]).astype(keep.dtype)
        send[pair ^ low] = jnp.where(core == 0, halves[1], halves[0]).astype(send.dtype)


def turned_block(high):
    return pl.BlockSpec((4, high, D), lambda group, place: (group ^ (place[0] >> 3), 0, 0))


def natural_block(shape):
    return pl.BlockSpec((8 * shape[0], shape[1] * D), lambda group, place: (group, 0))


class Flow:
    def __init__(self):
        self.live = {}
        self.ended = {}

    def begin(self, name, chain, skips=()):
        self.step(name, chain, None, list(skips))

    def step(self, name, chain, arrays, skips):
        try:
            waiting = chain.send(arrays)
            self.live[name] = [chain, waiting, skips, skips.pop(0) if skips else 0]
        except StopIteration as stop:
            self.ended[name] = stop.value

    def slot(self, values):
        due = [name for name, entry in self.live.items() if entry[3] == 0]
        for entry in self.live.values():
            entry[3] -= 1
        values, waited = lax.optimization_barrier(
            (values, [self.live[name][1] for name in due])
        )
        for name, arrays in zip(due, waited):
            chain, _, skips, _ = self.live.pop(name)
            self.step(name, chain, arrays, skips)
        return values

    def end(self, name):
        return self.ended.pop(name)


def gather_chain(shards, turned):
    shapes = shapes_of(shards, 1)
    packed = jnp.concatenate([to_rows(shard, 1)[0] for shard in shards], 0)
    if not in_pairs(shapes):
        return gather_whole(packed, shapes)
    top = pair_bits()
    held = packed.reshape((1,) * top + packed.shape)
    for bit in hop_order(turned):
        other = swap_bit(held, bit)
        held, other = yield (held, other)
        held = jnp.concatenate([held, other], top - bit)
    other = swap_bit(held, 0)
    held, other = yield (held, other)
    return join_halves(shapes, held, other)


def gather_whole(packed, shapes):
    rows = lax.all_gather(packed, ("stream", "dp"), axis=0, tiled=False)
    pieces = []
    offset = 0
    for own, side in shapes:
        pieces.append(from_rows(rows, offset, own, side))
        offset += own * side
    return pieces


def join_halves(shapes, mine, theirs):
    high = mine.shape[-2]
    pairs = 1 << pair_bits()
    parts = 2 * pairs
    return pl.pallas_call(
        functools.partial(assemble, shapes),
        grid_spec=pltpu.PrefetchScalarGridSpec(
            num_scalar_prefetch=1,
            grid=(pairs // 4,),
            in_specs=[turned_block(high)] * 2,
            out_specs=[natural_block(shape) for shape in shapes],
        ),
        out_shape=[
            jax.ShapeDtypeStruct((parts * rows, side * D), jnp.bfloat16) for rows, side in shapes
        ],
        compiler_params=pltpu.CompilerParams(vmem_limit_bytes=40 << 20),
        cost_estimate=pl.CostEstimate(
            flops=0, bytes_accessed=4 * parts * high * D, transcendentals=0
        ),
    )(my_place(), mine.reshape(pairs, high, D), theirs.reshape(pairs, high, D))


def scatter_whole(grads):
    parts = lax.axis_size("dp") * lax.axis_size("stream")
    packed = jnp.concatenate([to_rows(grad, parts) for grad in grads], 1)
    total = lax.psum_scatter(
        packed.reshape(-1, D), ("stream", "dp"), scatter_dimension=0, tiled=True
    ).astype(jnp.float32)
    return own_pieces(total, shapes_of(grads, parts))


def own_pieces(total, shapes):
    pieces = []
    offset = 0
    for own, side in shapes:
        pieces.append(from_rows(total[None], offset, own, side))
        offset += own * side
    return pieces


def scatter_chain(grads, turned):
    parts = lax.axis_size("dp") * lax.axis_size("stream")
    shapes = shapes_of(grads, parts)
    if not in_pairs(shapes):
        return scatter_whole(grads)
    pairs = parts // 2
    high = sum(rows * side for rows, side in shapes)
    half = jax.ShapeDtypeStruct((pairs, high, D), jnp.bfloat16)
    kept, sent = pl.pallas_call(
        functools.partial(apart, shapes),
        grid_spec=pltpu.PrefetchScalarGridSpec(
            num_scalar_prefetch=1,
            grid=(pairs // 4,),
            in_specs=[natural_block(shape) for shape in shapes],
            out_specs=[turned_block(high)] * 2,
        ),
        out_shape=[half, half],
        compiler_params=pltpu.CompilerParams(vmem_limit_bytes=40 << 20),
        cost_estimate=pl.CostEstimate(
            flops=0, bytes_accessed=4 * parts * high * D, transcendentals=0
        ),
    )(my_place(), *[grad.astype(jnp.bfloat16) for grad in grads])
    other = swap_bit(sent, 0)
    kept, other = yield (kept, other)
    total = kept.astype(jnp.float32) + other.astype(jnp.float32)
    top = pair_bits()
    total = total.reshape((2,) * top + (high, D))
    for bit in reversed(hop_order(turned)):
        axis = top - bit
        other = swap_bit(lax.slice_in_dim(total, 1, 2, axis=axis).astype(jnp.bfloat16), bit)
        kept, other = yield (lax.slice_in_dim(total, 0, 1, axis=axis), other)
        total = kept + other.astype(jnp.float32)
    return own_pieces(total.reshape(high, D), shapes)


def swap_chain(block):
    other = yield partner(block, "stream", 0)
    return other


def product(former, latter):
    return jnp.dot(former, latter, preferred_element_type=jnp.float32)


def inner_rows(former, latter):
    return lax.dot_general(
        former, latter, (((0,), (0,)), ((), ())), preferred_element_type=jnp.float32
    )


def inner_cols(former, latter):
    return lax.dot_general(
        former, latter, (((1,), (1,)), ((), ())), preferred_element_type=jnp.float32
    )


def norm_gain(values, scales):
    center = jnp.mean(values, axis=-1, keepdims=True)
    shifted = values - center
    spread = jnp.mean(shifted * shifted, axis=-1, keepdims=True)
    return shifted * lax.rsqrt(spread + 1e-05) * scales


def rows_before(matrix):
    return jnp.concatenate([jnp.zeros_like(matrix[:1]), matrix[:-1]], 0)


def rows_after(matrix):
    return jnp.concatenate([matrix[1:], jnp.zeros_like(matrix[:1])], 0)


def char_segments(lengths, char_count):
    starts = jnp.cumsum(lengths) - lengths
    markers = jnp.zeros((char_count,), jnp.int32).at[starts].add(1)
    return jnp.cumsum(markers) - 1


def step_rates():
    return (
        0.5 * D ** (-0.5),
        0.5 * (3 * D // LEN) ** (-0.5),
        0.5 * D ** (-0.5),
        0.5 * FF ** (-0.5),
        0.5 * D ** (-0.5),
        0.5 * (6 * D) ** (-0.5),
        0.5,
        0.2,
    )


def adamw(master, first_m, second_m, grad_sum, step_rate):
    mean_new = 0.5 * first_m + 0.5 * grad_sum
    power = 0.5 * second_m + 0.5 * grad_sum * grad_sum
    correct = 1.0 - 0.5**STEP
    fresh_w = master - step_rate * (
        mean_new / correct / (jnp.sqrt(power / correct) + 1e-08) + 0.01 * master
    )
    return (fresh_w, mean_new, power)


STEP_ROWS = 512
UNROLL = 8


def contract(former, latter, left, right):
    return lax.dot_general(
        former, latter, (((left,), (right,)), ((), ())), preferred_element_type=jnp.float32
    )


def lane_blocks(width):
    blocks = []
    for number in range(2 * width // 128):
        side, lane = divmod(number * 128, width)
        blocks.append((number * 128, 2 * side * width + lane, 4 * side + lane // 128))
    return blocks


def eight(offset):
    return pl.ds(pl.multiple_of(offset, 8), 8)


def chars_ahead(rows_f, rows_b, ends, table, w_gru, shares, letters, before, pooled, running, spans, carry):
    block = pl.program_id(0)
    total = rows_f.shape[0]
    width = w_gru.shape[1] // 4

    @pl.when(block == 0)
    def start():
        logits = jnp.dot(table[...], w_gru[...], preferred_element_type=jnp.float32)
        letters[...] = jnp.zeros_like(letters)
        carry[...] = jnp.zeros_like(carry)
        for _, left, place in lane_blocks(width):
            update = jax.nn.sigmoid(logits[:, left : left + 128])
            letters[:, place, :] = 1.0 - update
            letters[:, 8 + place, :] = update * logits[:, left + width : left + width + 128]

    leading = lax.broadcasted_iota(jnp.int32, (8, 128), 0) < 4

    def several(group, held):
        state, total_state = held
        first = block * STEP_ROWS + group * UNROLL
        factors, adds = [], []
        for inner in range(UNROLL):
            id_f, id_b = rows_f[first + inner], rows_b[first + inner]
            factors.append(jnp.where(leading, letters[id_f, 0:8], letters[id_b, 0:8]))
            adds.append(jnp.where(leading, letters[id_f, 8:16], letters[id_b, 8:16]))
        for inner in range(UNROLL):
            before[group * UNROLL + inner] = state
            running[first + inner] = total_state
            state = factors[inner] * state + adds[inner]
            total_state = total_state + state
        return state, total_state

    state, total_state = lax.fori_loop(0, STEP_ROWS // UNROLL, several, (carry[0], carry[1]))
    carry[0] = state
    carry[1] = total_state

    @pl.when(block == pl.num_programs(0) - 1)
    def finish():
        running[total] = total_state

        def tokens(group, prior):
            found = []
            for inner in range(UNROLL):
                end = ends[group * UNROLL + inner]
                found.append(jnp.where(leading, running[end], -running[total - end]))
            for inner in range(UNROLL):
                spans[group * UNROLL + inner] = found[inner] - prior
                prior = found[inner]
            return prior

        lax.fori_loop(0, ends.shape[0] // UNROLL, tokens, jnp.where(leading, running[0], -running[total]))
        for at, _, place in lane_blocks(width):
            pooled[:, at : at + 128] = (spans[:, place, :] * shares[...]).astype(pooled.dtype)


def chars_back(
    rows_f, rows_b, owners_f, owners_b, upstream, shares, table, w_gru, letters, before,
    grad_gru, grad_table, spread, sums_f, sums_b, more_f, more_b, full, carry
):
    block = pl.num_programs(0) - 1 - pl.program_id(0)
    width = full.shape[1] // 4

    @pl.when(pl.program_id(0) == 0)
    def start():
        for held in (sums_f, sums_b, more_f, more_b):
            held[...] = jnp.zeros_like(held)
        carry[...] = jnp.zeros_like(carry)
        for at, _, place in lane_blocks(width):
            spread[:, place, :] = upstream[:, at : at + 128] * shares[...]
        for place in (3, 7):
            spread[:, place, :] = jnp.zeros((spread.shape[0], 128), jnp.float32)

    leading = lax.broadcasted_iota(jnp.int32, (8, 128), 0) < 4

    def several(group, passed):
        steps = [STEP_ROWS - 1 - group * UNROLL - inner for inner in range(UNROLL)]
        kept, given, priors, owned = [], [], [], []
        for step in steps:
            place = block * STEP_ROWS + step
            id_f, id_b = rows_f[place], rows_b[place]
            owned.append((id_f, id_b))
            kept.append(jnp.where(leading, letters[id_f, 0:8], letters[id_b, 0:8]))
            given.append(jnp.where(leading, spread[owners_f[place]], spread[owners_b[place]]))
            priors.append(before[step])
        for inner in range(UNROLL):
            carried = given[inner] + passed
            passed = kept[inner] * carried
            moved = carried * priors[inner]
            id_f, id_b = owned[inner]
            for held, row, value in (
                ((sums_f, more_f)[inner % 2], id_f, jnp.where(leading, carried, pltpu.roll(moved, 4, 0))),
                ((sums_b, more_b)[inner % 2], id_b, jnp.where(leading, pltpu.roll(carried, 4, 0), moved)),
            ):
                held[row] += value
        return passed

    carry[...] = lax.fori_loop(0, STEP_ROWS // UNROLL, several, carry[...])

    @pl.when(block == 0)
    def finish():
        sums_f[...] += more_f[...]
        sums_b[...] += more_b[...]
        for _, left, place in lane_blocks(width):
            found = sums_f if place < 4 else sums_b
            lane = place % 4
            kept = letters[:, place, :]
            update = 1.0 - kept
            total = found[:, lane, :]
            full[:, left : left + 128] = kept * (
                letters[:, 8 + place, :] * total - update * found[:, 4 + lane, :]
            )
            full[:, left + width : left + width + 128] = update * total
        upper = full[...].astype(jnp.bfloat16)
        lower = (full[...] - upper.astype(jnp.float32)).astype(jnp.bfloat16)
        grad_gru[...] = (
            contract(table[...], upper, 0, 0) + contract(table[...], lower, 0, 0)
        ).astype(grad_gru.dtype)
        grad_table[...] = (
            contract(upper, w_gru[...], 1, 1) + contract(lower, w_gru[...], 1, 1)
        ).astype(grad_table.dtype)


def whole(array):
    return pl.BlockSpec(array.shape, lambda block: (0,) * len(array.shape))


def scalars():
    return pl.BlockSpec(memory_space=pltpu.SMEM)


def run_chars(ids, ends, table, w_gru, shares):
    total, count = ids.shape[0], shares.shape[0]
    f32 = jnp.float32
    outs = (
        jax.ShapeDtypeStruct((table.shape[0], 16, 128), f32),
        jax.ShapeDtypeStruct((total, 8, 128), f32),
        jax.ShapeDtypeStruct((count, w_gru.shape[1] // 2), jnp.bfloat16),
    )
    return pl.pallas_call(
        chars_ahead,
        grid=(total // STEP_ROWS,),
        in_specs=[scalars(), scalars(), scalars(), whole(table), whole(w_gru), whole(shares)],
        out_specs=[
            whole(outs[0]),
            pl.BlockSpec((STEP_ROWS, 8, 128), lambda block: (block, 0, 0)),
            whole(outs[2]),
        ],
        out_shape=outs,
        scratch_shapes=[
            pltpu.VMEM((total + 1, 8, 128), f32),
            pltpu.VMEM((count, 8, 128), f32),
            pltpu.VMEM((2, 8, 128), f32),
        ],
        compiler_params=pltpu.CompilerParams(vmem_limit_bytes=56 << 20),
        cost_estimate=pl.CostEstimate(
            flops=20_000_000_000, bytes_accessed=40 << 20, transcendentals=0
        ),
    )(ids, jnp.flip(ids), ends, table, w_gru, shares)


def run_chars_back(ids, owners, upstream, shares, table, w_gru, letters, before):
    total, count = ids.shape[0], shares.shape[0]
    f32 = jnp.float32
    blocks = total // STEP_ROWS
    outs = (
        jax.ShapeDtypeStruct(w_gru.shape, jnp.bfloat16),
        jax.ShapeDtypeStruct(table.shape, jnp.bfloat16),
    )
    return pl.pallas_call(
        chars_back,
        grid=(blocks,),
        in_specs=[scalars()] * 4
        + [
            whole(upstream),
            whole(shares),
            whole(table),
            whole(w_gru),
            whole(letters),
            pl.BlockSpec((STEP_ROWS, 8, 128), lambda block: (blocks - 1 - block, 0, 0)),
        ],
        out_specs=[whole(outs[0]), whole(outs[1])],
        out_shape=outs,
        scratch_shapes=[
            pltpu.VMEM((count, 8, 128), f32),
            pltpu.VMEM((table.shape[0], 8, 128), f32),
            pltpu.VMEM((table.shape[0], 8, 128), f32),
            pltpu.VMEM((table.shape[0], 8, 128), f32),
            pltpu.VMEM((table.shape[0], 8, 128), f32),
            pltpu.VMEM((table.shape[0], w_gru.shape[1]), f32),
            pltpu.VMEM((8, 128), f32),
        ],
        compiler_params=pltpu.CompilerParams(vmem_limit_bytes=56 << 20),
        cost_estimate=pl.CostEstimate(
            flops=20_000_000_000, bytes_accessed=40 << 20, transcendentals=0
        ),
    )(ids, jnp.flip(ids), owners, jnp.flip(owners), upstream, shares, table, w_gru, letters, before)


ROWS = 256


def attend(queries, key_rows, value_rows, context, logsum):
    size = key_rows.shape[1] // 2
    lanes = lax.broadcasted_iota(jnp.int32, (1, 2 * size), 1)
    scale = size ** (-0.5)

    def some_rows(number, _):
        at = pl.ds(pl.multiple_of(number * ROWS, ROWS), ROWS)
        row_block = queries[at, :]
        parts = []
        sums = []
        for head in range(2):
            own = (lanes < size) if head == 0 else (lanes >= size)
            scores = contract(jnp.where(own, row_block, 0) * scale, key_rows[...], 1, 1)
            row_max = jnp.max(scores, axis=-1, keepdims=True)
            exponent = jnp.exp(scores - row_max)
            row_total = jnp.sum(exponent, axis=-1, keepdims=True)
            probs = (exponent * (1.0 / row_total)).astype(jnp.bfloat16)
            parts.append(contract(probs, value_rows[...], 1, 0))
            sums.append(row_max + jnp.log(row_total))
        context[at, :] = jnp.where(lanes < size, parts[0], parts[1]).astype(context.dtype)
        both = jnp.where(lanes < size, sums[0], sums[1])
        turned = jnp.transpose(both)
        logsum[0:8, at] = turned[0:8]
        logsum[8:16, at] = turned[size : size + 8]
        return 0

    lax.fori_loop(0, queries.shape[0] // ROWS, some_rows, 0)


def attend_back(queries, key_rows, value_rows, logsum, grads, query_grad, key_grad, value_grad, key_sum, value_sum):
    size = key_rows.shape[1] // 2
    lanes = lax.broadcasted_iota(jnp.int32, (1, 2 * size), 1)
    scale = size ** (-0.5)
    key_sum[...] = jnp.zeros_like(key_sum)
    value_sum[...] = jnp.zeros_like(value_sum)

    def some_rows(number, _):
        at = pl.ds(pl.multiple_of(number * ROWS, ROWS), ROWS)
        row_block = queries[at, :]
        grad_block = grads[at, :]
        parts = []
        for head in range(2):
            own = (lanes < size) if head == 0 else (lanes >= size)
            own_rows = jnp.where(own, row_block, 0) * scale
            own_grads = jnp.where(own, grad_block, 0)
            scores = contract(key_rows[...], own_rows, 1, 1)
            probs = jnp.exp(scores - logsum[8 * head : 8 * head + 1, at])
            value_sum[...] += contract(probs.astype(jnp.bfloat16), own_grads, 1, 0)
            prob_grad = contract(value_rows[...], own_grads, 1, 1)
            center = jnp.sum(prob_grad * probs, axis=0, keepdims=True)
            score_grad = (probs * (prob_grad - center)).astype(jnp.bfloat16)
            key_sum[...] += contract(score_grad, own_rows, 1, 0)
            parts.append(contract(score_grad, key_rows[...], 0, 0))
        query_grad[at, :] = (
            jnp.where(lanes < size, parts[0], parts[1]) * scale
        ).astype(query_grad.dtype)
        return 0

    lax.fori_loop(0, queries.shape[0] // ROWS, some_rows, 0)
    key_grad[...] = key_sum[...].astype(key_grad.dtype)
    value_grad[...] = value_sum[...].astype(value_grad.dtype)


def column(rows, width, offset):
    return pl.BlockSpec((rows, width), lambda pair: (0, offset + pair))


def run_attend(qkv):
    length, across = qkv.shape
    model = across // 3
    pairs = model // 128
    return pl.pallas_call(
        attend,
        grid=(pairs,),
        in_specs=[column(length, 128, pairs * part) for part in range(3)],
        out_specs=[column(length, 128, 0), pl.BlockSpec((16, length), lambda pair: (pair, 0))],
        out_shape=(
            jax.ShapeDtypeStruct((length, model), jnp.bfloat16),
            jax.ShapeDtypeStruct((16 * pairs, length), jnp.float32),
        ),
        compiler_params=pltpu.CompilerParams(vmem_limit_bytes=40 << 20),
        cost_estimate=pl.CostEstimate(flops=4 * length * length * model, bytes_accessed=8 * length * model, transcendentals=length * length * 12),
    )(qkv, qkv, qkv)


def run_attend_back(qkv, logsum, grads):
    length, across = qkv.shape
    model = across // 3
    pairs = model // 128
    part = jax.ShapeDtypeStruct((length, model), jnp.bfloat16)
    return pl.pallas_call(
        attend_back,
        grid=(pairs,),
        in_specs=[column(length, 128, pairs * part) for part in range(3)]
        + [pl.BlockSpec((16, length), lambda pair: (pair, 0)), column(length, 128, 0)],
        out_specs=[column(length, 128, 0)] * 3,
        out_shape=(part, part, part),
        scratch_shapes=[pltpu.VMEM((length, 128), jnp.float32)] * 2,
        compiler_params=pltpu.CompilerParams(vmem_limit_bytes=40 << 20),
        cost_estimate=pl.CostEstimate(flops=10 * length * length * model, bytes_accessed=16 * length * model, transcendentals=length * length * 12),
    )(qkv, qkv, qkv, logsum, grads)


def on_device(
    tokens_in,
    char_ids,
    char_lengths,
    out_grad,
    w_qkv,
    first_qkv,
    second_qkv,
    w_out,
    first_out,
    second_out,
    w_up,
    first_up,
    second_up,
    w_down,
    first_down,
    second_down,
    w_gru,
    first_gru,
    second_gru,
    w_blend,
    first_blend,
    second_blend,
    char_table,
    first_table,
    second_table,
    gains,
    first_gains,
    second_gains,
):
    masters = (w_qkv, w_out, w_up, w_down, w_gru, w_blend, char_table, gains)
    firsts = (
        first_qkv,
        first_out,
        first_up,
        first_down,
        first_gru,
        first_blend,
        first_table,
        first_gains,
    )
    seconds = (
        second_qkv,
        second_out,
        second_up,
        second_down,
        second_gru,
        second_blend,
        second_table,
        second_gains,
    )
    parts = lax.axis_size("stream") * lax.axis_size("dp")
    on_first = lax.axis_index("stream") == 0
    half_len = tokens_in.shape[1]
    flow = Flow()

    def both_halves(pair, got):
        kept = jnp.where(on_first, pair[0], pair[1])
        return jnp.where(
            on_first, jnp.concatenate([kept, got], 0), jnp.concatenate([got, kept], 0)
        )

    groups = 3
    by_group = w_qkv.reshape(w_qkv.shape[0], 3, groups, -1).transpose(0, 2, 1, 3)
    by_group = by_group.reshape(w_qkv.shape[0], groups, -1)
    ids_row = jnp.where(on_first, char_ids[0], char_ids[1])
    lengths_row = jnp.where(on_first, char_lengths[0], char_lengths[1])
    segment = char_segments(lengths_row, ids_row.shape[0])
    shares = 1.0 / lengths_row.astype(jnp.float32)[:, None]
    ends = jnp.cumsum(lengths_row)

    flow.begin("tokens", swap_chain(jnp.where(on_first, tokens_in[1], tokens_in[0])), [4])
    flow.begin("first", gather_chain([by_group[:, 0]], False))
    flow.begin("second", gather_chain([by_group[:, 1]], True))
    flow.slot(())
    flow.slot(())
    flow.begin("third", gather_chain([by_group[:, 2], w_out], True))
    flow.slot(())
    shards = flow.slot((char_table, w_gru, gains_row(gains), w_blend))
    flow.begin("up", gather_chain([w_up], True), [0, 0, 0, 1, 0])
    shapes = shapes_of(shards[:3], 1)
    packed = jnp.concatenate([to_rows(shard, 1)[0] for shard in shards[:3]], 0)
    rest = gather_whole(packed, shapes)
    blend_all = lax.all_gather(
        shards[3].astype(jnp.bfloat16), ("stream", "dp"), axis=0, tiled=True
    )
    flow.slot(())
    tokens = both_halves(tokens_in, flow.end("tokens"))
    (w_first,) = flow.end("first")
    (w_second,) = flow.end("second")
    flow.begin("down", gather_chain([w_down], True), [0, 0, 0, 1, 0])
    flow.begin("out_grad", swap_chain(jnp.where(on_first, out_grad[1], out_grad[0])), [2])
    qkv_parts, contexts, logsums = [], [], []

    def attend_group(w_group):
        qkv = product(tokens, w_group).astype(jnp.bfloat16)
        context, logsum = run_attend(qkv)
        return qkv, context, logsum

    qkv, context, logsum = attend_group(w_first)
    qkv, context, logsum, tokens = flow.slot((qkv, context, logsum, tokens))
    qkv_parts.append(qkv)
    contexts.append(context)
    logsums.append(logsum)
    qkv, context, logsum = attend_group(w_second)
    qkv, context, logsum, tokens = flow.slot((qkv, context, logsum, tokens))
    qkv_parts.append(qkv)
    contexts.append(context)
    logsums.append(logsum)
    w_third, out_all = flow.end("third")
    qkv, context, logsum = attend_group(w_third)
    qkv, context, logsum, tokens = flow.slot((qkv, context, logsum, tokens))
    qkv_parts.append(qkv)
    contexts.append(context)
    logsums.append(logsum)
    context = jnp.concatenate(contexts, 1)
    mixed_sum = tokens.astype(jnp.float32) + product(context, out_all)
    mixed_sum, rest = flow.slot((mixed_sum, rest))
    table_all, gru_all, gain_all = rest
    gain_all = gain_all.reshape(parts, -1, D)[:, 0, : gains.size]
    gain_all = gain_all.reshape(parts, 3, -1).transpose(1, 0, 2).reshape(3, -1).astype(jnp.float32)
    letters, before, pooled = run_chars(ids_row, ends, table_all, gru_all, shares)
    letters, before, pooled, mixed_sum = flow.slot((letters, before, pooled, mixed_sum))
    normed = norm_gain(mixed_sum, gain_all[0])
    (up_all,) = flow.end("up")
    hidden = product(normed.astype(jnp.bfloat16), up_all)
    active = jax.nn.gelu(hidden).astype(jnp.bfloat16)
    active, hidden, normed = flow.slot((active, hidden, normed))
    (down_all,) = flow.end("down")
    summed = normed + product(active, down_all)
    feature = norm_gain(summed, gain_all[1]).astype(jnp.bfloat16)

    whole_grad = both_halves(out_grad, flow.end("out_grad"))
    joined = jnp.concatenate([feature, pooled], 1)
    stacked = jnp.concatenate([rows_before(joined), joined, rows_after(joined)], 1)
    blend_in = product(stacked, blend_all)
    blended, gelu_pull = jax.vjp(jax.nn.gelu, blend_in)
    result, norm_pull = jax.vjp(norm_gain, feature.astype(jnp.float32) + blended, gain_all[2])
    total_grad, gain_blend = norm_pull(whole_grad.astype(jnp.float32))
    blend_grad = gelu_pull(total_grad)[0].astype(jnp.bfloat16)
    grad_blend = inner_rows(stacked, blend_grad)
    stacked_grad = inner_cols(blend_grad, blend_all)
    pair_width = joined.shape[1]
    joined_grad = (
        stacked_grad[:, pair_width : 2 * pair_width]
        + rows_after(stacked_grad[:, :pair_width])
        + rows_before(stacked_grad[:, 2 * pair_width :])
    )
    feature_grad = (total_grad + joined_grad[:, :D]).astype(jnp.bfloat16)
    result = result.astype(jnp.bfloat16)
    flow.begin(
        "result", swap_chain(jnp.where(on_first, result[half_len:], result[:half_len])), [2]
    )
    (blend_sum,) = scatter_whole([grad_blend])

    summed_grad, gain_ffn = jax.vjp(norm_gain, summed, gain_all[1])[1](
        feature_grad.astype(jnp.float32)
    )
    ffn_grad = summed_grad.astype(jnp.bfloat16)
    grad_down = inner_rows(active, ffn_grad).astype(jnp.bfloat16)
    hidden_grad = jax.vjp(jax.nn.gelu, hidden)[1](inner_cols(ffn_grad, down_all))[0].astype(
        jnp.bfloat16
    )
    grad_up = inner_rows(normed.astype(jnp.bfloat16), hidden_grad).astype(jnp.bfloat16)
    normed_grad = summed_grad + inner_cols(hidden_grad, up_all)
    flow.begin("down", scatter_chain([grad_down], True))
    flow.begin("up", scatter_chain([grad_up], False))
    mixed_grad, gain_attn = jax.vjp(norm_gain, mixed_sum, gain_all[0])[1](normed_grad)
    attended_grad = mixed_grad.astype(jnp.bfloat16)
    grad_out = inner_rows(context, attended_grad).astype(jnp.bfloat16)
    context_grad = inner_cols(attended_grad, out_all).astype(jnp.bfloat16)
    gain_grads = jnp.stack([gain_attn, gain_ffn, gain_blend])
    state_grad = joined_grad[:, D:]
    context_grad, grad_out, gain_grads, mixed_grad, state_grad = flow.slot(
        (context_grad, grad_out, gain_grads, mixed_grad, state_grad)
    )
    grad_gru, grad_table = run_chars_back(
        ids_row, segment, state_grad, shares, table_all, gru_all, letters, before
    )
    context_grad, grad_gru, grad_table = flow.slot((context_grad, grad_gru, grad_table))
    flow.begin("letters", scatter_chain([grad_gru, grad_table, grad_out], True))
    gain_rows = gain_grads.reshape(3, parts, -1).transpose(1, 0, 2).reshape(parts, -1)
    gain_rows = jnp.pad(gain_rows[:, None], ((0, 0), (0, 7), (0, D - gain_rows.shape[1])))
    gain_rows = gain_rows.reshape(8 * parts, D)
    tokens_grad = mixed_grad
    weights = (w_first, w_second, w_third)
    for number in range(groups):
        width = context_grad.shape[1] // groups
        qkv_grad = jnp.concatenate(
            run_attend_back(
                qkv_parts[number],
                logsums[number],
                context_grad[:, number * width : number * width + width],
            ),
            1,
        )
        grad_group = inner_rows(tokens, qkv_grad).astype(jnp.bfloat16)
        tokens_grad = tokens_grad + inner_cols(qkv_grad, weights[number])
        if number < 2:
            context_grad, grad_group, tokens_grad = flow.slot(
                (context_grad, grad_group, tokens_grad)
            )
        grads = [grad_group, gain_rows] if number == 0 else [grad_group]
        flow.begin("qkv%d" % number, scatter_chain(grads, number % 2 == 1))
    tokens_grad = tokens_grad.astype(jnp.bfloat16)
    flow.begin(
        "tokens", swap_chain(jnp.where(on_first, tokens_grad[half_len:], tokens_grad[:half_len])), [4]
    )
    while flow.live:
        flow.slot(())
    own_result = jnp.where(on_first, result[:half_len], result[half_len:])
    own_grad = jnp.where(on_first, tokens_grad[:half_len], tokens_grad[half_len:])
    back_result, back_grad = flow.end("result"), flow.end("tokens")
    block_parts = [
        jnp.where(on_first, own_result, back_result),
        jnp.where(on_first, back_result, own_result),
    ]
    grad_parts = [
        jnp.where(on_first, own_grad, back_grad),
        jnp.where(on_first, back_grad, own_grad),
    ]
    first_sum, gain_sum = flow.end("qkv0")
    group_sums = jnp.stack([first_sum, flow.end("qkv1")[0], flow.end("qkv2")[0]], 1)
    qkv_sum = group_sums.reshape(w_qkv.shape[0], groups, 3, -1).transpose(0, 2, 1, 3)
    letter_sums = flow.end("letters")
    sums = (
        qkv_sum.reshape(w_qkv.shape),
        letter_sums[2],
        flow.end("up")[0],
        flow.end("down")[0],
        letter_sums[0],
        blend_sum,
        letter_sums[1],
        gain_sum[0, : gains.size].reshape(gains.shape),
    )
    rates = step_rates()
    results = [
        adamw(masters[number], firsts[number], seconds[number], sums[number], rates[number])
        for number in range(8)
    ]
    return (
        jnp.stack(block_parts),
        jnp.stack(grad_parts),
        results[0][0],
        results[0][1],
        results[0][2],
        results[1][0],
        results[1][1],
        results[1][2],
        results[2][0],
        results[2][1],
        results[2][2],
        results[3][0],
        results[3][1],
        results[3][2],
        results[4][0],
        results[4][1],
        results[4][2],
        results[5][0],
        results[5][1],
        results[5][2],
        results[6][0],
        results[6][1],
        results[6][2],
        results[7][0],
        results[7][1],
        results[7][2],
    )


def solution(mesh):
    in_specs = (
        P("dp", "stream", None),
        P("dp", None),
        P("dp", None),
        P("dp", "stream", None),
        P(("stream", "dp"), None),
        P(("stream", "dp"), None),
        P(("stream", "dp"), None),
        P(("stream", "dp"), None),
        P(("stream", "dp"), None),
        P(("stream", "dp"), None),
        P(("stream", "dp"), None),
        P(("stream", "dp"), None),
        P(("stream", "dp"), None),
        P(("stream", "dp"), None),
        P(("stream", "dp"), None),
        P(("stream", "dp"), None),
        P(("stream", "dp"), None),
        P(("stream", "dp"), None),
        P(("stream", "dp"), None),
        P(("stream", "dp"), None),
        P(("stream", "dp"), None),
        P(("stream", "dp"), None),
        P(("stream", "dp"), None),
        P(("stream", "dp"), None),
        P(("stream", "dp"), None),
        P(None, ("stream", "dp")),
        P(None, ("stream", "dp")),
        P(None, ("stream", "dp")),
    )
    out_specs = (
        P("dp", "stream", None),
        P("dp", "stream", None),
        P(("stream", "dp"), None),
        P(("stream", "dp"), None),
        P(("stream", "dp"), None),
        P(("stream", "dp"), None),
        P(("stream", "dp"), None),
        P(("stream", "dp"), None),
        P(("stream", "dp"), None),
        P(("stream", "dp"), None),
        P(("stream", "dp"), None),
        P(("stream", "dp"), None),
        P(("stream", "dp"), None),
        P(("stream", "dp"), None),
        P(("stream", "dp"), None),
        P(("stream", "dp"), None),
        P(("stream", "dp"), None),
        P(("stream", "dp"), None),
        P(("stream", "dp"), None),
        P(("stream", "dp"), None),
        P(("stream", "dp"), None),
        P(("stream", "dp"), None),
        P(("stream", "dp"), None),
        P(None, ("stream", "dp")),
        P(None, ("stream", "dp")),
        P(None, ("stream", "dp")),
    )
    return jax.shard_map(
        on_device, mesh=mesh, in_specs=in_specs, out_specs=out_specs, check_vma=False
    )
```

```python
import functools

import jax
import jax.numpy as jnp
from jax import lax
from jax.experimental import pallas as pl
from jax.experimental.pallas import tpu as pltpu
from jax.sharding import PartitionSpec as P

D = 768
HEADS = 12
FF = 3072
LEN = 1024
STEP = 5


def to_rows(matrix, parts):
    side = matrix.shape[1] // D
    own = matrix.shape[0] // parts
    blocks = matrix.astype(jnp.bfloat16).reshape(parts, own, side, D)
    return blocks.transpose(0, 2, 1, 3).reshape(parts, side * own, D)


def from_rows(rows, offset, own, side):
    parts = rows.shape[0]
    blocks = rows[:, offset : offset + own * side].reshape(parts, side, own, D)
    return blocks.transpose(0, 2, 1, 3).reshape(parts * own, side * D)


def gains_row(gains):
    return jnp.pad(gains.reshape(1, -1), ((0, 7), (0, D - gains.size)))


def swap(block, mask):
    parts = lax.axis_size("dp") * lax.axis_size("stream")
    return lax.ppermute(block, ("stream", "dp"), [(place, place ^ mask) for place in range(parts)])


def pair_bits():
    return (lax.axis_size("dp") * lax.axis_size("stream")).bit_length() - 2


def in_pairs(shapes):
    parts = lax.axis_size("dp") * lax.axis_size("stream")
    return parts >= 8 and parts & (parts - 1) == 0 and all(rows % 8 == 0 for rows, _ in shapes)


def my_place():
    return (lax.axis_index("stream") * lax.axis_size("dp") + lax.axis_index("dp")).reshape(1)


def shapes_of(matrices, parts):
    return [(matrix.shape[0] // parts, matrix.shape[1] // D) for matrix in matrices]


def assemble(shapes, place, mine, theirs, *weights):
    core = place[0] & 1
    low = (place[0] >> 1) & 3
    pieces = []
    for pair in range(4):
        own = mine[pair ^ low].astype(jnp.float32)
        other = theirs[pair ^ low].astype(jnp.float32)
        pieces.append(jnp.where(core == 0, own, other))
        pieces.append(jnp.where(core == 0, other, own))
    offset = 0
    for (rows, side), weight in zip(shapes, weights):
        for number in range(side):
            block = jnp.concatenate([piece[offset : offset + rows] for piece in pieces], 0)
            weight[:, number * D : number * D + D] = block.astype(weight.dtype)
            offset += rows


def apart(shapes, place, *refs):
    grads, keep, send = refs[: len(shapes)], refs[-2], refs[-1]
    core = place[0] & 1
    low = (place[0] >> 1) & 3
    for pair in range(4):
        halves = []
        for side in range(2):
            pieces = []
            for (rows, across), grad in zip(shapes, grads):
                first = (2 * pair + side) * rows
                for number in range(across):
                    pieces.append(
                        grad[first : first + rows, number * D : number * D + D].astype(jnp.float32)
                    )
            halves.append(jnp.concatenate(pieces, 0))
        keep[pair ^ low] = jnp.where(core == 0, halves[0], halves[1]).astype(keep.dtype)
        send[pair ^ low] = jnp.where(core == 0, halves[1], halves[0]).astype(send.dtype)


def turned_block(high):
    return pl.BlockSpec((4, high, D), lambda group, place: (group ^ (place[0] >> 3), 0, 0))


def natural_block(shape):
    return pl.BlockSpec((8 * shape[0], shape[1] * D), lambda group, place: (group, 0))


class Flow:
    def __init__(self):
        self.live = {}
        self.ended = {}

    def begin(self, name, chain, skips=()):
        self.step(name, chain, None, list(skips))

    def step(self, name, chain, arrays, skips):
        try:
            waiting = chain.send(arrays)
            self.live[name] = [chain, waiting, skips, skips.pop(0) if skips else 0]
        except StopIteration as stop:
            self.ended[name] = stop.value

    def slot(self, values):
        due = [name for name, entry in self.live.items() if entry[3] == 0]
        for entry in self.live.values():
            entry[3] -= 1
        values, waited = lax.optimization_barrier(
            (values, [self.live[name][1] for name in due])
        )
        for name, arrays in zip(due, waited):
            chain, _, skips, _ = self.live.pop(name)
            self.step(name, chain, arrays, skips)
        return values

    def end(self, name):
        return self.ended.pop(name)


def gather_chain(shards, near_first=False):
    shapes = shapes_of(shards, 1)
    packed = jnp.concatenate([to_rows(shard, 1)[0] for shard in shards], 0)
    if not in_pairs(shapes):
        return gather_whole(packed, shapes)
    top = pair_bits()
    far = 1 << (top - 2)
    high = packed.shape[0]
    corner = 1 << top
    near = (2, corner, corner | 2)
    held = packed[None, None, None]
    for turn in range(2):
        if near_first == (turn == 0):
            held, *got = yield (held, *[swap(held, mask) for mask in near])
            held = jnp.concatenate(
                [jnp.concatenate([held, got[0]], 2), jnp.concatenate(got[1:], 2)], 0
            )
        else:
            held, *got = yield (held, *[swap(held, step << 2) for step in range(1, far)])
            held = jnp.concatenate([held, *got], 1)
    held = held.reshape(4 * far, high, D)
    held, other = yield (held, swap(held, 1))
    return join_halves(shapes, held, other)


def gather_steps(shards, turned):
    shapes = shapes_of(shards, 1)
    packed = jnp.concatenate([to_rows(shard, 1)[0] for shard in shards], 0)
    if not in_pairs(shapes):
        return gather_whole(packed, shapes)
    top = pair_bits()
    held = packed.reshape((1,) * top + packed.shape)
    for bit in list(range(2, top)) + ([1, top] if turned else [top, 1]):
        held, other = yield (held, swap(held, 1 << bit))
        held = jnp.concatenate([held, other], top - bit)
    held = held.reshape(1 << top, *packed.shape)
    held, other = yield (held, swap(held, 1))
    return join_halves(shapes, held, other)


def unpack(shapes, rows, *weights):
    pieces = [rows[number].astype(jnp.float32) for number in range(8)]
    offset = 0
    for (own, side), weight in zip(shapes, weights):
        for number in range(side):
            block = jnp.concatenate([piece[offset : offset + own] for piece in pieces], 0)
            weight[:, number * D : number * D + D] = block.astype(weight.dtype)
            offset += own


def unpack_rows(rows, shapes):
    parts, high = rows.shape[:2]
    if not in_pairs(shapes):
        return unpack_plain(rows, shapes)
    return pl.pallas_call(
        functools.partial(unpack, shapes),
        grid=(parts // 8,),
        in_specs=[pl.BlockSpec((8, high, D), lambda group: (group, 0, 0))],
        out_specs=[
            pl.BlockSpec((8 * own, side * D), lambda group: (group, 0)) for own, side in shapes
        ],
        out_shape=[
            jax.ShapeDtypeStruct((parts * own, side * D), jnp.bfloat16) for own, side in shapes
        ],
        compiler_params=pltpu.CompilerParams(vmem_limit_bytes=40 << 20),
        cost_estimate=spent(3),
    )(rows)


def unpack_plain(rows, shapes):
    pieces = []
    offset = 0
    for own, side in shapes:
        pieces.append(from_rows(rows, offset, own, side))
        offset += own * side
    return pieces


def gather_whole(packed, shapes):
    return unpack_rows(lax.all_gather(packed, ("stream", "dp"), axis=0, tiled=False), shapes)


def join_halves(shapes, mine, theirs):
    high = mine.shape[-2]
    pairs = 1 << pair_bits()
    parts = 2 * pairs
    return pl.pallas_call(
        functools.partial(assemble, shapes),
        grid_spec=pltpu.PrefetchScalarGridSpec(
            num_scalar_prefetch=1,
            grid=(pairs // 4,),
            in_specs=[turned_block(high)] * 2,
            out_specs=[natural_block(shape) for shape in shapes],
        ),
        out_shape=[
            jax.ShapeDtypeStruct((parts * rows, side * D), jnp.bfloat16) for rows, side in shapes
        ],
        compiler_params=pltpu.CompilerParams(vmem_limit_bytes=40 << 20),
        cost_estimate=spent(4),
    )(my_place(), mine.reshape(pairs, high, D), theirs.reshape(pairs, high, D))


def scatter_whole(grads):
    parts = lax.axis_size("dp") * lax.axis_size("stream")
    packed = jnp.concatenate([to_rows(grad, parts) for grad in grads], 1)
    total = lax.psum_scatter(
        packed.reshape(-1, D), ("stream", "dp"), scatter_dimension=0, tiled=True
    ).astype(jnp.float32)
    return own_pieces(total, shapes_of(grads, parts))


def own_pieces(total, shapes):
    pieces = []
    offset = 0
    for own, side in shapes:
        pieces.append(from_rows(total[None], offset, own, side))
        offset += own * side
    return pieces


def scatter_chain(grads, split=False):
    parts = lax.axis_size("dp") * lax.axis_size("stream")
    shapes = shapes_of(grads, parts)
    if not in_pairs(shapes):
        return scatter_whole(grads)
    pairs = parts // 2
    high = sum(rows * side for rows, side in shapes)
    half = jax.ShapeDtypeStruct((pairs, high, D), jnp.bfloat16)
    kept, sent = pl.pallas_call(
        functools.partial(apart, shapes),
        grid_spec=pltpu.PrefetchScalarGridSpec(
            num_scalar_prefetch=1,
            grid=(pairs // 4,),
            in_specs=[natural_block(shape) for shape in shapes],
            out_specs=[turned_block(high)] * 2,
        ),
        out_shape=[half, half],
        compiler_params=pltpu.CompilerParams(vmem_limit_bytes=40 << 20),
        cost_estimate=spent(4),
    )(my_place(), *[grad.astype(jnp.bfloat16) for grad in grads])
    kept, other = yield (kept, swap(sent, 1))
    top = pair_bits()
    far = 1 << (top - 2)
    corner = 1 << top
    near = [(1, 0), (0, 1), (1, 1)]
    quarter = jax.ShapeDtypeStruct((far, high, D), jnp.bfloat16)
    views = [
        pl.BlockSpec((1, 1, 1, high, D), lambda row, x=x, y=y: (x, row, y, 0, 0))
        for x, y in [(0, 0)] + near
    ]
    total, *sent = pl.pallas_call(
        sum_quarters,
        grid=(far,),
        in_specs=views + views,
        out_specs=[pl.BlockSpec((1, high, D), lambda row: (row, 0, 0))] * 4,
        out_shape=[jax.ShapeDtypeStruct(quarter.shape, jnp.float32)] + [quarter] * 3,
        compiler_params=pltpu.CompilerParams(vmem_limit_bytes=40 << 20),
        cost_estimate=spent(3),
    )(*[kept.reshape(2, far, 2, high, D)] * 4, *[other.reshape(2, far, 2, high, D)] * 4)
    got = [swap(sent[0], corner), swap(sent[1], 2)]
    if split:
        total, last, *got = yield (total, sent[2], *got)
        total, got, last = yield (total, got, swap(last, corner | 2))
    else:
        total, last, *got = yield (total, swap(sent[2], corner | 2), *got)
    total = total + sum(block.astype(jnp.float32) for block in [last, *got])
    others = [
        swap(total[number].astype(jnp.bfloat16), number << 2) for number in range(1, far)
    ]
    kept, *others = yield (total[0], *others)
    total = kept + sum(other.astype(jnp.float32) for other in others)
    return own_pieces(total, shapes)


def sum_quarters(*refs):
    for former, latter, out in zip(refs[:4], refs[4:8], refs[8:]):
        total = former[0, 0, 0].astype(jnp.float32) + latter[0, 0, 0].astype(jnp.float32)
        out[0] = total.astype(out.dtype)


def swap_chain(block):
    other = yield swap(block, lax.axis_size("dp"))
    return other


def product(former, latter):
    return jnp.dot(former, latter, preferred_element_type=jnp.float32)


def inner_rows(former, latter):
    return lax.dot_general(
        former, latter, (((0,), (0,)), ((), ())), preferred_element_type=jnp.float32
    )


def inner_cols(former, latter):
    return lax.dot_general(
        former, latter, (((1,), (1,)), ((), ())), preferred_element_type=jnp.float32
    )


def norm_gain(values, scales):
    center = jnp.mean(values, axis=-1, keepdims=True)
    shifted = values - center
    spread = jnp.mean(shifted * shifted, axis=-1, keepdims=True)
    return shifted * lax.rsqrt(spread + 1e-05) * scales


def rows_before(matrix):
    return jnp.concatenate([jnp.zeros_like(matrix[:1]), matrix[:-1]], 0)


def rows_after(matrix):
    return jnp.concatenate([matrix[1:], jnp.zeros_like(matrix[:1])], 0)


def char_segments(lengths, char_count):
    starts = jnp.cumsum(lengths) - lengths
    markers = jnp.zeros((char_count,), jnp.int32).at[starts].add(1)
    return jnp.cumsum(markers) - 1


def step_rates():
    return (
        0.5 * D ** (-0.5),
        0.5 * (3 * D // LEN) ** (-0.5),
        0.5 * D ** (-0.5),
        0.5 * FF ** (-0.5),
        0.5 * D ** (-0.5),
        0.5 * (6 * D) ** (-0.5),
        0.5,
        0.2,
    )


def adamw(master, first_m, second_m, grad_sum, step_rate):
    mean_new = 0.5 * first_m + 0.5 * grad_sum
    power = 0.5 * second_m + 0.5 * grad_sum * grad_sum
    correct = 1.0 - 0.5**STEP
    fresh_w = master - step_rate * (
        mean_new / correct / (jnp.sqrt(power / correct) + 1e-08) + 0.01 * master
    )
    return (fresh_w, mean_new, power)


STEP_ROWS = 512


def spent(microseconds):
    return pl.CostEstimate(
        flops=int(microseconds * 1e9), bytes_accessed=1, transcendentals=0
    )


UNROLL = 16


def contract(former, latter, left, right):
    return lax.dot_general(
        former, latter, (((left,), (right,)), ((), ())), preferred_element_type=jnp.float32
    )


def lane_blocks(width):
    blocks = []
    for number in range(2 * width // 128):
        side, lane = divmod(number * 128, width)
        blocks.append((number * 128, 2 * side * width + lane, 4 * side + lane // 128))
    return blocks


def eight(offset):
    return pl.ds(pl.multiple_of(offset, 8), 8)


def chars_ahead(rows_f, rows_b, ends, table, w_gru, shares, letters, before, pooled, running, spans, carry):
    block = pl.program_id(0)
    total = rows_f.shape[0]
    width = w_gru.shape[1] // 4

    @pl.when(block == 0)
    def start():
        logits = jnp.dot(table[...], w_gru[...], preferred_element_type=jnp.float32)
        letters[...] = jnp.zeros_like(letters)
        carry[...] = jnp.zeros_like(carry)
        for _, left, place in lane_blocks(width):
            update = jax.nn.sigmoid(logits[:, left : left + 128])
            letters[:, place, :] = 1.0 - update
            letters[:, 8 + place, :] = update * logits[:, left + width : left + width + 128]

    leading = lax.broadcasted_iota(jnp.int32, (8, 128), 0) < 4

    def several(group, held):
        state, total_state = held
        first = block * STEP_ROWS + group * UNROLL
        factors, adds = [], []
        for inner in range(UNROLL):
            id_f, id_b = rows_f[first + inner], rows_b[first + inner]
            factors.append(jnp.where(leading, letters[id_f, 0:8], letters[id_b, 0:8]))
            adds.append(jnp.where(leading, letters[id_f, 8:16], letters[id_b, 8:16]))
        for inner in range(UNROLL):
            before[group * UNROLL + inner] = state
            running[first + inner] = total_state
            state = factors[inner] * state + adds[inner]
            total_state = total_state + state
        return state, total_state

    state, total_state = lax.fori_loop(0, STEP_ROWS // UNROLL, several, (carry[0], carry[1]))
    carry[0] = state
    carry[1] = total_state

    @pl.when(block == pl.num_programs(0) - 1)
    def finish():
        running[total] = total_state

        def tokens(group, prior):
            found = []
            for inner in range(UNROLL):
                end = ends[group * UNROLL + inner]
                found.append(jnp.where(leading, running[end], -running[total - end]))
            for inner in range(UNROLL):
                spans[group * UNROLL + inner] = found[inner] - prior
                prior = found[inner]
            return prior

        lax.fori_loop(0, ends.shape[0] // UNROLL, tokens, jnp.where(leading, running[0], -running[total]))
        for at, _, place in lane_blocks(width):
            pooled[:, at : at + 128] = (spans[:, place, :] * shares[...]).astype(pooled.dtype)


def chars_back(blocks, opening, closing, *refs):
    rows_f, rows_b, owners_f, owners_b, letters, before = refs[:6]
    rest = list(refs[6:])
    take = lambda count: [rest.pop(0) for _ in range(count)]
    if opening:
        upstream, shares = take(2)
    else:
        spread, carry_in, *sums_in = take(6)
    if closing:
        table, w_gru = take(2)
    if opening:
        (spread,) = take(1)
    if closing:
        grad_gru, grad_table = take(2)
    else:
        carry_out, *sums_out = take(5)
    *sums, carry = take(5)
    if closing:
        (full,) = take(1)
    sums_f, sums_b, more_f, more_b = sums
    step_number = pl.program_id(0)
    block = blocks[0] - 1 - step_number
    width = 384

    @pl.when(step_number == 0)
    def start():
        if opening:
            for held in sums:
                held[...] = jnp.zeros_like(held)
            carry[...] = jnp.zeros_like(carry)
            for at, _, place in lane_blocks(width):
                spread[:, place, :] = upstream[:, at : at + 128] * shares[...]
            for place in (3, 7):
                spread[:, place, :] = jnp.zeros((spread.shape[0], 128), jnp.float32)
        else:
            for held, given in zip(sums, sums_in):
                held[...] = given[...]
            carry[...] = carry_in[...]

    leading = lax.broadcasted_iota(jnp.int32, (8, 128), 0) < 4

    def several(group, passed):
        steps = [STEP_ROWS - 1 - group * UNROLL - inner for inner in range(UNROLL)]
        kept, given, priors, owned = [], [], [], []
        for step in steps:
            place = block * STEP_ROWS + step
            id_f, id_b = rows_f[place], rows_b[place]
            owned.append((id_f, id_b))
            kept.append(jnp.where(leading, letters[id_f, 0:8], letters[id_b, 0:8]))
            given.append(jnp.where(leading, spread[owners_f[place]], spread[owners_b[place]]))
            priors.append(before[step])
        for inner in range(UNROLL):
            carried = given[inner] + passed
            passed = kept[inner] * carried
            moved = carried * priors[inner]
            id_f, id_b = owned[inner]
            for held, row, value in (
                (
                    (sums_f, more_f)[inner % 2],
                    id_f,
                    jnp.where(leading, carried, pltpu.roll(moved, 4, 0)),
                ),
                (
                    (sums_b, more_b)[inner % 2],
                    id_b,
                    jnp.where(leading, pltpu.roll(carried, 4, 0), moved),
                ),
            ):
                held[row] += value
        return passed

    carry[...] = lax.fori_loop(0, STEP_ROWS // UNROLL, several, carry[...])

    @pl.when(step_number == pl.num_programs(0) - 1)
    def finish():
        if not closing:
            carry_out[...] = carry[...]
            for held, given in zip(sums, sums_out):
                given[...] = held[...]
            return
        sums_f[...] += more_f[...]
        sums_b[...] += more_b[...]
        for _, left, place in lane_blocks(width):
            found = sums_f if place < 4 else sums_b
            lane = place % 4
            kept = letters[:, place, :]
            update = 1.0 - kept
            total = found[:, lane, :]
            full[:, left : left + 128] = kept * (
                letters[:, 8 + place, :] * total - update * found[:, 4 + lane, :]
            )
            full[:, left + width : left + width + 128] = update * total
        upper = full[...].astype(jnp.bfloat16)
        lower = (full[...] - upper.astype(jnp.float32)).astype(jnp.bfloat16)
        grad_gru[...] = (
            contract(table[...], upper, 0, 0) + contract(table[...], lower, 0, 0)
        ).astype(grad_gru.dtype)
        grad_table[...] = (
            contract(upper, w_gru[...], 1, 1) + contract(lower, w_gru[...], 1, 1)
        ).astype(grad_table.dtype)


def whole(array):
    return pl.BlockSpec(array.shape, lambda block: (0,) * len(array.shape))


def scalars():
    return pl.BlockSpec(memory_space=pltpu.SMEM)


def run_chars(ids, ends, table, w_gru, shares):
    total, count = ids.shape[0], shares.shape[0]
    f32 = jnp.float32
    outs = (
        jax.ShapeDtypeStruct((table.shape[0], 16, 128), f32),
        jax.ShapeDtypeStruct((total, 8, 128), f32),
        jax.ShapeDtypeStruct((count, w_gru.shape[1] // 2), jnp.bfloat16),
    )
    return pl.pallas_call(
        chars_ahead,
        grid=(total // STEP_ROWS,),
        in_specs=[scalars(), scalars(), scalars(), whole(table), whole(w_gru), whole(shares)],
        out_specs=[
            whole(outs[0]),
            pl.BlockSpec((STEP_ROWS, 8, 128), lambda block: (block, 0, 0)),
            whole(outs[2]),
        ],
        out_shape=outs,
        scratch_shapes=[
            pltpu.VMEM((total + 1, 8, 128), f32),
            pltpu.VMEM((count, 8, 128), f32),
            pltpu.VMEM((2, 8, 128), f32),
        ],
        compiler_params=pltpu.CompilerParams(vmem_limit_bytes=56 << 20),
        cost_estimate=spent(24),
    )(ids, jnp.flip(ids), ends, table, w_gru, shares)


def run_chars_back(last, count, ids, owners, letters, before, *, upstream=None, held=None, ends=None):
    f32 = jnp.float32
    tile = jax.ShapeDtypeStruct((letters.shape[0], 8, 128), f32)
    flat = jax.ShapeDtypeStruct((8, 128), f32)
    inputs = [ids, jnp.flip(ids), owners, jnp.flip(owners), letters, before]
    blocks = [scalars()] * 4 + [
        whole(letters),
        pl.BlockSpec((STEP_ROWS, 8, 128), lambda block: (last - 1 - block, 0, 0)),
    ]
    outs = []
    if upstream is not None:
        inputs += upstream
        outs.append(jax.ShapeDtypeStruct((upstream[0].shape[0], 8, 128), f32))
    else:
        inputs += held
    if ends is not None:
        inputs += ends
        outs.append(jax.ShapeDtypeStruct(ends[1].shape, jnp.bfloat16))
        outs.append(jax.ShapeDtypeStruct(ends[0].shape, jnp.bfloat16))
    else:
        outs += [flat] + [tile] * 4
    blocks += [whole(array) for array in inputs[6:]]
    scratch = [pltpu.VMEM(tile.shape, f32)] * 4 + [pltpu.VMEM(flat.shape, f32)]
    if ends is not None:
        scratch.append(pltpu.VMEM((ends[0].shape[0], ends[1].shape[1]), f32))
    return pl.pallas_call(
        functools.partial(chars_back, (last,), upstream is not None, ends is not None),
        grid=(count,),
        in_specs=blocks,
        out_specs=[whole(out) for out in outs],
        out_shape=outs,
        scratch_shapes=scratch,
        compiler_params=pltpu.CompilerParams(vmem_limit_bytes=56 << 20),
        cost_estimate=spent(6 * count),
    )(*inputs)


def attend(queries, key_rows, value_rows, context, logsum):
    size = key_rows.shape[1] // 2
    lanes = lax.broadcasted_iota(jnp.int32, (1, 2 * size), 1)
    scale = size ** (-0.5)
    parts = []
    sums = []
    for head in range(2):
        own = (lanes < size) if head == 0 else (lanes >= size)
        scores = contract(jnp.where(own, queries[...], 0) * scale, key_rows[...], 1, 1)
        row_max = jnp.max(scores, axis=-1, keepdims=True)
        exponent = jnp.exp(scores - row_max)
        row_total = jnp.sum(exponent, axis=-1, keepdims=True)
        parts.append(
            contract(exponent.astype(jnp.bfloat16), value_rows[...], 1, 0) * (1.0 / row_total)
        )
        sums.append(row_max + jnp.log(row_total))
    context[...] = jnp.where(lanes < size, parts[0], parts[1]).astype(context.dtype)
    turned = jnp.transpose(jnp.where(lanes < size, sums[0], sums[1]))
    logsum[0:8, :] = turned[0:8]
    logsum[8:16, :] = turned[size : size + 8]


def attend_back(queries, key_rows, value_rows, logsum, grads, query_grad, key_grad, value_grad):
    size = key_rows.shape[1] // 2
    lanes = lax.broadcasted_iota(jnp.int32, (1, 2 * size), 1)
    scale = size ** (-0.5)
    parts = []
    key_sum, value_sum = 0.0, 0.0
    for head in range(2):
        own = (lanes < size) if head == 0 else (lanes >= size)
        own_rows = jnp.where(own, queries[...], 0) * scale
        own_grads = jnp.where(own, grads[...], 0)
        scores = contract(key_rows[...], own_rows, 1, 1)
        probs = jnp.exp(scores - logsum[8 * head : 8 * head + 1, :])
        value_sum = value_sum + contract(probs.astype(jnp.bfloat16), own_grads, 1, 0)
        prob_grad = contract(value_rows[...], own_grads, 1, 1)
        center = jnp.sum(prob_grad * probs, axis=0, keepdims=True)
        score_grad = (probs * (prob_grad - center)).astype(jnp.bfloat16)
        key_sum = key_sum + contract(score_grad, own_rows, 1, 0)
        parts.append(contract(score_grad, key_rows[...], 0, 0))
    query_grad[...] = (jnp.where(lanes < size, parts[0], parts[1]) * scale).astype(query_grad.dtype)
    key_grad[...] = key_sum.astype(key_grad.dtype)
    value_grad[...] = value_sum.astype(value_grad.dtype)


def column(rows, width, offset):
    return pl.BlockSpec((rows, width), lambda pair: (0, offset + pair))


def run_attend(qkv, first, pairs):
    length, across = qkv.shape
    every = across // 384
    return pl.pallas_call(
        attend,
        grid=(pairs,),
        in_specs=[column(length, 128, every * part + first) for part in range(3)],
        out_specs=[column(length, 128, 0), pl.BlockSpec((16, length), lambda pair: (pair, 0))],
        out_shape=(
            jax.ShapeDtypeStruct((length, 128 * pairs), jnp.bfloat16),
            jax.ShapeDtypeStruct((16 * pairs, length), jnp.float32),
        ),
        compiler_params=pltpu.CompilerParams(vmem_limit_bytes=40 << 20),
        cost_estimate=spent(5 * pairs),
    )(qkv, qkv, qkv)


def run_attend_back(qkv, logsum, grads, first, pairs):
    length, across = qkv.shape
    every = across // 384
    part = jax.ShapeDtypeStruct((length, 128 * pairs), jnp.bfloat16)
    return pl.pallas_call(
        attend_back,
        grid=(pairs,),
        in_specs=[column(length, 128, every * part + first) for part in range(3)]
        + [
            pl.BlockSpec((16, length), lambda pair: (first + pair, 0)),
            column(length, 128, first),
        ],
        out_specs=[column(length, 128, 0)] * 3,
        out_shape=(part, part, part),
        compiler_params=pltpu.CompilerParams(vmem_limit_bytes=40 << 20),
        cost_estimate=spent(1),
    )(qkv, qkv, qkv, logsum, grads)


CHUNK = 512
SLOPE = 0.7978845608028654


def gelu_pair(values):
    square = values * values
    curve = jnp.tanh(SLOPE * values * (1.0 + 0.044715 * square))
    half = 0.5 * (1.0 + curve)
    slope = half + (0.5 * SLOPE) * values * (1.0 - curve * curve) * (1.0 + 3 * 0.044715 * square)
    return values * half, slope


def unit(values):
    center = jnp.mean(values, axis=-1, keepdims=True)
    shifted = values - center
    spread = jnp.mean(shifted * shifted, axis=-1, keepdims=True)
    root = lax.rsqrt(spread + 1e-05)
    return shifted * root, root


def unit_back(normal, root, given):
    return (
        given
        - jnp.mean(given, axis=-1, keepdims=True)
        - normal * jnp.mean(given * normal, axis=-1, keepdims=True)
    ) * root


def column_sum(values):
    return jnp.sum(values.reshape(-1, 8, values.shape[1]), axis=0)


def feed_ahead(mixed, gains, up, down, summed, feature):
    normal, _ = unit(mixed[...])
    normed = normal * gains[0:1]
    hidden = contract(normed.astype(jnp.bfloat16), up[...], 1, 0)
    active, _ = gelu_pair(hidden)
    total = normed + contract(active.astype(jnp.bfloat16), down[...], 1, 0)
    summed[...] = total
    normal, _ = unit(total)
    feature[...] = (normal * gains[1:2]).astype(feature.dtype)


def feed_back(
    mixed, summed, feature_grad, gains, up, down, out,
    active_out, hidden_grad, ffn_out, normed_out, mixed_grad, attended, context_grad, gain_sums
):
    @pl.when(pl.program_id(0) == 0)
    def start():
        gain_sums[...] = jnp.zeros_like(gain_sums)

    normal, root = unit(summed[...])
    given = feature_grad[...].astype(jnp.float32)
    gain_sums[8:16] += column_sum(given * normal)
    summed_grad = unit_back(normal, root, given * gains[1:2])
    ffn_grad = summed_grad.astype(jnp.bfloat16)
    ffn_out[...] = ffn_grad
    normal, root = unit(mixed[...])
    normed = (normal * gains[0:1]).astype(jnp.bfloat16)
    normed_out[...] = normed
    hidden = contract(normed, up[...], 1, 0)
    active, slope = gelu_pair(hidden)
    active_out[...] = active.astype(jnp.bfloat16)
    hidden_grad[...] = (slope * contract(ffn_grad, down[...], 1, 1)).astype(jnp.bfloat16)
    normed_grad = summed_grad + contract(hidden_grad[...], up[...], 1, 1)
    gain_sums[0:8] += column_sum(normed_grad * normal)
    total = unit_back(normal, root, normed_grad * gains[0:1])
    mixed_grad[...] = total
    attended[...] = total.astype(jnp.bfloat16)
    context_grad[...] = contract(attended[...], out[...], 1, 1).astype(jnp.bfloat16)


def blend_both(
    feature, pooled, out_grad, gains, blend,
    result, feature_grad, state_grad, grads, gain_sum, early, middle, late, spread, total
):
    length = feature.shape[0]
    pair = 2 * D
    rows = 128
    chunks = [slice(at, at + rows) for at in range(0, length, rows)]

    def ahead(number):
        return contract(feature[...], blend[number * pair : number * pair + D, :], 1, 0) + contract(
            pooled[...], blend[number * pair + D : number * pair + pair, :], 1, 0
        )

    edge = jnp.zeros((8, D), jnp.float32)
    early[0:8] = edge
    late[length : length + 8] = edge
    spread[0:8] = edge
    spread[length + 8 : length + 16] = edge
    early[8 : length + 8] = ahead(0)
    middle[...] = ahead(1)
    late[0:length] = ahead(2)
    gain_sum[...] = jnp.zeros_like(gain_sum)
    for chunk in chunks:
        before = slice(chunk.start + 7, chunk.stop + 7)
        after = slice(chunk.start + 1, chunk.stop + 1)
        blended, slope = gelu_pair(middle[chunk] + early[before] + late[after])
        normal, root = unit(feature[chunk].astype(jnp.float32) + blended)
        result[chunk] = (normal * gains[2:3]).astype(result.dtype)
        given = out_grad[chunk].astype(jnp.float32)
        gain_sum[...] += column_sum(given * normal)
        whole_grad = unit_back(normal, root, given * gains[2:3])
        total[chunk] = whole_grad
        spread[slice(chunk.start + 8, chunk.stop + 8)] = whole_grad * slope
    for chunk in chunks:
        for number, offset in ((0, 9), (1, 8), (2, 7)):
            grads[chunk, number * D : number * D + D] = spread[
                slice(chunk.start + offset, chunk.stop + offset)
            ].astype(jnp.bfloat16)

    def back(left):
        return sum(
            contract(
                grads[:, number * D : number * D + D],
                blend[number * pair + left : number * pair + left + D, :],
                1,
                1,
            )
            for number in range(3)
        )

    feature_grad[...] = (total[...] + back(0)).astype(feature_grad.dtype)
    state_grad[...] = back(D)


def params(size):
    return pltpu.CompilerParams(vmem_limit_bytes=size << 20)


def rows_block(width):
    return pl.BlockSpec((CHUNK, width), lambda step: (step, 0))


def fixed(*shape):
    return pl.BlockSpec(shape, lambda step: (0,) * len(shape))


def run_feed(mixed, gains, up, down):
    length = mixed.shape[0]
    wide = up.shape[1]
    return pl.pallas_call(
        feed_ahead,
        grid=(length // CHUNK,),
        in_specs=[rows_block(D), fixed(3, D), fixed(D, wide), fixed(wide, D)],
        out_specs=[rows_block(D), rows_block(D)],
        out_shape=[
            jax.ShapeDtypeStruct((length, D), jnp.float32),
            jax.ShapeDtypeStruct((length, D), jnp.bfloat16),
        ],
        compiler_params=params(56),
        cost_estimate=spent(18),
    )(mixed, gains, up, down)


def run_feed_back(mixed, summed, feature_grad, gains, up, down, out):
    length = mixed.shape[0]
    wide = up.shape[1]
    bf = jnp.bfloat16
    f32 = jnp.float32
    widths = [(wide, bf), (wide, bf), (D, bf), (D, bf), (D, f32), (D, bf), (D, bf)]
    return pl.pallas_call(
        feed_back,
        grid=(length // CHUNK,),
        in_specs=[rows_block(D)] * 3 + [fixed(3, D), fixed(D, wide), fixed(wide, D), fixed(D, D)],
        out_specs=[rows_block(width) for width, _ in widths] + [fixed(16, D)],
        out_shape=[jax.ShapeDtypeStruct((length, width), kind) for width, kind in widths]
        + [jax.ShapeDtypeStruct((16, D), f32)],
        compiler_params=params(60),
        cost_estimate=spent(32),
    )(mixed, summed, feature_grad, gains, up, down, out)


def run_blend(feature, pooled, out_grad, gains, blend):
    length = feature.shape[0]
    bf = jnp.bfloat16
    f32 = jnp.float32
    return pl.pallas_call(
        blend_both,
        out_shape=[
            jax.ShapeDtypeStruct((length, D), bf),
            jax.ShapeDtypeStruct((length, D), bf),
            jax.ShapeDtypeStruct((length, D), f32),
            jax.ShapeDtypeStruct((length, 3 * D), bf),
            jax.ShapeDtypeStruct((8, D), f32),
        ],
        scratch_shapes=[
            pltpu.VMEM((length + 8, D), f32),
            pltpu.VMEM((length, D), f32),
            pltpu.VMEM((length + 8, D), f32),
            pltpu.VMEM((length + 16, D), f32),
            pltpu.VMEM((length, D), f32),
        ],
        compiler_params=params(60),
        cost_estimate=spent(26),
    )(feature, pooled, out_grad, gains, blend)


def blend_weight_grad(feature, pooled, grads, out):
    out[0:D, :] = contract(feature[...], grads[...], 0, 0).astype(out.dtype)
    out[D : 2 * D, :] = contract(pooled[...], grads[...], 0, 0).astype(out.dtype)


def run_blend_grad(feature, pooled, grads):
    length = feature.shape[0]
    return pl.pallas_call(
        blend_weight_grad,
        grid=(3,),
        in_specs=[
            fixed(length, D),
            fixed(length, D),
            pl.BlockSpec((length, D), lambda third: (0, third)),
        ],
        out_specs=pl.BlockSpec((2 * D, D), lambda third: (third, 0)),
        out_shape=jax.ShapeDtypeStruct((6 * D, D), jnp.bfloat16),
        compiler_params=params(48),
        cost_estimate=spent(12),
    )(feature, pooled, grads)


def on_device(
    tokens_in,
    char_ids,
    char_lengths,
    out_grad,
    w_qkv,
    first_qkv,
    second_qkv,
    w_out,
    first_out,
    second_out,
    w_up,
    first_up,
    second_up,
    w_down,
    first_down,
    second_down,
    w_gru,
    first_gru,
    second_gru,
    w_blend,
    first_blend,
    second_blend,
    char_table,
    first_table,
    second_table,
    gains,
    first_gains,
    second_gains,
):
    masters = (w_qkv, w_out, w_up, w_down, w_gru, w_blend, char_table, gains)
    firsts = (
        first_qkv,
        first_out,
        first_up,
        first_down,
        first_gru,
        first_blend,
        first_table,
        first_gains,
    )
    seconds = (
        second_qkv,
        second_out,
        second_up,
        second_down,
        second_gru,
        second_blend,
        second_table,
        second_gains,
    )
    parts = lax.axis_size("stream") * lax.axis_size("dp")
    on_first = lax.axis_index("stream") == 0
    half_len = tokens_in.shape[1]
    flow = Flow()

    def both_halves(pair, got):
        kept = jnp.where(on_first, pair[0], pair[1])
        return jnp.where(
            on_first, jnp.concatenate([kept, got], 0), jnp.concatenate([got, kept], 0)
        )

    ids_row = jnp.where(on_first, char_ids[0], char_ids[1])
    lengths_row = jnp.where(on_first, char_lengths[0], char_lengths[1])

    queries = HEADS // 2
    groups = 3
    pairs = queries // groups
    wide = 128 * pairs
    everyone = ("stream", "dp")
    by_group = w_qkv.reshape(w_qkv.shape[0], 3, groups, -1).transpose(0, 2, 1, 3)
    by_group = by_group.reshape(w_qkv.shape[0], groups, -1)
    flow.begin("tokens", swap_chain(jnp.where(on_first, tokens_in[1], tokens_in[0])), [4])
    flow.begin("group0", gather_steps([by_group[:, 0]], False))
    flow.begin("group1", gather_steps([by_group[:, 1]], True))
    flow.slot(())
    flow.slot(())
    flow.begin("group2", gather_steps([by_group[:, 2], w_out], True))
    flow.begin("up", gather_steps([w_up], True), [0, 1, 0, 1, 0])
    flow.slot(())
    shards = flow.slot((char_table, w_gru, gains_row(gains), w_blend))
    shapes = shapes_of(shards[:3], 1)
    packed = jnp.concatenate([to_rows(shard, 1)[0] for shard in shards[:3]], 0)
    rest = lax.all_gather(packed, everyone, axis=0, tiled=False)
    blend_all = lax.all_gather(
        shards[3].astype(jnp.bfloat16), everyone, axis=0, tiled=True
    )
    flow.begin("down", gather_steps([w_down], True), [0, 0, 1, 0, 0])
    flow.slot(())
    tokens = both_halves(tokens_in, flow.end("tokens"))
    weights, parts_qkv, contexts, logsums = [], [], [], []
    for number in range(groups):
        w_group, *w_more = flow.end("group%d" % number)
        if number == 2:
            segment = char_segments(lengths_row, ids_row.shape[0])
            shares = 1.0 / lengths_row.astype(jnp.float32)[:, None]
            ends = jnp.cumsum(lengths_row)
            lengths_row = (segment, shares, ends)
        qkv = product(tokens, w_group).astype(jnp.bfloat16)
        context, logsum = run_attend(qkv, 0, pairs)
        qkv, context, logsum, tokens, lengths_row = flow.slot(
            (qkv, context, logsum, tokens, lengths_row)
        )
        weights.append(w_group)
        parts_qkv.append(qkv)
        contexts.append(context)
        logsums.append(logsum)
    (out_all,) = w_more
    segment, shares, ends = lengths_row
    context = jnp.concatenate(contexts, 1)
    table_all, gru_all, gain_all = unpack_rows(rest, shapes)
    gain_all = gain_all.reshape(parts, -1, D)[:, 0, : gains.size]
    gain_all = gain_all.reshape(parts, 3, -1).transpose(1, 0, 2).reshape(3, -1).astype(jnp.float32)
    letters, before, pooled = run_chars(ids_row, ends, table_all, gru_all, shares)
    letters, before, pooled, context, tokens = flow.slot((letters, before, pooled, context, tokens))
    mixed_sum = tokens.astype(jnp.float32) + product(context, out_all)
    mixed_sum, gain_all = flow.slot((mixed_sum, gain_all))
    flow.begin("out_grad", swap_chain(jnp.where(on_first, out_grad[1], out_grad[0])))
    (up_all,) = flow.end("up")
    (down_all,) = flow.end("down")
    summed, feature = run_feed(mixed_sum, gain_all, up_all, down_all)
    summed, feature, blend_all = flow.slot((summed, feature, blend_all))
    whole_grad = both_halves(out_grad, flow.end("out_grad"))
    result, feature_grad, state_grad, blend_grads, gain_blend = run_blend(
        feature, pooled, whole_grad, gain_all, blend_all
    )
    grad_blend = run_blend_grad(feature, pooled, blend_grads)
    result, grad_blend, feature_grad = flow.slot((result, grad_blend, feature_grad))
    (blend_sum,) = scatter_whole([grad_blend])
    flow.begin("result", swap_chain(jnp.where(on_first, result[half_len:], result[:half_len])))
    active, hidden_grad, ffn_grad, normed, mixed_grad, attended_grad, context_grad, gain_sums = (
        run_feed_back(mixed_sum, summed, feature_grad, gain_all, up_all, down_all, out_all)
    )
    gain_grads = jnp.stack(
        [jnp.sum(gain_sums[:8], 0), jnp.sum(gain_sums[8:], 0), jnp.sum(gain_blend, 0)]
    )
    gain_rows = gain_grads.reshape(3, parts, -1).transpose(1, 0, 2).reshape(parts, -1)
    gain_rows = jnp.pad(gain_rows[:, None], ((0, 0), (0, 7), (0, D - gain_rows.shape[1])))
    gain_rows = gain_rows.reshape(8 * parts, D)
    grad_down = inner_rows(active, ffn_grad).astype(jnp.bfloat16)
    grad_up = inner_rows(normed, hidden_grad).astype(jnp.bfloat16)
    grad_out = inner_rows(context, attended_grad).astype(jnp.bfloat16)
    grad_down, grad_up, grad_out, state_grad, context_grad, gain_rows = flow.slot(
        (grad_down, grad_up, grad_out, state_grad, context_grad, gain_rows)
    )
    flow.begin("feed", scatter_chain([grad_down, grad_up]))
    tokens_grad = mixed_grad
    group_grads = []
    for number in range(groups):
        left = wide * number
        qkv_grad = jnp.concatenate(
            run_attend_back(
                parts_qkv[number], logsums[number], context_grad[:, left : left + wide], 0, pairs
            ),
            1,
        )
        tokens_grad = tokens_grad + inner_cols(qkv_grad, weights[number])
        grad_group = inner_rows(tokens, qkv_grad).astype(jnp.bfloat16)
        if number == groups - 1:
            tokens_grad = tokens_grad.astype(jnp.bfloat16)
        if number != 1:
            done = (context_grad, grad_group, tokens_grad, state_grad)
            done, blend_sum = flow.slot((done, blend_sum)) if number else (flow.slot(done), blend_sum)
            context_grad, grad_group, tokens_grad, state_grad = done
        group_grads.append(grad_group)
    flow.begin(
        "tokens", swap_chain(jnp.where(on_first, tokens_grad[half_len:], tokens_grad[:half_len]))
    )
    flow.begin("qkv", scatter_chain(group_grads + [grad_out, gain_rows]), [0, 0, 1])
    blocks = ids_row.shape[0] // STEP_ROWS
    spread, *held = run_chars_back(
        blocks, blocks // 2, ids_row, segment, letters, before, upstream=[state_grad, shares]
    )
    spread, held = flow.slot((spread, held))
    grad_gru, grad_table = run_chars_back(
        blocks // 2,
        blocks // 2,
        ids_row,
        segment,
        letters,
        before,
        held=[spread, *held],
        ends=[table_all, gru_all],
    )
    grad_gru, grad_table = flow.slot((grad_gru, grad_table))
    flow.begin("letters", scatter_chain([grad_gru, grad_table]))
    while flow.live:
        flow.slot(())
    own_result = jnp.where(on_first, result[:half_len], result[half_len:])
    own_grad = jnp.where(on_first, tokens_grad[:half_len], tokens_grad[half_len:])
    back_result, back_grad = flow.end("result"), flow.end("tokens")
    block_parts = [
        jnp.where(on_first, own_result, back_result),
        jnp.where(on_first, back_result, own_result),
    ]
    grad_parts = [
        jnp.where(on_first, own_grad, back_grad),
        jnp.where(on_first, back_grad, own_grad),
    ]
    *group_sums, out_sum, gain_sum = flow.end("qkv")
    group_sums = jnp.stack(group_sums, 1)
    qkv_sum = group_sums.reshape(w_qkv.shape[0], groups, 3, -1).transpose(0, 2, 1, 3)
    letter_sums = flow.end("letters")
    feed_sums = flow.end("feed")
    sums = (
        qkv_sum.reshape(w_qkv.shape),
        out_sum,
        feed_sums[1],
        feed_sums[0],
        letter_sums[0],
        blend_sum,
        letter_sums[1],
        gain_sum[0, : gains.size].reshape(gains.shape),
    )
    rates = step_rates()
    results = [
        adamw(masters[number], firsts[number], seconds[number], sums[number], rates[number])
        for number in range(8)
    ]
    return (
        jnp.stack(block_parts),
        jnp.stack(grad_parts),
        results[0][0],
        results[0][1],
        results[0][2],
        results[1][0],
        results[1][1],
        results[1][2],
        results[2][0],
        results[2][1],
        results[2][2],
        results[3][0],
        results[3][1],
        results[3][2],
        results[4][0],
        results[4][1],
        results[4][2],
        results[5][0],
        results[5][1],
        results[5][2],
        results[6][0],
        results[6][1],
        results[6][2],
        results[7][0],
        results[7][1],
        results[7][2],
    )


def solution(mesh):
    in_specs = (
        P("dp", "stream", None),
        P("dp", None),
        P("dp", None),
        P("dp", "stream", None),
        P(("stream", "dp"), None),
        P(("stream", "dp"), None),
        P(("stream", "dp"), None),
        P(("stream", "dp"), None),
        P(("stream", "dp"), None),
        P(("stream", "dp"), None),
        P(("stream", "dp"), None),
        P(("stream", "dp"), None),
        P(("stream", "dp"), None),
        P(("stream", "dp"), None),
        P(("stream", "dp"), None),
        P(("stream", "dp"), None),
        P(("stream", "dp"), None),
        P(("stream", "dp"), None),
        P(("stream", "dp"), None),
        P(("stream", "dp"), None),
        P(("stream", "dp"), None),
        P(("stream", "dp"), None),
        P(("stream", "dp"), None),
        P(("stream", "dp"), None),
        P(("stream", "dp"), None),
        P(None, ("stream", "dp")),
        P(None, ("stream", "dp")),
        P(None, ("stream", "dp")),
    )
    out_specs = (
        P("dp", "stream", None),
        P("dp", "stream", None),
        P(("stream", "dp"), None),
        P(("stream", "dp"), None),
        P(("stream", "dp"), None),
        P(("stream", "dp"), None),
        P(("stream", "dp"), None),
        P(("stream", "dp"), None),
        P(("stream", "dp"), None),
        P(("stream", "dp"), None),
        P(("stream", "dp"), None),
        P(("stream", "dp"), None),
        P(("stream", "dp"), None),
        P(("stream", "dp"), None),
        P(("stream", "dp"), None),
        P(("stream", "dp"), None),
        P(("stream", "dp"), None),
        P(("stream", "dp"), None),
        P(("stream", "dp"), None),
        P(("stream", "dp"), None),
        P(("stream", "dp"), None),
        P(("stream", "dp"), None),
        P(("stream", "dp"), None),
        P(None, ("stream", "dp")),
        P(None, ("stream", "dp")),
        P(None, ("stream", "dp")),
    )
    return jax.shard_map(
        on_device, mesh=mesh, in_specs=in_specs, out_specs=out_specs, check_vma=False
    )
```

```python
import functools

import jax
import jax.numpy as jnp
from jax import lax
from jax.experimental import pallas as pl
from jax.experimental.pallas import tpu as pltpu
from jax.sharding import PartitionSpec as P

D = 768
HEADS = 12
FF = 3072
LEN = 1024
STEP = 5


def to_rows(matrix, parts):
    side = matrix.shape[1] // D
    own = matrix.shape[0] // parts
    blocks = matrix.astype(jnp.bfloat16).reshape(parts, own, side, D)
    return blocks.transpose(0, 2, 1, 3).reshape(parts, side * own, D)


def from_rows(rows, offset, own, side):
    parts = rows.shape[0]
    blocks = rows[:, offset : offset + own * side].reshape(parts, side, own, D)
    return blocks.transpose(0, 2, 1, 3).reshape(parts * own, side * D)


def gains_rows(gains):
    blank = jnp.zeros((8, D), jnp.float32)
    return lax.dynamic_update_slice(blank, gains, (0, my_place()[0] * gains.shape[1]))


def swap(block, mask):
    parts = lax.axis_size("dp") * lax.axis_size("stream")
    return lax.ppermute(block, ("stream", "dp"), [(place, place ^ mask) for place in range(parts)])


def pair_bits():
    return (lax.axis_size("dp") * lax.axis_size("stream")).bit_length() - 2


def in_pairs(shapes):
    parts = lax.axis_size("dp") * lax.axis_size("stream")
    return parts == 32 and all(rows % 8 == 0 for rows, _ in shapes)


def my_place():
    return (lax.axis_index("stream") * lax.axis_size("dp") + lax.axis_index("dp")).reshape(1)


def shapes_of(matrices, parts):
    return [(matrix.shape[0] // parts, matrix.shape[1] // D) for matrix in matrices]


def assemble(shapes, place, mine, theirs, *weights):
    core = place[0] & 1
    low = (place[0] >> 1) & 3
    pieces = []
    for pair in range(4):
        own = mine[pair ^ low].astype(jnp.float32)
        other = theirs[pair ^ low].astype(jnp.float32)
        pieces.append(jnp.where(core == 0, own, other))
        pieces.append(jnp.where(core == 0, other, own))
    offset = 0
    for (rows, side), weight in zip(shapes, weights):
        for number in range(side):
            block = jnp.concatenate([piece[offset : offset + rows] for piece in pieces], 0)
            weight[:, number * D : number * D + D] = block.astype(weight.dtype)
            offset += rows


def apart(shapes, place, *refs):
    grads, keep, send = refs[: len(shapes)], refs[-2], refs[-1]
    core = place[0] & 1
    low = (place[0] >> 1) & 3
    for pair in range(4):
        halves = []
        for side in range(2):
            pieces = []
            for (rows, across), grad in zip(shapes, grads):
                first = (2 * pair + side) * rows
                for number in range(across):
                    pieces.append(
                        grad[first : first + rows, number * D : number * D + D].astype(jnp.float32)
                    )
            halves.append(jnp.concatenate(pieces, 0))
        keep[pair ^ low] = jnp.where(core == 0, halves[0], halves[1]).astype(keep.dtype)
        send[pair ^ low] = jnp.where(core == 0, halves[1], halves[0]).astype(send.dtype)


def turned_block(high):
    return pl.BlockSpec((4, high, D), lambda group, place: (group ^ (place[0] >> 3), 0, 0))


def natural_block(shape):
    return pl.BlockSpec((8 * shape[0], shape[1] * D), lambda group, place: (group, 0))


class Flow:
    def __init__(self):
        self.live = {}
        self.ended = {}

    def begin(self, name, chain, skips=()):
        self.step(name, chain, None, list(skips))

    def step(self, name, chain, arrays, skips):
        try:
            waiting = chain.send(arrays)
            self.live[name] = [chain, waiting, skips, skips.pop(0) if skips else 0]
        except StopIteration as stop:
            self.ended[name] = stop.value

    def slot(self, values):
        due = [name for name, entry in self.live.items() if entry[3] == 0]
        for entry in self.live.values():
            entry[3] -= 1
        values, waited = lax.optimization_barrier(
            (values, [self.live[name][1] for name in due])
        )
        for name, arrays in zip(due, waited):
            chain, _, skips, _ = self.live.pop(name)
            self.step(name, chain, arrays, skips)
        return values

    def end(self, name):
        return self.ended.pop(name)


def gather_chain(shards, near_first=False):
    shapes = shapes_of(shards, 1)
    packed = jnp.concatenate([to_rows(shard, 1)[0] for shard in shards], 0)
    if not in_pairs(shapes):
        return gather_whole(packed, shapes)
    top = pair_bits()
    far = 1 << (top - 2)
    high = packed.shape[0]
    corner = 1 << top
    near = (2, corner, corner | 2)
    held = packed[None, None, None]
    for turn in range(2):
        if near_first == (turn == 0):
            held, *got = yield (held, *[swap(held, mask) for mask in near])
            held = jnp.concatenate(
                [jnp.concatenate([held, got[0]], 2), jnp.concatenate(got[1:], 2)], 0
            )
        else:
            held, *got = yield (held, *[swap(held, step << 2) for step in range(1, far)])
            held = jnp.concatenate([held, *got], 1)
    held = held.reshape(4 * far, high, D)
    held, other = yield (held, swap(held, 1))
    return join_halves(shapes, held, other)


def gather_steps(shards, turned):
    shapes = shapes_of(shards, 1)
    packed = jnp.concatenate([to_rows(shard, 1)[0] for shard in shards], 0)
    if not in_pairs(shapes):
        return gather_whole(packed, shapes)
    top = pair_bits()
    held = packed.reshape((1,) * top + packed.shape)
    for bit in list(range(2, top)) + ([1, top] if turned else [top, 1]):
        held, other = yield (held, swap(held, 1 << bit))
        held = jnp.concatenate([held, other], top - bit)
    held = held.reshape(1 << top, *packed.shape)
    held, other = yield (held, swap(held, 1))
    return join_halves(shapes, held, other)


def unpack(shapes, rows, *weights):
    pieces = [rows[number].astype(jnp.float32) for number in range(8)]
    offset = 0
    for (own, side), weight in zip(shapes, weights):
        for number in range(side):
            block = jnp.concatenate([piece[offset : offset + own] for piece in pieces], 0)
            weight[:, number * D : number * D + D] = block.astype(weight.dtype)
            offset += own


def unpack_rows(rows, shapes):
    parts, high = rows.shape[:2]
    if not in_pairs(shapes):
        return unpack_plain(rows, shapes)
    return pl.pallas_call(
        functools.partial(unpack, shapes),
        grid=(parts // 8,),
        in_specs=[pl.BlockSpec((8, high, D), lambda group: (group, 0, 0))],
        out_specs=[
            pl.BlockSpec((8 * own, side * D), lambda group: (group, 0)) for own, side in shapes
        ],
        out_shape=[
            jax.ShapeDtypeStruct((parts * own, side * D), jnp.bfloat16) for own, side in shapes
        ],
        compiler_params=pltpu.CompilerParams(vmem_limit_bytes=16 << 20),
        cost_estimate=spent(3),
    )(rows)


def unpack_plain(rows, shapes):
    pieces = []
    offset = 0
    for own, side in shapes:
        pieces.append(from_rows(rows, offset, own, side))
        offset += own * side
    return pieces


def gather_whole(packed, shapes):
    return unpack_rows(lax.all_gather(packed, ("stream", "dp"), axis=0, tiled=False), shapes)


def join_halves(shapes, mine, theirs):
    high = mine.shape[-2]
    pairs = 1 << pair_bits()
    parts = 2 * pairs
    return pl.pallas_call(
        functools.partial(assemble, shapes),
        grid_spec=pltpu.PrefetchScalarGridSpec(
            num_scalar_prefetch=1,
            grid=(pairs // 4,),
            in_specs=[turned_block(high)] * 2,
            out_specs=[natural_block(shape) for shape in shapes],
        ),
        out_shape=[
            jax.ShapeDtypeStruct((parts * rows, side * D), jnp.bfloat16) for rows, side in shapes
        ],
        compiler_params=pltpu.CompilerParams(vmem_limit_bytes=16 << 20),
        cost_estimate=spent(4),
    )(my_place(), mine.reshape(pairs, high, D), theirs.reshape(pairs, high, D))


def scatter_whole(grads):
    parts = lax.axis_size("dp") * lax.axis_size("stream")
    packed = jnp.concatenate([to_rows(grad, parts) for grad in grads], 1)
    total = lax.psum_scatter(
        packed.reshape(-1, D), ("stream", "dp"), scatter_dimension=0, tiled=True
    ).astype(jnp.float32)
    return own_pieces(total, shapes_of(grads, parts))


def own_pieces(total, shapes):
    pieces = []
    offset = 0
    for own, side in shapes:
        pieces.append(from_rows(total[None], offset, own, side))
        offset += own * side
    return pieces


def feed_grads(place, former, latter, given, source, keep, send, held):
    step = pl.program_id(0)
    core = place[0] & 1
    low = place[0] >> 1

    @pl.when(step < 4)
    def down():
        whole_grad = contract(former[...], given[...], 0, 0)
        rows = whole_grad.shape[0] // 8
        for pair in range(4):
            there = (4 * step + pair) ^ low
            first = whole_grad[2 * pair * rows : (2 * pair + 1) * rows]
            second = whole_grad[(2 * pair + 1) * rows : (2 * pair + 2) * rows]
            keep[there, 0:rows] = jnp.where(core == 0, first, second).astype(keep.dtype)
            send[there, 0:rows] = jnp.where(core == 0, second, first).astype(send.dtype)

    rows = D // held.shape[0]
    for number in range(4):

        @pl.when(step == 4 + number)
        def up():
            whole_grad = contract(source[...], latter[...], 0, 0)
            held[:, number * rows : number * rows + rows] = whole_grad.reshape(-1, rows, D)

    @pl.when(step == 7)
    def finish():
        start = 4 * rows
        for pair in range(held.shape[0] // 2):
            first, second = held[2 * pair], held[2 * pair + 1]
            there = pair ^ low
            keep[there, start:] = jnp.where(core == 0, first, second).astype(keep.dtype)
            send[there, start:] = jnp.where(core == 0, second, first).astype(send.dtype)


def run_feed_grads(active, ffn_grad, normed, hidden_grad):
    length, wide = active.shape
    parts = lax.axis_size("dp") * lax.axis_size("stream")
    pairs = parts // 2
    high = 2 * wide // parts
    half = jax.ShapeDtypeStruct((pairs, high, D), jnp.bfloat16)
    whole_half = pl.BlockSpec(half.shape, lambda step, place: (0, 0, 0))
    kept_rows = pl.BlockSpec((length, D), lambda step, place: (0, 0))
    return pl.pallas_call(
        feed_grads,
        grid_spec=pltpu.PrefetchScalarGridSpec(
            num_scalar_prefetch=1,
            grid=(8,),
            in_specs=[
                pl.BlockSpec((length, D), lambda step, place: (0, jnp.minimum(step, 3))),
                pl.BlockSpec((length, D), lambda step, place: (0, jnp.maximum(step - 4, 0))),
                kept_rows,
                kept_rows,
            ],
            out_specs=[whole_half, whole_half],
            scratch_shapes=[pltpu.VMEM((parts, high // 2, D), jnp.float32)],
        ),
        out_shape=[half, half],
        compiler_params=params(56),
        cost_estimate=spent(16),
    )(my_place(), active, hidden_grad, ffn_grad, normed)


def scatter_chain(grads):
    parts = lax.axis_size("dp") * lax.axis_size("stream")
    shapes = shapes_of(grads, parts)
    if not in_pairs(shapes):
        return scatter_whole(grads)
    total = yield from halves_chain(*core_halves(grads, shapes, parts))
    return own_pieces(total, shapes)


def core_halves(grads, shapes, parts):
    pairs = parts // 2
    high = sum(rows * side for rows, side in shapes)
    half = jax.ShapeDtypeStruct((pairs, high, D), jnp.bfloat16)
    return pl.pallas_call(
        functools.partial(apart, shapes),
        grid_spec=pltpu.PrefetchScalarGridSpec(
            num_scalar_prefetch=1,
            grid=(pairs // 4,),
            in_specs=[natural_block(shape) for shape in shapes],
            out_specs=[turned_block(high)] * 2,
        ),
        out_shape=[half, half],
        compiler_params=pltpu.CompilerParams(vmem_limit_bytes=16 << 20),
        cost_estimate=spent(4),
    )(my_place(), *[grad.astype(jnp.bfloat16) for grad in grads])


def halves_chain(kept, sent, split=False):
    high = kept.shape[1]
    kept, other = yield (kept, swap(sent, 1))
    top = pair_bits()
    far = 1 << (top - 2)
    corner = 1 << top
    near = [(1, 0), (0, 1), (1, 1)]
    quarter = jax.ShapeDtypeStruct((far, high, D), jnp.bfloat16)
    views = [
        pl.BlockSpec((1, 1, 1, high, D), lambda row, x=x, y=y: (x, row, y, 0, 0))
        for x, y in [(0, 0)] + near
    ]
    total, *sent = pl.pallas_call(
        sum_quarters,
        grid=(far,),
        in_specs=views + views,
        out_specs=[pl.BlockSpec((1, high, D), lambda row: (row, 0, 0))] * 4,
        out_shape=[jax.ShapeDtypeStruct(quarter.shape, jnp.float32)] + [quarter] * 3,
        compiler_params=pltpu.CompilerParams(vmem_limit_bytes=16 << 20),
        cost_estimate=spent(3),
    )(*[kept.reshape(2, far, 2, high, D)] * 4, *[other.reshape(2, far, 2, high, D)] * 4)
    got = [swap(sent[0], corner), swap(sent[1], 2)]
    if split:
        total, last, *got = yield (total, sent[2], *got)
        total, got, last = yield (total, got, swap(last, corner | 2))
    else:
        total, last, *got = yield (total, swap(sent[2], corner | 2), *got)
    total = total + sum(block.astype(jnp.float32) for block in [last, *got])
    while split and far > 1:
        far //= 2
        kept, other = yield (total[:far], swap(total[far:].astype(jnp.bfloat16), far << 2))
        total = kept + other.astype(jnp.float32)
    if split:
        return total[0]
    others = [
        swap(total[number].astype(jnp.bfloat16), number << 2) for number in range(1, far)
    ]
    kept, *others = yield (total[0], *others)
    return kept + sum(other.astype(jnp.float32) for other in others)


def sum_quarters(*refs):
    for former, latter, out in zip(refs[:4], refs[4:8], refs[8:]):
        total = former[0, 0, 0].astype(jnp.float32) + latter[0, 0, 0].astype(jnp.float32)
        out[0] = total.astype(out.dtype)


def feed_chain(halves, shapes):
    if not in_pairs(shapes):
        return scatter_whole(halves)
    total = yield from halves_chain(*halves, True)
    return own_pieces(total, shapes)


def swap_chain(block):
    other = yield swap(block, lax.axis_size("dp"))
    return other


def product(former, latter):
    return jnp.dot(former, latter, preferred_element_type=jnp.float32)


def inner_rows(former, latter):
    return lax.dot_general(
        former, latter, (((0,), (0,)), ((), ())), preferred_element_type=jnp.float32
    )


def inner_cols(former, latter):
    return lax.dot_general(
        former, latter, (((1,), (1,)), ((), ())), preferred_element_type=jnp.float32
    )


def norm_gain(values, scales):
    center = jnp.mean(values, axis=-1, keepdims=True)
    shifted = values - center
    spread = jnp.mean(shifted * shifted, axis=-1, keepdims=True)
    return shifted * lax.rsqrt(spread + 1e-05) * scales


def rows_before(matrix):
    return jnp.concatenate([jnp.zeros_like(matrix[:1]), matrix[:-1]], 0)


def rows_after(matrix):
    return jnp.concatenate([matrix[1:], jnp.zeros_like(matrix[:1])], 0)


def char_segments(ends, char_count):
    places = lax.broadcasted_iota(jnp.int32, (ends.shape[0], char_count), 1)
    return jnp.sum((ends[:, None] <= places).astype(jnp.int32), axis=0)


def step_rates():
    return (
        0.5 * D ** (-0.5),
        0.5 * (3 * D // LEN) ** (-0.5),
        0.5 * D ** (-0.5),
        0.5 * FF ** (-0.5),
        0.5 * D ** (-0.5),
        0.5 * (6 * D) ** (-0.5),
        0.5,
        0.2,
    )


def adamw(master, first_m, second_m, grad_sum, step_rate):
    mean_new = 0.5 * first_m + 0.5 * grad_sum
    power = 0.5 * second_m + 0.5 * grad_sum * grad_sum
    correct = 1.0 - 0.5**STEP
    fresh_w = master - step_rate * (
        mean_new / correct / (jnp.sqrt(power / correct) + 1e-08) + 0.01 * master
    )
    return (fresh_w, mean_new, power)


STEP_ROWS = 512


def spent(microseconds):
    return pl.CostEstimate(
        flops=int(microseconds * 1e9), bytes_accessed=1, transcendentals=0
    )


UNROLL = 16


def contract(former, latter, left, right):
    return lax.dot_general(
        former, latter, (((left,), (right,)), ((), ())), preferred_element_type=jnp.float32
    )


def lane_blocks(width):
    blocks = []
    for number in range(2 * width // 128):
        side, lane = divmod(number * 128, width)
        blocks.append((number * 128, 2 * side * width + lane, 4 * side + lane // 128))
    return blocks


def eight(offset):
    return pl.ds(pl.multiple_of(offset, 8), 8)


def chars_ahead(rows_f, rows_b, ends, table, w_gru, shares, letters, before, pooled, running, spans, carry):
    block = pl.program_id(0)
    total = rows_f.shape[0]
    width = w_gru.shape[1] // 4

    @pl.when(block == 0)
    def start():
        logits = jnp.dot(table[...], w_gru[...], preferred_element_type=jnp.float32)
        letters[...] = jnp.zeros_like(letters)
        carry[...] = jnp.zeros_like(carry)
        for _, left, place in lane_blocks(width):
            update = jax.nn.sigmoid(logits[:, left : left + 128])
            letters[:, place, :] = 1.0 - update
            letters[:, 8 + place, :] = update * logits[:, left + width : left + width + 128]

    leading = lax.broadcasted_iota(jnp.int32, (8, 128), 0) < 4

    def several(group, held):
        state, total_state = held
        first = block * STEP_ROWS + group * UNROLL
        factors, adds = [], []
        for inner in range(UNROLL):
            id_f, id_b = rows_f[first + inner], rows_b[first + inner]
            factors.append(jnp.where(leading, letters[id_f, 0:8], letters[id_b, 0:8]))
            adds.append(jnp.where(leading, letters[id_f, 8:16], letters[id_b, 8:16]))
        for inner in range(UNROLL):
            before[group * UNROLL + inner] = state
            running[first + inner] = total_state
            state = factors[inner] * state + adds[inner]
            total_state = total_state + state
        return state, total_state

    state, total_state = lax.fori_loop(0, STEP_ROWS // UNROLL, several, (carry[0], carry[1]))
    carry[0] = state
    carry[1] = total_state

    @pl.when(block == pl.num_programs(0) - 1)
    def finish():
        running[total] = total_state

        def tokens(group, prior):
            found = []
            for inner in range(UNROLL):
                end = ends[group * UNROLL + inner]
                found.append(jnp.where(leading, running[end], -running[total - end]))
            for inner in range(UNROLL):
                spans[group * UNROLL + inner] = found[inner] - prior
                prior = found[inner]
            return prior

        lax.fori_loop(0, ends.shape[0] // UNROLL, tokens, jnp.where(leading, running[0], -running[total]))
        for at, _, place in lane_blocks(width):
            pooled[:, at : at + 128] = (spans[:, place, :] * shares[...]).astype(pooled.dtype)


def chars_back(blocks, opening, closing, *refs):
    rows_f, rows_b, owners_f, owners_b, letters, before = refs[:6]
    rest = list(refs[6:])
    take = lambda count: [rest.pop(0) for _ in range(count)]
    if opening:
        upstream, shares = take(2)
    else:
        spread, carry_in, *sums_in = take(6)
    if closing:
        table, w_gru = take(2)
    if opening:
        (spread,) = take(1)
    if closing:
        grad_gru, grad_table = take(2)
    else:
        carry_out, *sums_out = take(5)
    *sums, carry = take(5)
    if closing:
        (full,) = take(1)
    sums_f, sums_b, more_f, more_b = sums
    step_number = pl.program_id(0)
    block = blocks[0] - 1 - step_number
    width = 384

    @pl.when(step_number == 0)
    def start():
        if opening:
            for held in sums:
                held[...] = jnp.zeros_like(held)
            carry[...] = jnp.zeros_like(carry)
            for at, _, place in lane_blocks(width):
                spread[:, place, :] = upstream[:, at : at + 128] * shares[...]
            for place in (3, 7):
                spread[:, place, :] = jnp.zeros((spread.shape[0], 128), jnp.float32)
        else:
            for held, given in zip(sums, sums_in):
                held[...] = given[...]
            carry[...] = carry_in[...]

    leading = lax.broadcasted_iota(jnp.int32, (8, 128), 0) < 4

    def several(group, passed):
        steps = [STEP_ROWS - 1 - group * UNROLL - inner for inner in range(UNROLL)]
        kept, given, priors, owned = [], [], [], []
        for step in steps:
            place = block * STEP_ROWS + step
            id_f, id_b = rows_f[place], rows_b[place]
            owned.append((id_f, id_b))
            kept.append(jnp.where(leading, letters[id_f, 0:8], letters[id_b, 0:8]))
            given.append(jnp.where(leading, spread[owners_f[place]], spread[owners_b[place]]))
            priors.append(before[step])
        for inner in range(UNROLL):
            carried = given[inner] + passed
            passed = kept[inner] * carried
            moved = carried * priors[inner]
            id_f, id_b = owned[inner]
            for held, row, value in (
                (
                    (sums_f, more_f)[inner % 2],
                    id_f,
                    jnp.where(leading, carried, pltpu.roll(moved, 4, 0)),
                ),
                (
                    (sums_b, more_b)[inner % 2],
                    id_b,
                    jnp.where(leading, pltpu.roll(carried, 4, 0), moved),
                ),
            ):
                held[row] += value
        return passed

    carry[...] = lax.fori_loop(0, STEP_ROWS // UNROLL, several, carry[...])

    @pl.when(step_number == pl.num_programs(0) - 1)
    def finish():
        if not closing:
            carry_out[...] = carry[...]
            for held, given in zip(sums, sums_out):
                given[...] = held[...]
            return
        sums_f[...] += more_f[...]
        sums_b[...] += more_b[...]
        for _, left, place in lane_blocks(width):
            found = sums_f if place < 4 else sums_b
            lane = place % 4
            kept = letters[:, place, :]
            update = 1.0 - kept
            total = found[:, lane, :]
            full[:, left : left + 128] = kept * (
                letters[:, 8 + place, :] * total - update * found[:, 4 + lane, :]
            )
            full[:, left + width : left + width + 128] = update * total
        found = full[...].astype(jnp.bfloat16)
        grad_gru[...] = contract(table[...], found, 0, 0).astype(grad_gru.dtype)
        grad_table[...] = contract(found, w_gru[...], 1, 1).astype(grad_table.dtype)


def whole(array):
    return pl.BlockSpec(array.shape, lambda block: (0,) * len(array.shape))


def scalars():
    return pl.BlockSpec(memory_space=pltpu.SMEM)


def run_chars(ids, ends, table, w_gru, shares):
    total, count = ids.shape[0], shares.shape[0]
    f32 = jnp.float32
    outs = (
        jax.ShapeDtypeStruct((table.shape[0], 16, 128), f32),
        jax.ShapeDtypeStruct((total, 8, 128), f32),
        jax.ShapeDtypeStruct((count, w_gru.shape[1] // 2), jnp.bfloat16),
    )
    return pl.pallas_call(
        chars_ahead,
        grid=(total // STEP_ROWS,),
        in_specs=[scalars(), scalars(), scalars(), whole(table), whole(w_gru), whole(shares)],
        out_specs=[
            whole(outs[0]),
            pl.BlockSpec((STEP_ROWS, 8, 128), lambda block: (block, 0, 0)),
            whole(outs[2]),
        ],
        out_shape=outs,
        scratch_shapes=[
            pltpu.VMEM((total + 1, 8, 128), f32),
            pltpu.VMEM((count, 8, 128), f32),
            pltpu.VMEM((2, 8, 128), f32),
        ],
        compiler_params=pltpu.CompilerParams(vmem_limit_bytes=44 << 20),
        cost_estimate=spent(24),
    )(ids, jnp.flip(ids), ends, table, w_gru, shares)


def run_chars_back(last, count, ids, owners, letters, before, *, upstream=None, held=None, ends=None):
    f32 = jnp.float32
    tile = jax.ShapeDtypeStruct((letters.shape[0], 8, 128), f32)
    flat = jax.ShapeDtypeStruct((8, 128), f32)
    inputs = [ids, jnp.flip(ids), owners, jnp.flip(owners), letters, before]
    blocks = [scalars()] * 4 + [
        whole(letters),
        pl.BlockSpec((STEP_ROWS, 8, 128), lambda block: (last - 1 - block, 0, 0)),
    ]
    outs = []
    if upstream is not None:
        inputs += upstream
        outs.append(jax.ShapeDtypeStruct((upstream[0].shape[0], 8, 128), f32))
    else:
        inputs += held
    if ends is not None:
        inputs += ends
        outs.append(jax.ShapeDtypeStruct(ends[1].shape, jnp.bfloat16))
        outs.append(jax.ShapeDtypeStruct(ends[0].shape, jnp.bfloat16))
    else:
        outs += [flat] + [tile] * 4
    blocks += [whole(array) for array in inputs[6:]]
    scratch = [pltpu.VMEM(tile.shape, f32)] * 4 + [pltpu.VMEM(flat.shape, f32)]
    if ends is not None:
        scratch.append(pltpu.VMEM((ends[0].shape[0], ends[1].shape[1]), f32))
    return pl.pallas_call(
        functools.partial(chars_back, (last,), upstream is not None, ends is not None),
        grid=(count,),
        in_specs=blocks,
        out_specs=[whole(out) for out in outs],
        out_shape=outs,
        scratch_shapes=scratch,
        compiler_params=pltpu.CompilerParams(vmem_limit_bytes=40 << 20),
        cost_estimate=spent(6 * count),
    )(*inputs)


def attend(queries, key_rows, value_rows, context, logsum):
    size = key_rows.shape[1] // 2
    lanes = lax.broadcasted_iota(jnp.int32, (1, 2 * size), 1)
    scale = size ** (-0.5)
    parts = []
    sums = []
    for head in range(2):
        own = (lanes < size) if head == 0 else (lanes >= size)
        scores = contract(jnp.where(own, queries[...], 0) * scale, key_rows[...], 1, 1)
        row_max = jnp.max(scores, axis=-1, keepdims=True)
        exponent = jnp.exp(scores - row_max)
        row_total = jnp.sum(exponent, axis=-1, keepdims=True)
        parts.append(
            contract(exponent.astype(jnp.bfloat16), value_rows[...], 1, 0) * (1.0 / row_total)
        )
        sums.append(row_max + jnp.log(row_total))
    context[...] = jnp.where(lanes < size, parts[0], parts[1]).astype(context.dtype)
    turned = jnp.transpose(jnp.where(lanes < size, sums[0], sums[1]))
    logsum[0:8, :] = turned[0:8]
    logsum[8:16, :] = turned[size : size + 8]


def attend_back(queries, key_rows, value_rows, logsum, grads, qkv_grad):
    size = key_rows.shape[1] // 2
    lanes = lax.broadcasted_iota(jnp.int32, (1, 2 * size), 1)
    scale = size ** (-0.5)
    parts = []
    key_sum, value_sum = 0.0, 0.0
    for head in range(2):
        own = (lanes < size) if head == 0 else (lanes >= size)
        own_rows = jnp.where(own, queries[...], 0) * scale
        own_grads = jnp.where(own, grads[...], 0)
        scores = contract(key_rows[...], own_rows, 1, 1)
        probs = jnp.exp(scores - logsum[8 * head : 8 * head + 1, :])
        value_sum = value_sum + contract(probs.astype(jnp.bfloat16), own_grads, 1, 0)
        prob_grad = contract(value_rows[...], own_grads, 1, 1)
        center = jnp.sum(prob_grad * probs, axis=0, keepdims=True)
        score_grad = (probs * (prob_grad - center)).astype(jnp.bfloat16)
        key_sum = key_sum + contract(score_grad, own_rows, 1, 0)
        parts.append(contract(score_grad, key_rows[...], 0, 0))
    query_sum = jnp.where(lanes < size, parts[0], parts[1]) * scale
    for number, total in enumerate((query_sum, key_sum, value_sum)):
        at = number * (qkv_grad.shape[1] // 3) + pl.program_id(0) * 2 * size
        qkv_grad[:, pl.ds(pl.multiple_of(at, 2 * size), 2 * size)] = total.astype(qkv_grad.dtype)


def column(rows, width, offset):
    return pl.BlockSpec((rows, width), lambda pair: (0, offset + pair))


def run_attend(qkv, first, pairs):
    length, across = qkv.shape
    every = across // 384
    return pl.pallas_call(
        attend,
        grid=(pairs,),
        in_specs=[column(length, 128, every * part + first) for part in range(3)],
        out_specs=[column(length, 128, 0), pl.BlockSpec((16, length), lambda pair: (pair, 0))],
        out_shape=(
            jax.ShapeDtypeStruct((length, 128 * pairs), jnp.bfloat16),
            jax.ShapeDtypeStruct((16 * pairs, length), jnp.float32),
        ),
        compiler_params=pltpu.CompilerParams(vmem_limit_bytes=28 << 20),
        cost_estimate=spent(5 * pairs),
    )(qkv, qkv, qkv)


def run_attend_back(qkv, logsum, grads, first):
    length, across = qkv.shape
    pairs = across // 384
    return pl.pallas_call(
        attend_back,
        grid=(pairs,),
        in_specs=[column(length, 128, pairs * part) for part in range(3)]
        + [pl.BlockSpec((16, length), lambda pair: (pair, 0)), column(length, 128, first)],
        out_specs=pl.BlockSpec((length, across), lambda pair: (0, 0)),
        out_shape=jax.ShapeDtypeStruct((length, across), jnp.bfloat16),
        compiler_params=pltpu.CompilerParams(vmem_limit_bytes=40 << 20),
        cost_estimate=spent(1),
    )(qkv, qkv, qkv, logsum, grads)


CHUNK = 512
SLOPE = 0.7978845608028654


def gelu_pair(values):
    square = values * values
    curve = jnp.tanh(SLOPE * values * (1.0 + 0.044715 * square))
    half = 0.5 * (1.0 + curve)
    slope = half + (0.5 * SLOPE) * values * (1.0 - curve * curve) * (1.0 + 3 * 0.044715 * square)
    return values * half, slope


def unit(values):
    center = jnp.mean(values, axis=-1, keepdims=True)
    shifted = values - center
    spread = jnp.mean(shifted * shifted, axis=-1, keepdims=True)
    root = lax.rsqrt(spread + 1e-05)
    return shifted * root, root


def unit_back(normal, root, given):
    return (
        given
        - jnp.mean(given, axis=-1, keepdims=True)
        - normal * jnp.mean(given * normal, axis=-1, keepdims=True)
    ) * root


def column_sum(values):
    return jnp.sum(values.reshape(-1, 8, values.shape[1]), axis=0)


def feed_ahead(mixed, gains, up, down, summed, feature):
    normal, _ = unit(mixed[...])
    normed = normal * gains[0:1]
    hidden = contract(normed.astype(jnp.bfloat16), up[...], 1, 0)
    active, _ = gelu_pair(hidden)
    total = normed + contract(active.astype(jnp.bfloat16), down[...], 1, 0)
    summed[...] = total
    normal, _ = unit(total)
    feature[...] = (normal * gains[1:2]).astype(feature.dtype)


def feed_back(
    mixed, summed, feature_grad, gains, up, down, out,
    active_out, hidden_grad, ffn_out, normed_out, mixed_grad, attended, context_grad, gain_sums
):
    @pl.when(pl.program_id(0) == 0)
    def start():
        gain_sums[...] = jnp.zeros_like(gain_sums)

    normal, root = unit(summed[...])
    given = feature_grad[...].astype(jnp.float32)
    gain_sums[8:16] += column_sum(given * normal)
    summed_grad = unit_back(normal, root, given * gains[1:2])
    ffn_grad = summed_grad.astype(jnp.bfloat16)
    ffn_out[...] = ffn_grad
    normal, root = unit(mixed[...])
    normed = (normal * gains[0:1]).astype(jnp.bfloat16)
    normed_out[...] = normed
    hidden = contract(normed, up[...], 1, 0)
    active, slope = gelu_pair(hidden)
    active_out[...] = active.astype(jnp.bfloat16)
    hidden_grad[...] = (slope * contract(ffn_grad, down[...], 1, 1)).astype(jnp.bfloat16)
    normed_grad = summed_grad + contract(hidden_grad[...], up[...], 1, 1)
    gain_sums[0:8] += column_sum(normed_grad * normal)
    total = unit_back(normal, root, normed_grad * gains[0:1])
    mixed_grad[...] = total
    attended[...] = total.astype(jnp.bfloat16)
    context_grad[...] = contract(attended[...], out[...], 1, 1).astype(jnp.bfloat16)


def blend_both(
    order, feature, pooled, mine, theirs, gains, blend,
    result, feature_grad, state_grad, grads, gain_sum, early, middle, late, spread, total
):
    length = feature.shape[0]
    pair = 2 * D
    rows = 128
    chunks = [slice(at, at + rows) for at in range(0, length, rows)]

    def ahead(number):
        return contract(feature[...], blend[number * pair : number * pair + D, :], 1, 0) + contract(
            pooled[...], blend[number * pair + D : number * pair + pair, :], 1, 0
        )

    edge = jnp.zeros((8, D), jnp.float32)
    early[0:8] = edge
    late[length : length + 8] = edge
    spread[0:8] = edge
    spread[length + 8 : length + 16] = edge
    early[8 : length + 8] = ahead(0)
    middle[...] = ahead(1)
    late[0:length] = ahead(2)
    gain_sum[...] = jnp.zeros_like(gain_sum)
    for chunk in chunks:
        before = slice(chunk.start + 7, chunk.stop + 7)
        after = slice(chunk.start + 1, chunk.stop + 1)
        blended, slope = gelu_pair(middle[chunk] + early[before] + late[after])
        normal, root = unit(feature[chunk].astype(jnp.float32) + blended)
        result[chunk] = (normal * gains[2:3]).astype(result.dtype)
        half = length // 2
        within = slice(chunk.start % half, chunk.start % half + rows)
        given = jnp.where(
            order[0] == chunk.start // half,
            mine[within].astype(jnp.float32),
            theirs[within].astype(jnp.float32),
        )
        gain_sum[...] += column_sum(given * normal)
        whole_grad = unit_back(normal, root, given * gains[2:3])
        total[chunk] = whole_grad
        spread[slice(chunk.start + 8, chunk.stop + 8)] = whole_grad * slope
    for chunk in chunks:
        for number, offset in ((0, 9), (1, 8), (2, 7)):
            grads[chunk, number * D : number * D + D] = spread[
                slice(chunk.start + offset, chunk.stop + offset)
            ].astype(jnp.bfloat16)

    def back(left):
        return sum(
            contract(
                grads[:, number * D : number * D + D],
                blend[number * pair + left : number * pair + left + D, :],
                1,
                1,
            )
            for number in range(3)
        )

    feature_grad[...] = (total[...] + back(0)).astype(feature_grad.dtype)
    state_grad[...] = back(D)


def params(size):
    return pltpu.CompilerParams(vmem_limit_bytes=size << 20)


def rows_block(width):
    return pl.BlockSpec((CHUNK, width), lambda step: (step, 0))


def fixed(*shape):
    return pl.BlockSpec(shape, lambda step: (0,) * len(shape))


def run_feed(mixed, gains, up, down):
    length = mixed.shape[0]
    wide = up.shape[1]
    return pl.pallas_call(
        feed_ahead,
        grid=(length // CHUNK,),
        in_specs=[rows_block(D), fixed(3, D), fixed(D, wide), fixed(wide, D)],
        out_specs=[rows_block(D), rows_block(D)],
        out_shape=[
            jax.ShapeDtypeStruct((length, D), jnp.float32),
            jax.ShapeDtypeStruct((length, D), jnp.bfloat16),
        ],
        compiler_params=params(56),
        cost_estimate=spent(18),
    )(mixed, gains, up, down)


def run_feed_back(mixed, summed, feature_grad, gains, up, down, out):
    length = mixed.shape[0]
    wide = up.shape[1]
    bf = jnp.bfloat16
    f32 = jnp.float32
    widths = [(wide, bf), (wide, bf), (D, bf), (D, bf), (D, f32), (D, bf), (D, bf)]
    return pl.pallas_call(
        feed_back,
        grid=(length // CHUNK,),
        in_specs=[rows_block(D)] * 3 + [fixed(3, D), fixed(D, wide), fixed(wide, D), fixed(D, D)],
        out_specs=[rows_block(width) for width, _ in widths] + [fixed(16, D)],
        out_shape=[jax.ShapeDtypeStruct((length, width), kind) for width, kind in widths]
        + [jax.ShapeDtypeStruct((16, D), f32)],
        compiler_params=params(60),
        cost_estimate=spent(32),
    )(mixed, summed, feature_grad, gains, up, down, out)


def run_blend(order, feature, pooled, mine, theirs, gains, blend):
    length = feature.shape[0]
    bf = jnp.bfloat16
    f32 = jnp.float32
    return pl.pallas_call(
        blend_both,
        in_specs=[scalars()] + [pl.BlockSpec(memory_space=pltpu.VMEM)] * 6,
        out_shape=[
            jax.ShapeDtypeStruct((length, D), bf),
            jax.ShapeDtypeStruct((length, D), bf),
            jax.ShapeDtypeStruct((length, D), f32),
            jax.ShapeDtypeStruct((length, 3 * D), bf),
            jax.ShapeDtypeStruct((8, D), f32),
        ],
        scratch_shapes=[
            pltpu.VMEM((length + 8, D), f32),
            pltpu.VMEM((length, D), f32),
            pltpu.VMEM((length + 8, D), f32),
            pltpu.VMEM((length + 16, D), f32),
            pltpu.VMEM((length, D), f32),
        ],
        compiler_params=params(60),
        cost_estimate=spent(26),
    )(order, feature, pooled, mine, theirs, gains, blend)


def blend_weight_grad(feature, pooled, grads, out):
    out[0:D, :] = contract(feature[...], grads[...], 0, 0).astype(out.dtype)
    out[D : 2 * D, :] = contract(pooled[...], grads[...], 0, 0).astype(out.dtype)


def run_blend_grad(feature, pooled, grads):
    length = feature.shape[0]
    return pl.pallas_call(
        blend_weight_grad,
        grid=(3,),
        in_specs=[
            fixed(length, D),
            fixed(length, D),
            pl.BlockSpec((length, D), lambda third: (0, third)),
        ],
        out_specs=pl.BlockSpec((2 * D, D), lambda third: (third, 0)),
        out_shape=jax.ShapeDtypeStruct((6 * D, D), jnp.bfloat16),
        compiler_params=params(48),
        cost_estimate=spent(12),
    )(feature, pooled, grads)


def on_device(
    tokens_in,
    char_ids,
    char_lengths,
    out_grad,
    w_qkv,
    first_qkv,
    second_qkv,
    w_out,
    first_out,
    second_out,
    w_up,
    first_up,
    second_up,
    w_down,
    first_down,
    second_down,
    w_gru,
    first_gru,
    second_gru,
    w_blend,
    first_blend,
    second_blend,
    char_table,
    first_table,
    second_table,
    gains,
    first_gains,
    second_gains,
):
    masters = (w_qkv, w_out, w_up, w_down, w_gru, w_blend, char_table, gains)
    firsts = (
        first_qkv,
        first_out,
        first_up,
        first_down,
        first_gru,
        first_blend,
        first_table,
        first_gains,
    )
    seconds = (
        second_qkv,
        second_out,
        second_up,
        second_down,
        second_gru,
        second_blend,
        second_table,
        second_gains,
    )
    parts = lax.axis_size("stream") * lax.axis_size("dp")
    on_first = lax.axis_index("stream") == 0
    half_len = tokens_in.shape[1]
    flow = Flow()

    def both_halves(pair, got):
        kept = jnp.where(on_first, pair[0], pair[1])
        return jnp.where(
            on_first, jnp.concatenate([kept, got], 0), jnp.concatenate([got, kept], 0)
        )

    ids_row = jnp.where(on_first, char_ids[0], char_ids[1])
    lengths_row = jnp.where(on_first, char_lengths[0], char_lengths[1])

    queries = HEADS // 2
    groups = 3
    pairs = queries // groups
    wide = 128 * pairs
    everyone = ("stream", "dp")
    by_group = w_qkv.reshape(w_qkv.shape[0], 3, groups, -1).transpose(0, 2, 1, 3)
    by_group = by_group.reshape(w_qkv.shape[0], groups, -1)
    flow.begin("tokens", swap_chain(jnp.where(on_first, tokens_in[1], tokens_in[0])), [4])
    flow.begin("group0", gather_steps([by_group[:, 0]], False))
    flow.begin("group1", gather_steps([by_group[:, 1]], True))
    flow.slot(())
    flow.slot(())
    flow.begin("group2", gather_steps([by_group[:, 2], w_out], True))
    flow.begin("up", gather_steps([w_up], True), [0, 1, 0, 1, 0])
    flow.slot(())
    shards = flow.slot((char_table, w_gru, gains_rows(gains), w_blend))
    shapes = shapes_of(shards[:3], 1)
    packed = jnp.concatenate([to_rows(shard, 1)[0] for shard in shards[:3]], 0)
    rest = lax.all_gather(packed, everyone, axis=0, tiled=False)
    blend_all = lax.all_gather(
        shards[3].astype(jnp.bfloat16), everyone, axis=0, tiled=True
    )
    flow.begin("down", gather_steps([w_down], True), [0, 0, 1, 0, 0])
    flow.slot(())
    tokens = both_halves(tokens_in, flow.end("tokens"))
    weights, parts_qkv, contexts, logsums = [], [], [], []
    for number in range(groups):
        w_group, *w_more = flow.end("group%d" % number)
        if number == 2:
            shares = 1.0 / lengths_row.astype(jnp.float32)[:, None]
            ends = jnp.cumsum(lengths_row)
            segment = char_segments(ends, ids_row.shape[0])
            lengths_row = (segment, shares, ends)
        qkv = product(tokens, w_group).astype(jnp.bfloat16)
        context, logsum = run_attend(qkv, 0, pairs)
        qkv, context, logsum, tokens, lengths_row = flow.slot(
            (qkv, context, logsum, tokens, lengths_row)
        )
        weights.append(w_group)
        parts_qkv.append(qkv)
        contexts.append(context)
        logsums.append(logsum)
    (out_all,) = w_more
    segment, shares, ends = lengths_row
    context = jnp.concatenate(contexts, 1)
    table_all, gru_all, gain_all = unpack_rows(rest, shapes)
    gain_all = jnp.sum(gain_all.reshape(parts, 8, D)[:, :3].astype(jnp.float32), 0)
    letters, before, pooled = run_chars(ids_row, ends, table_all, gru_all, shares)
    letters, before, pooled, context, tokens = flow.slot((letters, before, pooled, context, tokens))
    mixed_sum = tokens.astype(jnp.float32) + product(context, out_all)
    mixed_sum, gain_all = flow.slot((mixed_sum, gain_all))
    flow.begin("out_grad", swap_chain(jnp.where(on_first, out_grad[1], out_grad[0])))
    (up_all,) = flow.end("up")
    (down_all,) = flow.end("down")
    summed, feature = run_feed(mixed_sum, gain_all, up_all, down_all)
    summed, feature, blend_all = flow.slot((summed, feature, blend_all))
    result, feature_grad, state_grad, blend_grads, gain_blend = run_blend(
        lax.axis_index("stream").reshape(1),
        feature,
        pooled,
        jnp.where(on_first, out_grad[0], out_grad[1]),
        flow.end("out_grad"),
        gain_all,
        blend_all,
    )
    grad_blend = run_blend_grad(feature, pooled, blend_grads)
    result, grad_blend, feature_grad = flow.slot((result, grad_blend, feature_grad))
    (blend_sum,) = scatter_whole([grad_blend])
    flow.begin("result", swap_chain(jnp.where(on_first, result[half_len:], result[:half_len])))
    active, hidden_grad, ffn_grad, normed, mixed_grad, attended_grad, context_grad, gain_sums = (
        run_feed_back(mixed_sum, summed, feature_grad, gain_all, up_all, down_all, out_all)
    )
    gain_grads = jnp.concatenate(
        [jnp.sum(sums, 0, keepdims=True) for sums in (gain_sums[:8], gain_sums[8:], gain_blend)], 0
    )
    gain_grads = jnp.pad(gain_grads, ((0, 5), (0, 0))).astype(jnp.bfloat16)
    gain_rows = jnp.broadcast_to(gain_grads[None], (parts, 8, D)).reshape(8 * parts, D)
    if in_pairs([(w_down.shape[0], 1), (w_up.shape[0], 4)]):
        feed_grad = run_feed_grads(active, ffn_grad, normed, hidden_grad)
    else:
        feed_grad = [
            inner_rows(active, ffn_grad).astype(jnp.bfloat16),
            inner_rows(normed, hidden_grad).astype(jnp.bfloat16),
        ]
    grad_out = inner_rows(context, attended_grad).astype(jnp.bfloat16)
    feed_grad, grad_out, state_grad, context_grad, gain_rows = flow.slot(
        (feed_grad, grad_out, state_grad, context_grad, gain_rows)
    )
    flow.begin(
        "feed",
        feed_chain(feed_grad, [(w_down.shape[0], 1), (w_up.shape[0], 4)]),
        [0, 0, 0, 0, 1],
    )
    tokens_grad = mixed_grad
    group_grads = []
    for number in range(groups):
        qkv_grad = run_attend_back(
            parts_qkv[number], logsums[number], context_grad, pairs * number
        )
        tokens_grad = tokens_grad + inner_cols(qkv_grad, weights[number])
        grad_group = inner_rows(tokens, qkv_grad).astype(jnp.bfloat16)
        if number == groups - 1:
            tokens_grad = tokens_grad.astype(jnp.bfloat16)
        if number != 1:
            done = (context_grad, grad_group, tokens_grad, state_grad)
            done, blend_sum = flow.slot((done, blend_sum)) if number else (flow.slot(done), blend_sum)
            context_grad, grad_group, tokens_grad, state_grad = done
        group_grads.append(grad_group)
    flow.begin("qkv", scatter_chain(group_grads + [grad_out, gain_rows]), [0, 0, 1])
    blocks = ids_row.shape[0] // STEP_ROWS
    spread, *held = run_chars_back(
        blocks, blocks // 2, ids_row, segment, letters, before, upstream=[state_grad, shares]
    )
    spread, held = flow.slot((spread, held))
    grad_gru, grad_table = run_chars_back(
        blocks // 2,
        blocks // 2,
        ids_row,
        segment,
        letters,
        before,
        held=[spread, *held],
        ends=[table_all, gru_all],
    )
    grad_gru, grad_table, tokens_grad = flow.slot((grad_gru, grad_table, tokens_grad))
    flow.begin("letters", scatter_chain([grad_gru, grad_table]))
    flow.begin(
        "tokens",
        swap_chain(jnp.where(on_first, tokens_grad[half_len:], tokens_grad[:half_len])),
        [1],
    )
    while flow.live:
        flow.slot(())
    own_result = jnp.where(on_first, result[:half_len], result[half_len:])
    own_grad = jnp.where(on_first, tokens_grad[:half_len], tokens_grad[half_len:])
    back_result, back_grad = flow.end("result"), flow.end("tokens")
    block_parts = [
        jnp.where(on_first, own_result, back_result),
        jnp.where(on_first, back_result, own_result),
    ]
    grad_parts = [
        jnp.where(on_first, own_grad, back_grad),
        jnp.where(on_first, back_grad, own_grad),
    ]
    *group_sums, out_sum, gain_sum = flow.end("qkv")
    group_sums = jnp.stack(group_sums, 1)
    qkv_sum = group_sums.reshape(w_qkv.shape[0], groups, 3, -1).transpose(0, 2, 1, 3)
    letter_sums = flow.end("letters")
    feed_sums = flow.end("feed")
    sums = (
        qkv_sum.reshape(w_qkv.shape),
        out_sum,
        feed_sums[1],
        feed_sums[0],
        letter_sums[0],
        blend_sum,
        letter_sums[1],
        lax.dynamic_slice(
            gain_sum, (0, my_place()[0] * gains.shape[1]), gains.shape
        ),
    )
    rates = step_rates()
    results = [
        adamw(masters[number], firsts[number], seconds[number], sums[number], rates[number])
        for number in range(8)
    ]
    return (
        jnp.stack(block_parts),
        jnp.stack(grad_parts),
        results[0][0],
        results[0][1],
        results[0][2],
        results[1][0],
        results[1][1],
        results[1][2],
        results[2][0],
        results[2][1],
        results[2][2],
        results[3][0],
        results[3][1],
        results[3][2],
        results[4][0],
        results[4][1],
        results[4][2],
        results[5][0],
        results[5][1],
        results[5][2],
        results[6][0],
        results[6][1],
        results[6][2],
        results[7][0],
        results[7][1],
        results[7][2],
    )


def solution(mesh):
    in_specs = (
        P("dp", "stream", None),
        P("dp", None),
        P("dp", None),
        P("dp", "stream", None),
        P(("stream", "dp"), None),
        P(("stream", "dp"), None),
        P(("stream", "dp"), None),
        P(("stream", "dp"), None),
        P(("stream", "dp"), None),
        P(("stream", "dp"), None),
        P(("stream", "dp"), None),
        P(("stream", "dp"), None),
        P(("stream", "dp"), None),
        P(("stream", "dp"), None),
        P(("stream", "dp"), None),
        P(("stream", "dp"), None),
        P(("stream", "dp"), None),
        P(("stream", "dp"), None),
        P(("stream", "dp"), None),
        P(("stream", "dp"), None),
        P(("stream", "dp"), None),
        P(("stream", "dp"), None),
        P(("stream", "dp"), None),
        P(("stream", "dp"), None),
        P(("stream", "dp"), None),
        P(None, ("stream", "dp")),
        P(None, ("stream", "dp")),
        P(None, ("stream", "dp")),
    )
    out_specs = (
        P("dp", "stream", None),
        P("dp", "stream", None),
        P(("stream", "dp"), None),
        P(("stream", "dp"), None),
        P(("stream", "dp"), None),
        P(("stream", "dp"), None),
        P(("stream", "dp"), None),
        P(("stream", "dp"), None),
        P(("stream", "dp"), None),
        P(("stream", "dp"), None),
        P(("stream", "dp"), None),
        P(("stream", "dp"), None),
        P(("stream", "dp"), None),
        P(("stream", "dp"), None),
        P(("stream", "dp"), None),
        P(("stream", "dp"), None),
        P(("stream", "dp"), None),
        P(("stream", "dp"), None),
        P(("stream", "dp"), None),
        P(("stream", "dp"), None),
        P(("stream", "dp"), None),
        P(("stream", "dp"), None),
        P(("stream", "dp"), None),
        P(None, ("stream", "dp")),
        P(None, ("stream", "dp")),
        P(None, ("stream", "dp")),
    )
    return jax.shard_map(
        on_device, mesh=mesh, in_specs=in_specs, out_specs=out_specs, check_vma=False
    )
```

```python
import functools

import jax
import jax.numpy as jnp
from jax import lax
from jax.experimental import pallas as pl
from jax.experimental.pallas import tpu as pltpu
from jax.sharding import PartitionSpec as P

D = 768
HEADS = 12
FF = 3072
LEN = 1024
STEP = 5


def to_rows(matrix, parts):
    side = matrix.shape[1] // D
    own = matrix.shape[0] // parts
    blocks = matrix.astype(jnp.bfloat16).reshape(parts, own, side, D)
    return blocks.transpose(0, 2, 1, 3).reshape(parts, side * own, D)


def from_rows(rows, offset, own, side):
    parts = rows.shape[0]
    blocks = rows[:, offset : offset + own * side].reshape(parts, side, own, D)
    return blocks.transpose(0, 2, 1, 3).reshape(parts * own, side * D)


def gains_rows(gains):
    blank = jnp.zeros((8, D), jnp.float32)
    return lax.dynamic_update_slice(blank, gains, (0, my_place()[0] * gains.shape[1]))


def swap(block, mask):
    parts = lax.axis_size("dp") * lax.axis_size("stream")
    return lax.ppermute(block, ("stream", "dp"), [(place, place ^ mask) for place in range(parts)])


def pair_bits():
    return (lax.axis_size("dp") * lax.axis_size("stream")).bit_length() - 2


def in_pairs(shapes):
    parts = lax.axis_size("dp") * lax.axis_size("stream")
    return parts == 32 and all(rows % 8 == 0 for rows, _ in shapes)


def my_place():
    return (lax.axis_index("stream") * lax.axis_size("dp") + lax.axis_index("dp")).reshape(1)


def shapes_of(matrices, parts):
    return [(matrix.shape[0] // parts, matrix.shape[1] // D) for matrix in matrices]


def assemble(shapes, place, mine, theirs, *weights):
    core = place[0] & 1
    low = (place[0] >> 1) & 3
    pieces = []
    for pair in range(4):
        own = mine[pair ^ low].astype(jnp.float32)
        other = theirs[pair ^ low].astype(jnp.float32)
        pieces.append(jnp.where(core == 0, own, other))
        pieces.append(jnp.where(core == 0, other, own))
    offset = 0
    for (rows, side), weight in zip(shapes, weights):
        for number in range(side):
            block = jnp.concatenate([piece[offset : offset + rows] for piece in pieces], 0)
            weight[:, number * D : number * D + D] = block.astype(weight.dtype)
            offset += rows


def apart(shapes, place, *refs):
    grads, keep, send = refs[: len(shapes)], refs[-2], refs[-1]
    core = place[0] & 1
    low = (place[0] >> 1) & 3
    for pair in range(4):
        halves = []
        for side in range(2):
            pieces = []
            for (rows, across), grad in zip(shapes, grads):
                first = (2 * pair + side) * rows
                for number in range(across):
                    pieces.append(
                        grad[first : first + rows, number * D : number * D + D].astype(jnp.float32)
                    )
            halves.append(jnp.concatenate(pieces, 0))
        keep[pair ^ low] = jnp.where(core == 0, halves[0], halves[1]).astype(keep.dtype)
        send[pair ^ low] = jnp.where(core == 0, halves[1], halves[0]).astype(send.dtype)


def turned_block(high):
    return pl.BlockSpec((4, high, D), lambda group, place: (group ^ (place[0] >> 3), 0, 0))


def natural_block(shape):
    return pl.BlockSpec((8 * shape[0], shape[1] * D), lambda group, place: (group, 0))


class Flow:
    def __init__(self):
        self.live = {}
        self.ended = {}

    def begin(self, name, chain, skips=()):
        self.step(name, chain, None, list(skips))

    def step(self, name, chain, arrays, skips):
        try:
            waiting = chain.send(arrays)
            self.live[name] = [chain, waiting, skips, skips.pop(0) if skips else 0]
        except StopIteration as stop:
            self.ended[name] = stop.value

    def slot(self, values):
        due = [name for name, entry in self.live.items() if entry[3] == 0]
        for entry in self.live.values():
            entry[3] -= 1
        values, waited = lax.optimization_barrier(
            (values, [self.live[name][1] for name in due])
        )
        for name, arrays in zip(due, waited):
            chain, _, skips, _ = self.live.pop(name)
            self.step(name, chain, arrays, skips)
        return values

    def end(self, name):
        return self.ended.pop(name)


def gather_chain(shards, near_first=False):
    shapes = shapes_of(shards, 1)
    packed = jnp.concatenate([to_rows(shard, 1)[0] for shard in shards], 0)
    if not in_pairs(shapes):
        return gather_whole(packed, shapes)
    top = pair_bits()
    far = 1 << (top - 2)
    high = packed.shape[0]
    corner = 1 << top
    near = (2, corner, corner | 2)
    held = packed[None, None, None]
    for turn in range(2):
        if near_first == (turn == 0):
            held, *got = yield (held, *[swap(held, mask) for mask in near])
            held = jnp.concatenate(
                [jnp.concatenate([held, got[0]], 2), jnp.concatenate(got[1:], 2)], 0
            )
        else:
            held, *got = yield (held, *[swap(held, step << 2) for step in range(1, far)])
            held = jnp.concatenate([held, *got], 1)
    held = held.reshape(4 * far, high, D)
    held, other = yield (held, swap(held, 1))
    return join_halves(shapes, held, other)


def gather_steps(shards, turned):
    shapes = shapes_of(shards, 1)
    packed = jnp.concatenate([to_rows(shard, 1)[0] for shard in shards], 0)
    if not in_pairs(shapes):
        return gather_whole(packed, shapes)
    top = pair_bits()
    held = packed.reshape((1,) * top + packed.shape)
    for bit in list(range(2, top)) + ([1, top] if turned else [top, 1]):
        held, other = yield (held, swap(held, 1 << bit))
        held = jnp.concatenate([held, other], top - bit)
    held = held.reshape(1 << top, *packed.shape)
    held, other = yield (held, swap(held, 1))
    return join_halves(shapes, held, other)


def unpack(shapes, rows, *weights):
    pieces = [rows[number].astype(jnp.float32) for number in range(8)]
    offset = 0
    for (own, side), weight in zip(shapes, weights):
        for number in range(side):
            block = jnp.concatenate([piece[offset : offset + own] for piece in pieces], 0)
            weight[:, number * D : number * D + D] = block.astype(weight.dtype)
            offset += own


def unpack_rows(rows, shapes):
    parts, high = rows.shape[:2]
    if not in_pairs(shapes):
        return unpack_plain(rows, shapes)
    return pl.pallas_call(
        functools.partial(unpack, shapes),
        grid=(parts // 8,),
        in_specs=[pl.BlockSpec((8, high, D), lambda group: (group, 0, 0))],
        out_specs=[
            pl.BlockSpec((8 * own, side * D), lambda group: (group, 0)) for own, side in shapes
        ],
        out_shape=[
            jax.ShapeDtypeStruct((parts * own, side * D), jnp.bfloat16) for own, side in shapes
        ],
        compiler_params=pltpu.CompilerParams(vmem_limit_bytes=16 << 20),
        cost_estimate=spent(3),
    )(rows)


def unpack_plain(rows, shapes):
    pieces = []
    offset = 0
    for own, side in shapes:
        pieces.append(from_rows(rows, offset, own, side))
        offset += own * side
    return pieces


def gather_whole(packed, shapes):
    return unpack_rows(lax.all_gather(packed, ("stream", "dp"), axis=0, tiled=False), shapes)


def join_halves(shapes, mine, theirs):
    high = mine.shape[-2]
    pairs = 1 << pair_bits()
    parts = 2 * pairs
    return pl.pallas_call(
        functools.partial(assemble, shapes),
        grid_spec=pltpu.PrefetchScalarGridSpec(
            num_scalar_prefetch=1,
            grid=(pairs // 4,),
            in_specs=[turned_block(high)] * 2,
            out_specs=[natural_block(shape) for shape in shapes],
        ),
        out_shape=[
            jax.ShapeDtypeStruct((parts * rows, side * D), jnp.bfloat16) for rows, side in shapes
        ],
        compiler_params=pltpu.CompilerParams(vmem_limit_bytes=16 << 20),
        cost_estimate=spent(4),
    )(my_place(), mine.reshape(pairs, high, D), theirs.reshape(pairs, high, D))


def scatter_whole(grads):
    parts = lax.axis_size("dp") * lax.axis_size("stream")
    packed = jnp.concatenate([to_rows(grad, parts) for grad in grads], 1)
    total = lax.psum_scatter(
        packed.reshape(-1, D), ("stream", "dp"), scatter_dimension=0, tiled=True
    ).astype(jnp.float32)
    return own_pieces(total, shapes_of(grads, parts))


def own_pieces(total, shapes):
    pieces = []
    offset = 0
    for own, side in shapes:
        pieces.append(from_rows(total[None], offset, own, side))
        offset += own * side
    return pieces


def feed_grads(place, former, latter, given, source, keep, send, held):
    step = pl.program_id(0)
    core = place[0] & 1
    low = place[0] >> 1

    @pl.when(step < 4)
    def down():
        whole_grad = contract(former[...], given[...], 0, 0)
        rows = whole_grad.shape[0] // 8
        for pair in range(4):
            there = (4 * step + pair) ^ low
            first = whole_grad[2 * pair * rows : (2 * pair + 1) * rows]
            second = whole_grad[(2 * pair + 1) * rows : (2 * pair + 2) * rows]
            keep[there, 0:rows] = jnp.where(core == 0, first, second).astype(keep.dtype)
            send[there, 0:rows] = jnp.where(core == 0, second, first).astype(send.dtype)

    rows = D // held.shape[0]
    for number in range(4):

        @pl.when(step == 4 + number)
        def up():
            whole_grad = contract(source[...], latter[...], 0, 0)
            held[:, number * rows : number * rows + rows] = whole_grad.reshape(-1, rows, D)

    @pl.when(step == 7)
    def finish():
        start = 4 * rows
        for pair in range(held.shape[0] // 2):
            first, second = held[2 * pair], held[2 * pair + 1]
            there = pair ^ low
            keep[there, start:] = jnp.where(core == 0, first, second).astype(keep.dtype)
            send[there, start:] = jnp.where(core == 0, second, first).astype(send.dtype)


def run_feed_grads(active, ffn_grad, normed, hidden_grad):
    length, wide = active.shape
    parts = lax.axis_size("dp") * lax.axis_size("stream")
    pairs = parts // 2
    high = 2 * wide // parts
    half = jax.ShapeDtypeStruct((pairs, high, D), jnp.bfloat16)
    whole_half = pl.BlockSpec(half.shape, lambda step, place: (0, 0, 0))
    kept_rows = pl.BlockSpec((length, D), lambda step, place: (0, 0))
    return pl.pallas_call(
        feed_grads,
        grid_spec=pltpu.PrefetchScalarGridSpec(
            num_scalar_prefetch=1,
            grid=(8,),
            in_specs=[
                pl.BlockSpec((length, D), lambda step, place: (0, jnp.minimum(step, 3))),
                pl.BlockSpec((length, D), lambda step, place: (0, jnp.maximum(step - 4, 0))),
                kept_rows,
                kept_rows,
            ],
            out_specs=[whole_half, whole_half],
            scratch_shapes=[pltpu.VMEM((parts, high // 2, D), jnp.float32)],
        ),
        out_shape=[half, half],
        compiler_params=params(56),
        cost_estimate=spent(16),
    )(my_place(), active, hidden_grad, ffn_grad, normed)


def scatter_chain(grads, halving=False):
    parts = lax.axis_size("dp") * lax.axis_size("stream")
    shapes = shapes_of(grads, parts)
    if not in_pairs(shapes):
        return scatter_whole(grads)
    total = yield from halves_chain(*core_halves(grads, shapes, parts), False, halving)
    return own_pieces(total, shapes)


def core_halves(grads, shapes, parts):
    pairs = parts // 2
    high = sum(rows * side for rows, side in shapes)
    half = jax.ShapeDtypeStruct((pairs, high, D), jnp.bfloat16)
    return pl.pallas_call(
        functools.partial(apart, shapes),
        grid_spec=pltpu.PrefetchScalarGridSpec(
            num_scalar_prefetch=1,
            grid=(pairs // 4,),
            in_specs=[natural_block(shape) for shape in shapes],
            out_specs=[turned_block(high)] * 2,
        ),
        out_shape=[half, half],
        compiler_params=pltpu.CompilerParams(vmem_limit_bytes=16 << 20),
        cost_estimate=spent(4),
    )(my_place(), *[grad.astype(jnp.bfloat16) for grad in grads])


def halves_chain(kept, sent, split=False, halving=False):
    high = kept.shape[1]
    kept, other = yield (kept, swap(sent, 1))
    top = pair_bits()
    far = 1 << (top - 2)
    corner = 1 << top
    near = [(1, 0), (0, 1), (1, 1)]
    quarter = jax.ShapeDtypeStruct((far, high, D), jnp.bfloat16)
    views = [
        pl.BlockSpec((1, 1, 1, high, D), lambda row, x=x, y=y: (x, row, y, 0, 0))
        for x, y in [(0, 0)] + near
    ]
    total, *sent = pl.pallas_call(
        sum_quarters,
        grid=(far,),
        in_specs=views + views,
        out_specs=[pl.BlockSpec((1, high, D), lambda row: (row, 0, 0))] * 4,
        out_shape=[jax.ShapeDtypeStruct(quarter.shape, jnp.float32)] + [quarter] * 3,
        compiler_params=pltpu.CompilerParams(vmem_limit_bytes=16 << 20),
        cost_estimate=spent(3),
    )(*[kept.reshape(2, far, 2, high, D)] * 4, *[other.reshape(2, far, 2, high, D)] * 4)
    got = [swap(sent[0], corner), swap(sent[1], 2)]
    if split:
        total, last, *got = yield (total, sent[2], *got)
        total, got, last = yield (total, got, swap(last, corner | 2))
    else:
        total, last, *got = yield (total, swap(sent[2], corner | 2), *got)
    total = total + sum(block.astype(jnp.float32) for block in [last, *got])
    while halving and far > 1:
        far //= 2
        kept, other = yield (total[:far], swap(total[far:].astype(jnp.bfloat16), far << 2))
        total = kept + other.astype(jnp.float32)
    if halving:
        return total[0]
    others = [
        swap(total[number].astype(jnp.bfloat16), number << 2) for number in range(1, far)
    ]
    kept, *others = yield (total[0], *others)
    return kept + sum(other.astype(jnp.float32) for other in others)


def sum_quarters(*refs):
    for former, latter, out in zip(refs[:4], refs[4:8], refs[8:]):
        total = former[0, 0, 0].astype(jnp.float32) + latter[0, 0, 0].astype(jnp.float32)
        out[0] = total.astype(out.dtype)


def feed_chain(halves, shapes, split, halving):
    if not in_pairs(shapes):
        return scatter_whole(halves)
    total = yield from halves_chain(*halves, split, halving)
    return own_pieces(total, shapes)


def swap_chain(block):
    other = yield swap(block, lax.axis_size("dp"))
    return other


def product(former, latter):
    return jnp.dot(former, latter, preferred_element_type=jnp.float32)


def inner_rows(former, latter):
    return lax.dot_general(
        former, latter, (((0,), (0,)), ((), ())), preferred_element_type=jnp.float32
    )


def inner_cols(former, latter):
    return lax.dot_general(
        former, latter, (((1,), (1,)), ((), ())), preferred_element_type=jnp.float32
    )


def norm_gain(values, scales):
    center = jnp.mean(values, axis=-1, keepdims=True)
    shifted = values - center
    spread = jnp.mean(shifted * shifted, axis=-1, keepdims=True)
    return shifted * lax.rsqrt(spread + 1e-05) * scales


def rows_before(matrix):
    return jnp.concatenate([jnp.zeros_like(matrix[:1]), matrix[:-1]], 0)


def rows_after(matrix):
    return jnp.concatenate([matrix[1:], jnp.zeros_like(matrix[:1])], 0)


def char_segments(ends, char_count):
    places = lax.broadcasted_iota(jnp.int32, (ends.shape[0], char_count), 1)
    return jnp.sum((ends[:, None] <= places).astype(jnp.int32), axis=0)


def step_rates():
    return (
        0.5 * D ** (-0.5),
        0.5 * (3 * D // LEN) ** (-0.5),
        0.5 * D ** (-0.5),
        0.5 * FF ** (-0.5),
        0.5 * D ** (-0.5),
        0.5 * (6 * D) ** (-0.5),
        0.5,
        0.2,
    )


def adamw(master, first_m, second_m, grad_sum, step_rate):
    mean_new = 0.5 * first_m + 0.5 * grad_sum
    power = 0.5 * second_m + 0.5 * grad_sum * grad_sum
    correct = 1.0 - 0.5**STEP
    fresh_w = master - step_rate * (
        mean_new / correct / (jnp.sqrt(power / correct) + 1e-08) + 0.01 * master
    )
    return (fresh_w, mean_new, power)


STEP_ROWS = 512


def spent(microseconds):
    return pl.CostEstimate(
        flops=int(microseconds * 1e9), bytes_accessed=1, transcendentals=0
    )


UNROLL = 16


def contract(former, latter, left, right):
    return lax.dot_general(
        former, latter, (((left,), (right,)), ((), ())), preferred_element_type=jnp.float32
    )


def lane_blocks(width):
    blocks = []
    for number in range(2 * width // 128):
        side, lane = divmod(number * 128, width)
        blocks.append((number * 128, 2 * side * width + lane, 4 * side + lane // 128))
    return blocks


def eight(offset):
    return pl.ds(pl.multiple_of(offset, 8), 8)


def chars_ahead(rows_f, rows_b, ends, table, w_gru, shares, letters, before, pooled, running, spans, carry):
    block = pl.program_id(0)
    total = rows_f.shape[0]
    width = w_gru.shape[1] // 4

    @pl.when(block == 0)
    def start():
        logits = jnp.dot(table[...], w_gru[...], preferred_element_type=jnp.float32)
        letters[...] = jnp.zeros_like(letters)
        carry[...] = jnp.zeros_like(carry)
        for _, left, place in lane_blocks(width):
            update = jax.nn.sigmoid(logits[:, left : left + 128])
            letters[:, place, :] = 1.0 - update
            letters[:, 8 + place, :] = update * logits[:, left + width : left + width + 128]

    leading = lax.broadcasted_iota(jnp.int32, (8, 128), 0) < 4

    def several(group, held):
        state, total_state = held
        first = block * STEP_ROWS + group * UNROLL
        factors, adds = [], []
        for inner in range(UNROLL):
            id_f, id_b = rows_f[first + inner], rows_b[first + inner]
            factors.append(jnp.where(leading, letters[id_f, 0:8], letters[id_b, 0:8]))
            adds.append(jnp.where(leading, letters[id_f, 8:16], letters[id_b, 8:16]))
        for inner in range(UNROLL):
            before[group * UNROLL + inner] = state
            running[first + inner] = total_state
            state = factors[inner] * state + adds[inner]
            total_state = total_state + state
        return state, total_state

    state, total_state = lax.fori_loop(0, STEP_ROWS // UNROLL, several, (carry[0], carry[1]))
    carry[0] = state
    carry[1] = total_state

    @pl.when(block == pl.num_programs(0) - 1)
    def finish():
        running[total] = total_state

        def tokens(group, prior):
            found = []
            for inner in range(UNROLL):
                end = ends[group * UNROLL + inner]
                found.append(jnp.where(leading, running[end], -running[total - end]))
            for inner in range(UNROLL):
                spans[group * UNROLL + inner] = found[inner] - prior
                prior = found[inner]
            return prior

        lax.fori_loop(0, ends.shape[0] // UNROLL, tokens, jnp.where(leading, running[0], -running[total]))
        for at, _, place in lane_blocks(width):
            pooled[:, at : at + 128] = (spans[:, place, :] * shares[...]).astype(pooled.dtype)


def chars_back(blocks, opening, closing, *refs):
    rows_f, rows_b, owners_f, owners_b, letters, before = refs[:6]
    rest = list(refs[6:])
    take = lambda count: [rest.pop(0) for _ in range(count)]
    if opening:
        upstream, shares = take(2)
    else:
        spread, carry_in, *sums_in = take(6)
    if closing:
        position, table, w_gru = take(3)
    if opening:
        (spread,) = take(1)
    if closing:
        grad_gru, grad_table = take(2)
    else:
        carry_out, *sums_out = take(5)
    *sums, carry = take(5)
    if closing:
        (full,) = take(1)
    sums_f, sums_b, more_f, more_b = sums
    step_number = pl.program_id(0)
    block = blocks[0] - 1 - step_number
    width = 384

    @pl.when(step_number == 0)
    def start():
        if opening:
            for held in sums:
                held[...] = jnp.zeros_like(held)
            carry[...] = jnp.zeros_like(carry)
            for at, _, place in lane_blocks(width):
                spread[:, place, :] = upstream[:, at : at + 128] * shares[...]
            for place in (3, 7):
                spread[:, place, :] = jnp.zeros((spread.shape[0], 128), jnp.float32)
        else:
            for held, given in zip(sums, sums_in):
                held[...] = given[...]
            carry[...] = carry_in[...]

    leading = lax.broadcasted_iota(jnp.int32, (8, 128), 0) < 4

    def several(group, passed):
        steps = [STEP_ROWS - 1 - group * UNROLL - inner for inner in range(UNROLL)]
        kept, given, priors, owned = [], [], [], []
        for step in steps:
            place = block * STEP_ROWS + step
            id_f, id_b = rows_f[place], rows_b[place]
            owned.append((id_f, id_b))
            kept.append(jnp.where(leading, letters[id_f, 0:8], letters[id_b, 0:8]))
            given.append(jnp.where(leading, spread[owners_f[place]], spread[owners_b[place]]))
            priors.append(before[step])
        for inner in range(UNROLL):
            carried = given[inner] + passed
            passed = kept[inner] * carried
            moved = carried * priors[inner]
            id_f, id_b = owned[inner]
            for held, row, value in (
                (
                    (sums_f, more_f)[inner % 2],
                    id_f,
                    jnp.where(leading, carried, pltpu.roll(moved, 4, 0)),
                ),
                (
                    (sums_b, more_b)[inner % 2],
                    id_b,
                    jnp.where(leading, pltpu.roll(carried, 4, 0), moved),
                ),
            ):
                held[row] += value
        return passed

    carry[...] = lax.fori_loop(0, STEP_ROWS // UNROLL, several, carry[...])

    @pl.when(step_number == pl.num_programs(0) - 1)
    def finish():
        if not closing:
            carry_out[...] = carry[...]
            for held, given in zip(sums, sums_out):
                given[...] = held[...]
            return
        sums_f[...] += more_f[...]
        sums_b[...] += more_b[...]
        for _, left, place in lane_blocks(width):
            found = sums_f if place < 4 else sums_b
            lane = place % 4
            kept = letters[:, place, :]
            update = 1.0 - kept
            total = found[:, lane, :]
            full[:, left : left + 128] = kept * (
                letters[:, 8 + place, :] * total - update * found[:, 4 + lane, :]
            )
            full[:, left + width : left + width + 128] = update * total
        found = full[...].astype(jnp.bfloat16)
        whole_gru = contract(table[...], found, 0, 0)
        whole_table = contract(found, w_gru[...], 1, 1)
        if grad_gru.shape[0] == whole_gru.shape[0]:
            grad_gru[...] = whole_gru.astype(grad_gru.dtype)
            grad_table[...] = whole_table.astype(grad_table.dtype)
            return
        pairs = grad_gru.shape[0]
        high, low = whole_gru.shape[0] // (2 * pairs), whole_table.shape[0] // (2 * pairs)
        core = position[0] & 1
        for pair in range(pairs):
            halves = []
            for side in range(2):
                at = 2 * pair + side
                rows = whole_gru[at * high : at * high + high]
                halves.append(
                    jnp.concatenate(
                        [rows[:, :D], rows[:, D:], whole_table[at * low : at * low + low]], 0
                    )
                )
            there = pair ^ (position[0] >> 1)
            grad_gru[there] = jnp.where(core == 0, halves[0], halves[1]).astype(grad_gru.dtype)
            grad_table[there] = jnp.where(core == 0, halves[1], halves[0]).astype(grad_table.dtype)


def whole(array):
    return pl.BlockSpec(array.shape, lambda block: (0,) * len(array.shape))


def scalars():
    return pl.BlockSpec(memory_space=pltpu.SMEM)


def run_chars(ids, ends, table, w_gru, shares):
    total, count = ids.shape[0], shares.shape[0]
    f32 = jnp.float32
    outs = (
        jax.ShapeDtypeStruct((table.shape[0], 16, 128), f32),
        jax.ShapeDtypeStruct((total, 8, 128), f32),
        jax.ShapeDtypeStruct((count, w_gru.shape[1] // 2), jnp.bfloat16),
    )
    return pl.pallas_call(
        chars_ahead,
        grid=(total // STEP_ROWS,),
        in_specs=[scalars(), scalars(), scalars(), whole(table), whole(w_gru), whole(shares)],
        out_specs=[
            whole(outs[0]),
            pl.BlockSpec((STEP_ROWS, 8, 128), lambda block: (block, 0, 0)),
            whole(outs[2]),
        ],
        out_shape=outs,
        scratch_shapes=[
            pltpu.VMEM((total + 1, 8, 128), f32),
            pltpu.VMEM((count, 8, 128), f32),
            pltpu.VMEM((2, 8, 128), f32),
        ],
        compiler_params=pltpu.CompilerParams(vmem_limit_bytes=44 << 20),
        cost_estimate=spent(24),
    )(ids, jnp.flip(ids), ends, table, w_gru, shares)


def letter_shapes(ends, parts):
    return [(ends[1].shape[0] // parts, ends[1].shape[1] // D), (ends[0].shape[0] // parts, 1)]


def run_chars_back(last, count, ids, owners, letters, before, *, upstream=None, held=None, ends=None):
    f32 = jnp.float32
    tile = jax.ShapeDtypeStruct((letters.shape[0], 8, 128), f32)
    flat = jax.ShapeDtypeStruct((8, 128), f32)
    inputs = [ids, jnp.flip(ids), owners, jnp.flip(owners), letters, before]
    blocks = [scalars()] * 4 + [
        whole(letters),
        pl.BlockSpec((STEP_ROWS, 8, 128), lambda block: (last - 1 - block, 0, 0)),
    ]
    outs = []
    if upstream is not None:
        inputs += upstream
        outs.append(jax.ShapeDtypeStruct((upstream[0].shape[0], 8, 128), f32))
    else:
        inputs += held
    if ends is not None:
        inputs += [my_place()] + ends
        parts = lax.axis_size("dp") * lax.axis_size("stream")
        if in_pairs(letter_shapes(ends, parts)):
            high = sum(rows * side for rows, side in letter_shapes(ends, parts))
            outs += [jax.ShapeDtypeStruct((parts // 2, high, D), jnp.bfloat16)] * 2
        else:
            outs += [jax.ShapeDtypeStruct(array.shape, jnp.bfloat16) for array in ends[::-1]]
    else:
        outs += [flat] + [tile] * 4
    blocks += [scalars() if array.shape == (1,) else whole(array) for array in inputs[6:]]
    scratch = [pltpu.VMEM(tile.shape, f32)] * 4 + [pltpu.VMEM(flat.shape, f32)]
    if ends is not None:
        scratch.append(pltpu.VMEM((ends[0].shape[0], ends[1].shape[1]), f32))
    return pl.pallas_call(
        functools.partial(chars_back, (last,), upstream is not None, ends is not None),
        grid=(count,),
        in_specs=blocks,
        out_specs=[whole(out) for out in outs],
        out_shape=outs,
        scratch_shapes=scratch,
        compiler_params=pltpu.CompilerParams(vmem_limit_bytes=40 << 20),
        cost_estimate=spent(6 * count),
    )(*inputs)


def attend(queries, key_rows, value_rows, context, logsum):
    size = key_rows.shape[1] // 2
    lanes = lax.broadcasted_iota(jnp.int32, (1, 2 * size), 1)
    scale = size ** (-0.5)
    parts = []
    sums = []
    for head in range(2):
        own = (lanes < size) if head == 0 else (lanes >= size)
        scores = contract(jnp.where(own, queries[...], 0) * scale, key_rows[...], 1, 1)
        row_max = jnp.max(scores, axis=-1, keepdims=True)
        exponent = jnp.exp(scores - row_max)
        row_total = jnp.sum(exponent, axis=-1, keepdims=True)
        parts.append(
            contract(exponent.astype(jnp.bfloat16), value_rows[...], 1, 0) * (1.0 / row_total)
        )
        sums.append(row_max + jnp.log(row_total))
    context[...] = jnp.where(lanes < size, parts[0], parts[1]).astype(context.dtype)
    turned = jnp.transpose(jnp.where(lanes < size, sums[0], sums[1]))
    logsum[0:8, :] = turned[0:8]
    logsum[8:16, :] = turned[size : size + 8]


def attend_back(queries, key_rows, value_rows, logsum, grads, qkv_grad):
    size = key_rows.shape[1] // 2
    lanes = lax.broadcasted_iota(jnp.int32, (1, 2 * size), 1)
    scale = size ** (-0.5)
    parts = []
    key_sum, value_sum = 0.0, 0.0
    for head in range(2):
        own = (lanes < size) if head == 0 else (lanes >= size)
        own_rows = jnp.where(own, queries[...], 0) * scale
        own_grads = jnp.where(own, grads[...], 0)
        scores = contract(key_rows[...], own_rows, 1, 1)
        probs = jnp.exp(scores - logsum[8 * head : 8 * head + 1, :])
        value_sum = value_sum + contract(probs.astype(jnp.bfloat16), own_grads, 1, 0)
        prob_grad = contract(value_rows[...], own_grads, 1, 1)
        center = jnp.sum(prob_grad * probs, axis=0, keepdims=True)
        score_grad = (probs * (prob_grad - center)).astype(jnp.bfloat16)
        key_sum = key_sum + contract(score_grad, own_rows, 1, 0)
        parts.append(contract(score_grad, key_rows[...], 0, 0))
    query_sum = jnp.where(lanes < size, parts[0], parts[1]) * scale
    for number, total in enumerate((query_sum, key_sum, value_sum)):
        at = number * (qkv_grad.shape[1] // 3) + pl.program_id(0) * 2 * size
        qkv_grad[:, pl.ds(pl.multiple_of(at, 2 * size), 2 * size)] = total.astype(qkv_grad.dtype)


def column(rows, width, offset):
    return pl.BlockSpec((rows, width), lambda pair: (0, offset + pair))


def run_attend(qkv, first, pairs):
    length, across = qkv.shape
    every = across // 384
    return pl.pallas_call(
        attend,
        grid=(pairs,),
        in_specs=[column(length, 128, every * part + first) for part in range(3)],
        out_specs=[column(length, 128, 0), pl.BlockSpec((16, length), lambda pair: (pair, 0))],
        out_shape=(
            jax.ShapeDtypeStruct((length, 128 * pairs), jnp.bfloat16),
            jax.ShapeDtypeStruct((16 * pairs, length), jnp.float32),
        ),
        compiler_params=pltpu.CompilerParams(vmem_limit_bytes=28 << 20),
        cost_estimate=spent(5 * pairs),
    )(qkv, qkv, qkv)


def run_attend_back(qkv, logsum, grads, first):
    length, across = qkv.shape
    pairs = across // 384
    return pl.pallas_call(
        attend_back,
        grid=(pairs,),
        in_specs=[column(length, 128, pairs * part) for part in range(3)]
        + [pl.BlockSpec((16, length), lambda pair: (pair, 0)), column(length, 128, first)],
        out_specs=pl.BlockSpec((length, across), lambda pair: (0, 0)),
        out_shape=jax.ShapeDtypeStruct((length, across), jnp.bfloat16),
        compiler_params=pltpu.CompilerParams(vmem_limit_bytes=30 << 20),
        cost_estimate=spent(1),
    )(qkv, qkv, qkv, logsum, grads)


CHUNK = 512
SLOPE = 0.7978845608028654


def gelu_pair(values):
    square = values * values
    curve = jnp.tanh(SLOPE * values * (1.0 + 0.044715 * square))
    half = 0.5 * (1.0 + curve)
    slope = half + (0.5 * SLOPE) * values * (1.0 - curve * curve) * (1.0 + 3 * 0.044715 * square)
    return values * half, slope


def unit(values):
    center = jnp.mean(values, axis=-1, keepdims=True)
    shifted = values - center
    spread = jnp.mean(shifted * shifted, axis=-1, keepdims=True)
    root = lax.rsqrt(spread + 1e-05)
    return shifted * root, root


def unit_back(normal, root, given):
    return (
        given
        - jnp.mean(given, axis=-1, keepdims=True)
        - normal * jnp.mean(given * normal, axis=-1, keepdims=True)
    ) * root


def column_sum(values):
    return jnp.sum(values.reshape(-1, 8, values.shape[1]), axis=0)


def feed_ahead(mixed, gains, up, down, summed, feature):
    normal, _ = unit(mixed[...])
    normed = normal * gains[0:1]
    hidden = contract(normed.astype(jnp.bfloat16), up[...], 1, 0)
    active, _ = gelu_pair(hidden)
    total = normed + contract(active.astype(jnp.bfloat16), down[...], 1, 0)
    summed[...] = total
    normal, _ = unit(total)
    feature[...] = (normal * gains[1:2]).astype(feature.dtype)


def feed_back(
    mixed, summed, feature_grad, gains, up, down, out,
    active_out, hidden_grad, ffn_out, normed_out, mixed_grad, attended, context_grad, gain_sums
):
    @pl.when(pl.program_id(0) == 0)
    def start():
        gain_sums[...] = jnp.zeros_like(gain_sums)

    normal, root = unit(summed[...])
    given = feature_grad[...].astype(jnp.float32)
    gain_sums[8:16] += column_sum(given * normal)
    summed_grad = unit_back(normal, root, given * gains[1:2])
    ffn_grad = summed_grad.astype(jnp.bfloat16)
    ffn_out[...] = ffn_grad
    normal, root = unit(mixed[...])
    normed = (normal * gains[0:1]).astype(jnp.bfloat16)
    normed_out[...] = normed
    hidden = contract(normed, up[...], 1, 0)
    active, slope = gelu_pair(hidden)
    active_out[...] = active.astype(jnp.bfloat16)
    hidden_grad[...] = (slope * contract(ffn_grad, down[...], 1, 1)).astype(jnp.bfloat16)
    normed_grad = summed_grad + contract(hidden_grad[...], up[...], 1, 1)
    gain_sums[0:8] += column_sum(normed_grad * normal)
    total = unit_back(normal, root, normed_grad * gains[0:1])
    mixed_grad[...] = total
    attended[...] = total.astype(jnp.bfloat16)
    context_grad[...] = contract(attended[...], out[...], 1, 1).astype(jnp.bfloat16)


def blend_both(
    order, feature, pooled, mine, theirs, gains, blend,
    result, feature_grad, state_grad, grads, gain_sum, early, middle, late, spread, total
):
    length = feature.shape[0]
    pair = 2 * D
    rows = 128
    chunks = [slice(at, at + rows) for at in range(0, length, rows)]

    def ahead(number):
        return contract(feature[...], blend[number * pair : number * pair + D, :], 1, 0) + contract(
            pooled[...], blend[number * pair + D : number * pair + pair, :], 1, 0
        )

    edge = jnp.zeros((8, D), jnp.float32)
    early[0:8] = edge
    late[length : length + 8] = edge
    spread[0:8] = edge
    spread[length + 8 : length + 16] = edge
    early[8 : length + 8] = ahead(0)
    middle[...] = ahead(1)
    late[0:length] = ahead(2)
    gain_sum[...] = jnp.zeros_like(gain_sum)
    for chunk in chunks:
        before = slice(chunk.start + 7, chunk.stop + 7)
        after = slice(chunk.start + 1, chunk.stop + 1)
        blended, slope = gelu_pair(middle[chunk] + early[before] + late[after])
        normal, root = unit(feature[chunk].astype(jnp.float32) + blended)
        result[chunk] = (normal * gains[2:3]).astype(result.dtype)
        half = length // 2
        within = slice(chunk.start % half, chunk.start % half + rows)
        given = jnp.where(
            order[0] == chunk.start // half,
            mine[within].astype(jnp.float32),
            theirs[within].astype(jnp.float32),
        )
        gain_sum[...] += column_sum(given * normal)
        whole_grad = unit_back(normal, root, given * gains[2:3])
        total[chunk] = whole_grad
        spread[slice(chunk.start + 8, chunk.stop + 8)] = whole_grad * slope
    for chunk in chunks:
        for number, offset in ((0, 9), (1, 8), (2, 7)):
            grads[chunk, number * D : number * D + D] = spread[
                slice(chunk.start + offset, chunk.stop + offset)
            ].astype(jnp.bfloat16)

    def back(left):
        return sum(
            contract(
                grads[:, number * D : number * D + D],
                blend[number * pair + left : number * pair + left + D, :],
                1,
                1,
            )
            for number in range(3)
        )

    feature_grad[...] = (total[...] + back(0)).astype(feature_grad.dtype)
    state_grad[...] = back(D)


def params(size):
    return pltpu.CompilerParams(vmem_limit_bytes=size << 20)


def rows_block(width):
    return pl.BlockSpec((CHUNK, width), lambda step: (step, 0))


def fixed(*shape):
    return pl.BlockSpec(shape, lambda step: (0,) * len(shape), pipeline_mode=pl.Buffered(1))


def run_feed(mixed, gains, up, down):
    length = mixed.shape[0]
    wide = up.shape[1]
    return pl.pallas_call(
        feed_ahead,
        grid=(length // CHUNK,),
        in_specs=[rows_block(D), fixed(3, D), fixed(D, wide), fixed(wide, D)],
        out_specs=[rows_block(D), rows_block(D)],
        out_shape=[
            jax.ShapeDtypeStruct((length, D), jnp.float32),
            jax.ShapeDtypeStruct((length, D), jnp.bfloat16),
        ],
        compiler_params=params(56),
        cost_estimate=spent(18),
    )(mixed, gains, up, down)


def run_feed_back(mixed, summed, feature_grad, gains, up, down, out):
    length = mixed.shape[0]
    wide = up.shape[1]
    bf = jnp.bfloat16
    f32 = jnp.float32
    widths = [(wide, bf), (wide, bf), (D, bf), (D, bf), (D, f32), (D, bf), (D, bf)]
    return pl.pallas_call(
        feed_back,
        grid=(length // CHUNK,),
        in_specs=[rows_block(D)] * 3 + [fixed(3, D), fixed(D, wide), fixed(wide, D), fixed(D, D)],
        out_specs=[rows_block(width) for width, _ in widths] + [fixed(16, D)],
        out_shape=[jax.ShapeDtypeStruct((length, width), kind) for width, kind in widths]
        + [jax.ShapeDtypeStruct((16, D), f32)],
        compiler_params=params(60),
        cost_estimate=spent(32),
    )(mixed, summed, feature_grad, gains, up, down, out)


def run_blend(order, feature, pooled, mine, theirs, gains, blend):
    length = feature.shape[0]
    bf = jnp.bfloat16
    f32 = jnp.float32
    return pl.pallas_call(
        blend_both,
        in_specs=[scalars()] + [pl.BlockSpec(memory_space=pltpu.VMEM)] * 6,
        out_shape=[
            jax.ShapeDtypeStruct((length, D), bf),
            jax.ShapeDtypeStruct((length, D), bf),
            jax.ShapeDtypeStruct((length, D), f32),
            jax.ShapeDtypeStruct((length, 3 * D), bf),
            jax.ShapeDtypeStruct((8, D), f32),
        ],
        scratch_shapes=[
            pltpu.VMEM((length + 8, D), f32),
            pltpu.VMEM((length, D), f32),
            pltpu.VMEM((length + 8, D), f32),
            pltpu.VMEM((length + 16, D), f32),
            pltpu.VMEM((length, D), f32),
        ],
        compiler_params=params(60),
        cost_estimate=spent(26),
    )(order, feature, pooled, mine, theirs, gains, blend)


def blend_weight_grad(feature, pooled, grads, out):
    out[0:D, :] = contract(feature[...], grads[...], 0, 0).astype(out.dtype)
    out[D : 2 * D, :] = contract(pooled[...], grads[...], 0, 0).astype(out.dtype)


def run_blend_grad(feature, pooled, grads):
    length = feature.shape[0]
    return pl.pallas_call(
        blend_weight_grad,
        grid=(3,),
        in_specs=[
            fixed(length, D),
            fixed(length, D),
            pl.BlockSpec((length, D), lambda third: (0, third)),
        ],
        out_specs=pl.BlockSpec((2 * D, D), lambda third: (third, 0)),
        out_shape=jax.ShapeDtypeStruct((6 * D, D), jnp.bfloat16),
        compiler_params=params(48),
        cost_estimate=spent(12),
    )(feature, pooled, grads)


def group_grads(place, tokens, first, second, third, context, attended, gains, keep, send, held):
    pairs, high, _ = keep.shape
    rows = D // (2 * pairs)
    pieces = [(tokens, first), (tokens, second), (tokens, third), (context, attended)]
    for number, (former, latter) in enumerate(pieces):
        whole_grad = contract(former[...], latter[...], 0, 0)
        held[:, number * rows : number * rows + rows] = whole_grad.reshape(2 * pairs, rows, D)
    held[:, 4 * rows :] = jnp.broadcast_to(gains[...][None], (2 * pairs, 8, D))
    core = place[0] & 1
    for pair in range(pairs):
        there = pair ^ (place[0] >> 1)
        former, latter = held[2 * pair], held[2 * pair + 1]
        keep[there] = jnp.where(core == 0, former, latter).astype(keep.dtype)
        send[there] = jnp.where(core == 0, latter, former).astype(send.dtype)


def run_group_grads(tokens, qkv_grads, context, attended, gains):
    parts = lax.axis_size("dp") * lax.axis_size("stream")
    high = 4 * (D // parts) + 8
    half = jax.ShapeDtypeStruct((parts // 2, high, D), jnp.bfloat16)
    return pl.pallas_call(
        group_grads,
        grid=(1,),
        in_specs=[scalars()]
        + [fixed(*array.shape) for array in (tokens, *qkv_grads, context, attended, gains)],
        out_specs=[fixed(*half.shape)] * 2,
        out_shape=[half, half],
        scratch_shapes=[pltpu.VMEM((parts, high, D), jnp.float32)],
        compiler_params=params(60),
        cost_estimate=spent(1),
    )(my_place(), tokens, *qkv_grads, context, attended, gains)


def on_device(
    tokens_in,
    char_ids,
    char_lengths,
    out_grad,
    w_qkv,
    first_qkv,
    second_qkv,
    w_out,
    first_out,
    second_out,
    w_up,
    first_up,
    second_up,
    w_down,
    first_down,
    second_down,
    w_gru,
    first_gru,
    second_gru,
    w_blend,
    first_blend,
    second_blend,
    char_table,
    first_table,
    second_table,
    gains,
    first_gains,
    second_gains,
):
    masters = (w_qkv, w_out, w_up, w_down, w_gru, w_blend, char_table, gains)
    firsts = (
        first_qkv,
        first_out,
        first_up,
        first_down,
        first_gru,
        first_blend,
        first_table,
        first_gains,
    )
    seconds = (
        second_qkv,
        second_out,
        second_up,
        second_down,
        second_gru,
        second_blend,
        second_table,
        second_gains,
    )
    parts = lax.axis_size("stream") * lax.axis_size("dp")
    on_first = lax.axis_index("stream") == 0
    half_len = tokens_in.shape[1]
    flow = Flow()

    def both_halves(pair, got):
        kept = jnp.where(on_first, pair[0], pair[1])
        return jnp.where(
            on_first, jnp.concatenate([kept, got], 0), jnp.concatenate([got, kept], 0)
        )

    ids_row = jnp.where(on_first, char_ids[0], char_ids[1])
    lengths_row = jnp.where(on_first, char_lengths[0], char_lengths[1])

    queries = HEADS // 2
    groups = 3
    pairs = queries // groups
    wide = 128 * pairs
    everyone = ("stream", "dp")
    by_group = w_qkv.reshape(w_qkv.shape[0], 3, groups, -1).transpose(0, 2, 1, 3)
    by_group = by_group.reshape(w_qkv.shape[0], groups, -1)
    flow.begin("tokens", swap_chain(jnp.where(on_first, tokens_in[1], tokens_in[0])), [4])
    flow.begin("group0", gather_steps([by_group[:, 0]], False))
    flow.begin("group1", gather_steps([by_group[:, 1]], True))
    flow.slot(())
    flow.slot(())
    flow.begin("group2", gather_steps([by_group[:, 2], w_out], True))
    flow.begin("up", gather_steps([w_up], True), [0, 1, 0, 1, 0])
    flow.slot(())
    shards = flow.slot((char_table, w_gru, gains_rows(gains), w_blend))
    shapes = shapes_of(shards[:3], 1)
    packed = jnp.concatenate([to_rows(shard, 1)[0] for shard in shards[:3]], 0)
    rest = lax.all_gather(packed, everyone, axis=0, tiled=False)
    blend_all = lax.all_gather(
        shards[3].astype(jnp.bfloat16), everyone, axis=0, tiled=True
    )
    flow.begin("down", gather_steps([w_down], True), [0, 0, 1, 0, 0])
    flow.slot(())
    tokens = both_halves(tokens_in, flow.end("tokens"))
    weights, parts_qkv, contexts, logsums = [], [], [], []
    for number in range(groups):
        w_group, *w_more = flow.end("group%d" % number)
        if number == 2:
            shares = 1.0 / lengths_row.astype(jnp.float32)[:, None]
            ends = jnp.cumsum(lengths_row)
            segment = char_segments(ends, ids_row.shape[0])
            lengths_row = (segment, shares, ends)
        qkv = product(tokens, w_group).astype(jnp.bfloat16)
        context, logsum = run_attend(qkv, 0, pairs)
        qkv, context, logsum, tokens, lengths_row = flow.slot(
            (qkv, context, logsum, tokens, lengths_row)
        )
        weights.append(w_group)
        parts_qkv.append(qkv)
        contexts.append(context)
        logsums.append(logsum)
    (out_all,) = w_more
    segment, shares, ends = lengths_row
    context = jnp.concatenate(contexts, 1)
    table_all, gru_all, gain_all = unpack_rows(rest, shapes)
    gain_all = jnp.sum(gain_all.reshape(parts, 8, D)[:, :3].astype(jnp.float32), 0)
    letters, before, pooled = run_chars(ids_row, ends, table_all, gru_all, shares)
    letters, before, pooled, context, tokens = flow.slot((letters, before, pooled, context, tokens))
    mixed_sum = tokens.astype(jnp.float32) + product(context, out_all)
    mixed_sum, gain_all = flow.slot((mixed_sum, gain_all))
    flow.begin("out_grad", swap_chain(jnp.where(on_first, out_grad[1], out_grad[0])))
    (up_all,) = flow.end("up")
    (down_all,) = flow.end("down")
    summed, feature = run_feed(mixed_sum, gain_all, up_all, down_all)
    summed, feature, blend_all = flow.slot((summed, feature, blend_all))
    result, feature_grad, state_grad, blend_grads, gain_blend = run_blend(
        lax.axis_index("stream").reshape(1),
        feature,
        pooled,
        jnp.where(on_first, out_grad[0], out_grad[1]),
        flow.end("out_grad"),
        gain_all,
        blend_all,
    )
    grad_blend = run_blend_grad(feature, pooled, blend_grads)
    result, grad_blend, feature_grad = flow.slot((result, grad_blend, feature_grad))
    (blend_sum,) = scatter_whole([grad_blend])
    flow.begin("result", swap_chain(jnp.where(on_first, result[half_len:], result[:half_len])))
    active, hidden_grad, ffn_grad, normed, mixed_grad, attended_grad, context_grad, gain_sums = (
        run_feed_back(mixed_sum, summed, feature_grad, gain_all, up_all, down_all, out_all)
    )
    gain_grads = jnp.concatenate(
        [jnp.sum(sums, 0, keepdims=True) for sums in (gain_sums[:8], gain_sums[8:], gain_blend)], 0
    )
    gain_grads = jnp.pad(gain_grads, ((0, 5), (0, 0)))
    if in_pairs([(w_down.shape[0], 1), (w_up.shape[0], 4)]):
        feed_grad = run_feed_grads(active, ffn_grad, normed, hidden_grad)
    else:
        feed_grad = [
            inner_rows(active, ffn_grad).astype(jnp.bfloat16),
            inner_rows(normed, hidden_grad).astype(jnp.bfloat16),
        ]
    feed_grad, state_grad, context_grad, gain_grads = flow.slot(
        (feed_grad, state_grad, context_grad, gain_grads)
    )
    flow.begin(
        "feed",
        feed_chain(feed_grad, [(w_down.shape[0], 1), (w_up.shape[0], 4)], True, True),
        [0, 0, 0, 0, 1],
    )
    tokens_grad = mixed_grad
    qkv_grads = []
    for number in range(groups):
        qkv_grad = run_attend_back(
            parts_qkv[number], logsums[number], context_grad, pairs * number
        )
        tokens_grad = tokens_grad + inner_cols(qkv_grad, weights[number])
        qkv_grads.append(qkv_grad)
        if number == 0:
            context_grad, tokens_grad, state_grad = flow.slot(
                (context_grad, tokens_grad, state_grad)
            )
    tokens_grad = tokens_grad.astype(jnp.bfloat16)
    qkv_shapes = [(w_qkv.shape[0], 1)] * 3 + [(w_out.shape[0], 1), (8, 1)]
    if in_pairs(qkv_shapes):
        qkv_halves = run_group_grads(tokens, qkv_grads, context, attended_grad, gain_grads)
    else:
        qkv_halves = [inner_rows(tokens, grad).astype(jnp.bfloat16) for grad in qkv_grads]
        qkv_halves.append(inner_rows(context, attended_grad).astype(jnp.bfloat16))
        gain_rows = jnp.broadcast_to(gain_grads[None], (parts, 8, D)).astype(jnp.bfloat16)
        qkv_halves.append(gain_rows.reshape(8 * parts, D))
    qkv_halves, tokens_grad, blend_sum = flow.slot((qkv_halves, tokens_grad, blend_sum))
    flow.begin("qkv", feed_chain(qkv_halves, qkv_shapes, False, True), [0, 0, 1, 0])
    blocks = ids_row.shape[0] // STEP_ROWS
    spread, *held = run_chars_back(
        blocks, blocks // 2, ids_row, segment, letters, before, upstream=[state_grad, shares]
    )
    spread, held = flow.slot((spread, held))
    grad_gru, grad_table = run_chars_back(
        blocks // 2,
        blocks // 2,
        ids_row,
        segment,
        letters,
        before,
        held=[spread, *held],
        ends=[table_all, gru_all],
    )
    grad_gru, grad_table, tokens_grad = flow.slot((grad_gru, grad_table, tokens_grad))
    flow.begin(
        "letters",
        feed_chain([grad_gru, grad_table], letter_shapes([table_all, gru_all], parts), False, False),
    )
    flow.begin(
        "tokens",
        swap_chain(jnp.where(on_first, tokens_grad[half_len:], tokens_grad[:half_len])),
        [1],
    )
    while flow.live:
        flow.slot(())
    own_result = jnp.where(on_first, result[:half_len], result[half_len:])
    own_grad = jnp.where(on_first, tokens_grad[:half_len], tokens_grad[half_len:])
    back_result, back_grad = flow.end("result"), flow.end("tokens")
    block_parts = [
        jnp.where(on_first, own_result, back_result),
        jnp.where(on_first, back_result, own_result),
    ]
    grad_parts = [
        jnp.where(on_first, own_grad, back_grad),
        jnp.where(on_first, back_grad, own_grad),
    ]
    *group_sums, out_sum, gain_sum = flow.end("qkv")
    group_sums = jnp.stack(group_sums, 1)
    qkv_sum = group_sums.reshape(w_qkv.shape[0], groups, 3, -1).transpose(0, 2, 1, 3)
    letter_sums = flow.end("letters")
    feed_sums = flow.end("feed")
    sums = (
        qkv_sum.reshape(w_qkv.shape),
        out_sum,
        feed_sums[1],
        feed_sums[0],
        letter_sums[0],
        blend_sum,
        letter_sums[1],
        lax.dynamic_slice(
            gain_sum, (0, my_place()[0] * gains.shape[1]), gains.shape
        ),
    )
    rates = step_rates()
    results = [
        adamw(masters[number], firsts[number], seconds[number], sums[number], rates[number])
        for number in range(8)
    ]
    return (
        jnp.stack(block_parts),
        jnp.stack(grad_parts),
        results[0][0],
        results[0][1],
        results[0][2],
        results[1][0],
        results[1][1],
        results[1][2],
        results[2][0],
        results[2][1],
        results[2][2],
        results[3][0],
        results[3][1],
        results[3][2],
        results[4][0],
        results[4][1],
        results[4][2],
        results[5][0],
        results[5][1],
        results[5][2],
        results[6][0],
        results[6][1],
        results[6][2],
        results[7][0],
        results[7][1],
        results[7][2],
    )


def solution(mesh):
    in_specs = (
        P("dp", "stream", None),
        P("dp", None),
        P("dp", None),
        P("dp", "stream", None),
        P(("stream", "dp"), None),
        P(("stream", "dp"), None),
        P(("stream", "dp"), None),
        P(("stream", "dp"), None),
        P(("stream", "dp"), None),
        P(("stream", "dp"), None),
        P(("stream", "dp"), None),
        P(("stream", "dp"), None),
        P(("stream", "dp"), None),
        P(("stream", "dp"), None),
        P(("stream", "dp"), None),
        P(("stream", "dp"), None),
        P(("stream", "dp"), None),
        P(("stream", "dp"), None),
        P(("stream", "dp"), None),
        P(("stream", "dp"), None),
        P(("stream", "dp"), None),
        P(("stream", "dp"), None),
        P(("stream", "dp"), None),
        P(("stream", "dp"), None),
        P(("stream", "dp"), None),
        P(None, ("stream", "dp")),
        P(None, ("stream", "dp")),
        P(None, ("stream", "dp")),
    )
    out_specs = (
        P("dp", "stream", None),
        P("dp", "stream", None),
        P(("stream", "dp"), None),
        P(("stream", "dp"), None),
        P(("stream", "dp"), None),
        P(("stream", "dp"), None),
        P(("stream", "dp"), None),
        P(("stream", "dp"), None),
        P(("stream", "dp"), None),
        P(("stream", "dp"), None),
        P(("stream", "dp"), None),
        P(("stream", "dp"), None),
        P(("stream", "dp"), None),
        P(("stream", "dp"), None),
        P(("stream", "dp"), None),
        P(("stream", "dp"), None),
        P(("stream", "dp"), None),
        P(("stream", "dp"), None),
        P(("stream", "dp"), None),
        P(("stream", "dp"), None),
        P(("stream", "dp"), None),
        P(("stream", "dp"), None),
        P(("stream", "dp"), None),
        P(None, ("stream", "dp")),
        P(None, ("stream", "dp")),
        P(None, ("stream", "dp")),
    )
    return jax.shard_map(
        on_device, mesh=mesh, in_specs=in_specs, out_specs=out_specs, check_vma=False
    )
```

```python
import functools

import jax
import jax.numpy as jnp
from jax import lax
from jax.experimental import pallas as pl
from jax.experimental.pallas import tpu as pltpu
from jax.sharding import PartitionSpec as P

D = 768
HEADS = 12
FF = 3072
LEN = 1024
STEP = 5


def to_rows(matrix, parts):
    side = matrix.shape[1] // D
    own = matrix.shape[0] // parts
    blocks = matrix.astype(jnp.bfloat16).reshape(parts, own, side, D)
    return blocks.transpose(0, 2, 1, 3).reshape(parts, side * own, D)


def from_rows(rows, offset, own, side):
    parts = rows.shape[0]
    blocks = rows[:, offset : offset + own * side].reshape(parts, side, own, D)
    return blocks.transpose(0, 2, 1, 3).reshape(parts * own, side * D)


def gains_rows(gains):
    blank = jnp.zeros((8, D), jnp.float32)
    return lax.dynamic_update_slice(blank, gains, (0, my_place()[0] * gains.shape[1]))


def swap(block, mask):
    parts = lax.axis_size("dp") * lax.axis_size("stream")
    return lax.ppermute(block, ("stream", "dp"), [(place, place ^ mask) for place in range(parts)])


def pair_bits():
    return (lax.axis_size("dp") * lax.axis_size("stream")).bit_length() - 2


def in_pairs(shapes):
    parts = lax.axis_size("dp") * lax.axis_size("stream")
    return parts == 32 and all(rows % 8 == 0 for rows, _ in shapes)


def my_place():
    return (lax.axis_index("stream") * lax.axis_size("dp") + lax.axis_index("dp")).reshape(1)


def shapes_of(matrices, parts):
    return [(matrix.shape[0] // parts, matrix.shape[1] // D) for matrix in matrices]


def assemble(shapes, place, mine, theirs, *weights):
    core = place[0] & 1
    low = (place[0] >> 1) & 3
    pieces = []
    for pair in range(4):
        own = mine[pair ^ low].astype(jnp.float32)
        other = theirs[pair ^ low].astype(jnp.float32)
        pieces.append(jnp.where(core == 0, own, other))
        pieces.append(jnp.where(core == 0, other, own))
    offset = 0
    for (rows, side), weight in zip(shapes, weights):
        for number in range(side):
            block = jnp.concatenate([piece[offset : offset + rows] for piece in pieces], 0)
            weight[:, number * D : number * D + D] = block.astype(weight.dtype)
            offset += rows


def apart(shapes, place, *refs):
    grads, keep, send = refs[: len(shapes)], refs[-2], refs[-1]
    core = place[0] & 1
    low = (place[0] >> 1) & 3
    for pair in range(4):
        halves = []
        for side in range(2):
            pieces = []
            for (rows, across), grad in zip(shapes, grads):
                first = (2 * pair + side) * rows
                for number in range(across):
                    pieces.append(
                        grad[first : first + rows, number * D : number * D + D].astype(jnp.float32)
                    )
            halves.append(jnp.concatenate(pieces, 0))
        keep[pair ^ low] = jnp.where(core == 0, halves[0], halves[1]).astype(keep.dtype)
        send[pair ^ low] = jnp.where(core == 0, halves[1], halves[0]).astype(send.dtype)


def turned_block(high):
    return pl.BlockSpec((4, high, D), lambda group, place: (group ^ (place[0] >> 3), 0, 0))


def natural_block(shape):
    return pl.BlockSpec((8 * shape[0], shape[1] * D), lambda group, place: (group, 0))


class Flow:
    def __init__(self):
        self.live = {}
        self.ended = {}

    def begin(self, name, chain, skips=()):
        self.step(name, chain, None, list(skips))

    def step(self, name, chain, arrays, skips):
        try:
            waiting = chain.send(arrays)
            self.live[name] = [chain, waiting, skips, skips.pop(0) if skips else 0]
        except StopIteration as stop:
            self.ended[name] = stop.value

    def slot(self, values):
        due = [name for name, entry in self.live.items() if entry[3] == 0]
        for entry in self.live.values():
            entry[3] -= 1
        values, waited = lax.optimization_barrier(
            (values, [self.live[name][1] for name in due])
        )
        for name, arrays in zip(due, waited):
            chain, _, skips, _ = self.live.pop(name)
            self.step(name, chain, arrays, skips)
        return values

    def end(self, name):
        return self.ended.pop(name)


def gather_chain(shards, near_first=False):
    shapes = shapes_of(shards, 1)
    packed = jnp.concatenate([to_rows(shard, 1)[0] for shard in shards], 0)
    if not in_pairs(shapes):
        return gather_whole(packed, shapes)
    top = pair_bits()
    far = 1 << (top - 2)
    high = packed.shape[0]
    corner = 1 << top
    near = (2, corner, corner | 2)
    held = packed[None, None, None]
    for turn in range(2):
        if near_first == (turn == 0):
            held, *got = yield (held, *[swap(held, mask) for mask in near])
            held = jnp.concatenate(
                [jnp.concatenate([held, got[0]], 2), jnp.concatenate(got[1:], 2)], 0
            )
        else:
            held, *got = yield (held, *[swap(held, step << 2) for step in range(1, far)])
            held = jnp.concatenate([held, *got], 1)
    held = held.reshape(4 * far, high, D)
    held, other = yield (held, swap(held, 1))
    return join_halves(shapes, held, other)


def gather_steps(shards, turned):
    shapes = shapes_of(shards, 1)
    packed = jnp.concatenate([to_rows(shard, 1)[0] for shard in shards], 0)
    if not in_pairs(shapes):
        return gather_whole(packed, shapes)
    top = pair_bits()
    held = packed.reshape((1,) * top + packed.shape)
    for bit in list(range(2, top)) + ([1, top] if turned else [top, 1]):
        held, other = yield (held, swap(held, 1 << bit))
        held = jnp.concatenate([held, other], top - bit)
    held = held.reshape(1 << top, *packed.shape)
    held, other = yield (held, swap(held, 1))
    return join_halves(shapes, held, other)


def unpack(shapes, rows, *weights):
    pieces = [rows[number].astype(jnp.float32) for number in range(8)]
    offset = 0
    for (own, side), weight in zip(shapes, weights):
        for number in range(side):
            block = jnp.concatenate([piece[offset : offset + own] for piece in pieces], 0)
            weight[:, number * D : number * D + D] = block.astype(weight.dtype)
            offset += own


def unpack_rows(rows, shapes):
    parts, high = rows.shape[:2]
    if not in_pairs(shapes):
        return unpack_plain(rows, shapes)
    return pl.pallas_call(
        functools.partial(unpack, shapes),
        grid=(parts // 8,),
        in_specs=[pl.BlockSpec((8, high, D), lambda group: (group, 0, 0))],
        out_specs=[
            pl.BlockSpec((8 * own, side * D), lambda group: (group, 0)) for own, side in shapes
        ],
        out_shape=[
            jax.ShapeDtypeStruct((parts * own, side * D), jnp.bfloat16) for own, side in shapes
        ],
        compiler_params=pltpu.CompilerParams(vmem_limit_bytes=16 << 20),
        cost_estimate=spent(3),
    )(rows)


def unpack_plain(rows, shapes):
    pieces = []
    offset = 0
    for own, side in shapes:
        pieces.append(from_rows(rows, offset, own, side))
        offset += own * side
    return pieces


def gather_whole(packed, shapes):
    return unpack_rows(lax.all_gather(packed, ("stream", "dp"), axis=0, tiled=False), shapes)


def join_halves(shapes, mine, theirs):
    high = mine.shape[-2]
    pairs = 1 << pair_bits()
    parts = 2 * pairs
    return pl.pallas_call(
        functools.partial(assemble, shapes),
        grid_spec=pltpu.PrefetchScalarGridSpec(
            num_scalar_prefetch=1,
            grid=(pairs // 4,),
            in_specs=[turned_block(high)] * 2,
            out_specs=[natural_block(shape) for shape in shapes],
        ),
        out_shape=[
            jax.ShapeDtypeStruct((parts * rows, side * D), jnp.bfloat16) for rows, side in shapes
        ],
        compiler_params=pltpu.CompilerParams(vmem_limit_bytes=16 << 20),
        cost_estimate=spent(4),
    )(my_place(), mine.reshape(pairs, high, D), theirs.reshape(pairs, high, D))


def scatter_whole(grads):
    parts = lax.axis_size("dp") * lax.axis_size("stream")
    packed = jnp.concatenate([to_rows(grad, parts) for grad in grads], 1)
    total = lax.psum_scatter(
        packed.reshape(-1, D), ("stream", "dp"), scatter_dimension=0, tiled=True
    ).astype(jnp.float32)
    return own_pieces(total, shapes_of(grads, parts))


def own_pieces(total, shapes):
    pieces = []
    offset = 0
    for own, side in shapes:
        pieces.append(from_rows(total[None], offset, own, side))
        offset += own * side
    return pieces


def feed_grads(place, former, latter, given, source, keep, send, held):
    step = pl.program_id(0)
    core = place[0] & 1
    low = place[0] >> 1

    @pl.when(step < 4)
    def down():
        whole_grad = contract(former[...], given[...], 0, 0)
        rows = whole_grad.shape[0] // 8
        for pair in range(4):
            there = (4 * step + pair) ^ low
            first = whole_grad[2 * pair * rows : (2 * pair + 1) * rows]
            second = whole_grad[(2 * pair + 1) * rows : (2 * pair + 2) * rows]
            keep[there, 0:rows] = jnp.where(core == 0, first, second).astype(keep.dtype)
            send[there, 0:rows] = jnp.where(core == 0, second, first).astype(send.dtype)

    rows = D // held.shape[0]
    for number in range(4):

        @pl.when(step == 4 + number)
        def up():
            whole_grad = contract(source[...], latter[...], 0, 0)
            held[:, number * rows : number * rows + rows] = whole_grad.reshape(-1, rows, D)

    @pl.when(step == 7)
    def finish():
        start = 4 * rows
        for pair in range(held.shape[0] // 2):
            first, second = held[2 * pair], held[2 * pair + 1]
            there = pair ^ low
            keep[there, start:] = jnp.where(core == 0, first, second).astype(keep.dtype)
            send[there, start:] = jnp.where(core == 0, second, first).astype(send.dtype)


def run_feed_grads(active, ffn_grad, normed, hidden_grad):
    length, wide = active.shape
    parts = lax.axis_size("dp") * lax.axis_size("stream")
    pairs = parts // 2
    high = 2 * wide // parts
    half = jax.ShapeDtypeStruct((pairs, high, D), jnp.bfloat16)
    whole_half = pl.BlockSpec(half.shape, lambda step, place: (0, 0, 0))
    kept_rows = pl.BlockSpec((length, D), lambda step, place: (0, 0))
    return pl.pallas_call(
        feed_grads,
        grid_spec=pltpu.PrefetchScalarGridSpec(
            num_scalar_prefetch=1,
            grid=(8,),
            in_specs=[
                pl.BlockSpec((length, D), lambda step, place: (0, jnp.minimum(step, 3))),
                pl.BlockSpec((length, D), lambda step, place: (0, jnp.maximum(step - 4, 0))),
                kept_rows,
                kept_rows,
            ],
            out_specs=[whole_half, whole_half],
            scratch_shapes=[pltpu.VMEM((parts, high // 2, D), jnp.float32)],
        ),
        out_shape=[half, half],
        compiler_params=params(56),
        cost_estimate=spent(16),
    )(my_place(), active, hidden_grad, ffn_grad, normed)


def scatter_chain(grads, halving=False):
    parts = lax.axis_size("dp") * lax.axis_size("stream")
    shapes = shapes_of(grads, parts)
    if not in_pairs(shapes):
        return scatter_whole(grads)
    total = yield from halves_chain(*core_halves(grads, shapes, parts), False, halving)
    return own_pieces(total, shapes)


def core_halves(grads, shapes, parts):
    pairs = parts // 2
    high = sum(rows * side for rows, side in shapes)
    half = jax.ShapeDtypeStruct((pairs, high, D), jnp.bfloat16)
    return pl.pallas_call(
        functools.partial(apart, shapes),
        grid_spec=pltpu.PrefetchScalarGridSpec(
            num_scalar_prefetch=1,
            grid=(pairs // 4,),
            in_specs=[natural_block(shape) for shape in shapes],
            out_specs=[turned_block(high)] * 2,
        ),
        out_shape=[half, half],
        compiler_params=pltpu.CompilerParams(vmem_limit_bytes=16 << 20),
        cost_estimate=spent(4),
    )(my_place(), *[grad.astype(jnp.bfloat16) for grad in grads])


def halves_chain(kept, sent, split=False, halving=False):
    high = kept.shape[1]
    kept, other = yield (kept, swap(sent, 1))
    top = pair_bits()
    far = 1 << (top - 2)
    corner = 1 << top
    near = [(1, 0), (0, 1), (1, 1)]
    quarter = jax.ShapeDtypeStruct((far, high, D), jnp.bfloat16)
    views = [
        pl.BlockSpec((1, 1, 1, high, D), lambda row, x=x, y=y: (x, row, y, 0, 0))
        for x, y in [(0, 0)] + near
    ]
    total, *sent = pl.pallas_call(
        sum_quarters,
        grid=(far,),
        in_specs=views + views,
        out_specs=[pl.BlockSpec((1, high, D), lambda row: (row, 0, 0))] * 4,
        out_shape=[jax.ShapeDtypeStruct(quarter.shape, jnp.float32)] + [quarter] * 3,
        compiler_params=pltpu.CompilerParams(vmem_limit_bytes=16 << 20),
        cost_estimate=spent(3),
    )(*[kept.reshape(2, far, 2, high, D)] * 4, *[other.reshape(2, far, 2, high, D)] * 4)
    got = [swap(sent[0], corner), swap(sent[1], 2)]
    if split:
        total, last, *got = yield (total, sent[2], *got)
        total, got, last = yield (total, got, swap(last, corner | 2))
    else:
        total, last, *got = yield (total, swap(sent[2], corner | 2), *got)
    total = total + sum(block.astype(jnp.float32) for block in [last, *got])
    while halving and far > 1:
        far //= 2
        kept, other = yield (total[:far], swap(total[far:].astype(jnp.bfloat16), far << 2))
        total = kept + other.astype(jnp.float32)
    if halving:
        return total[0]
    others = [
        swap(total[number].astype(jnp.bfloat16), number << 2) for number in range(1, far)
    ]
    kept, *others = yield (total[0], *others)
    return kept + sum(other.astype(jnp.float32) for other in others)


def sum_quarters(*refs):
    for former, latter, out in zip(refs[:4], refs[4:8], refs[8:]):
        total = former[0, 0, 0].astype(jnp.float32) + latter[0, 0, 0].astype(jnp.float32)
        out[0] = total.astype(out.dtype)


def feed_chain(halves, shapes, split, halving):
    if not in_pairs(shapes):
        return scatter_whole(halves)
    total = yield from halves_chain(*halves, split, halving)
    return own_pieces(total, shapes)


def swap_chain(block):
    other = yield swap(block, lax.axis_size("dp"))
    return other


def product(former, latter):
    return jnp.dot(former, latter, preferred_element_type=jnp.float32)


def inner_rows(former, latter):
    return lax.dot_general(
        former, latter, (((0,), (0,)), ((), ())), preferred_element_type=jnp.float32
    )


def inner_cols(former, latter):
    return lax.dot_general(
        former, latter, (((1,), (1,)), ((), ())), preferred_element_type=jnp.float32
    )


def norm_gain(values, scales):
    center = jnp.mean(values, axis=-1, keepdims=True)
    shifted = values - center
    spread = jnp.mean(shifted * shifted, axis=-1, keepdims=True)
    return shifted * lax.rsqrt(spread + 1e-05) * scales


def rows_before(matrix):
    return jnp.concatenate([jnp.zeros_like(matrix[:1]), matrix[:-1]], 0)


def rows_after(matrix):
    return jnp.concatenate([matrix[1:], jnp.zeros_like(matrix[:1])], 0)


def char_segments(ends, char_count):
    places = lax.broadcasted_iota(jnp.int32, (ends.shape[0], char_count), 1)
    return jnp.sum((ends[:, None] <= places).astype(jnp.int32), axis=0)


def step_rates():
    return (
        0.5 * D ** (-0.5),
        0.5 * (3 * D // LEN) ** (-0.5),
        0.5 * D ** (-0.5),
        0.5 * FF ** (-0.5),
        0.5 * D ** (-0.5),
        0.5 * (6 * D) ** (-0.5),
        0.5,
        0.2,
    )


def adamw(master, first_m, second_m, grad_sum, step_rate):
    mean_new = 0.5 * first_m + 0.5 * grad_sum
    power = 0.5 * second_m + 0.5 * grad_sum * grad_sum
    correct = 1.0 - 0.5**STEP
    fresh_w = master - step_rate * (
        mean_new / correct / (jnp.sqrt(power / correct) + 1e-08) + 0.01 * master
    )
    return (fresh_w, mean_new, power)


STEP_ROWS = 512


def spent(microseconds):
    return pl.CostEstimate(
        flops=int(microseconds * 1e9), bytes_accessed=1, transcendentals=0
    )


UNROLL = 16


def contract(former, latter, left, right):
    return lax.dot_general(
        former, latter, (((left,), (right,)), ((), ())), preferred_element_type=jnp.float32
    )


def lane_blocks(width):
    blocks = []
    for number in range(2 * width // 128):
        side, lane = divmod(number * 128, width)
        blocks.append((number * 128, 2 * side * width + lane, 4 * side + lane // 128))
    return blocks


def eight(offset):
    return pl.ds(pl.multiple_of(offset, 8), 8)


def chars_ahead(rows_f, rows_b, ends, table, w_gru, shares, letters, before, pooled, running, spans, carry):
    block = pl.program_id(0)
    total = rows_f.shape[0]
    width = w_gru.shape[1] // 4

    @pl.when(block == 0)
    def start():
        logits = jnp.dot(table[...], w_gru[...], preferred_element_type=jnp.float32)
        letters[...] = jnp.zeros_like(letters)
        carry[...] = jnp.zeros_like(carry)
        for _, left, place in lane_blocks(width):
            update = jax.nn.sigmoid(logits[:, left : left + 128])
            letters[:, place, :] = 1.0 - update
            letters[:, 8 + place, :] = update * logits[:, left + width : left + width + 128]

    leading = lax.broadcasted_iota(jnp.int32, (8, 128), 0) < 4

    def several(group, held):
        state, total_state = held
        first = block * STEP_ROWS + group * UNROLL
        factors, adds = [], []
        for inner in range(UNROLL):
            id_f, id_b = rows_f[first + inner], rows_b[first + inner]
            factors.append(jnp.where(leading, letters[id_f, 0:8], letters[id_b, 0:8]))
            adds.append(jnp.where(leading, letters[id_f, 8:16], letters[id_b, 8:16]))
        for inner in range(UNROLL):
            before[group * UNROLL + inner] = state
            running[first + inner] = total_state
            state = factors[inner] * state + adds[inner]
            total_state = total_state + state
        return state, total_state

    state, total_state = lax.fori_loop(0, STEP_ROWS // UNROLL, several, (carry[0], carry[1]))
    carry[0] = state
    carry[1] = total_state

    @pl.when(block == pl.num_programs(0) - 1)
    def finish():
        running[total] = total_state

        def tokens(group, prior):
            found = []
            for inner in range(UNROLL):
                end = ends[group * UNROLL + inner]
                found.append(jnp.where(leading, running[end], -running[total - end]))
            for inner in range(UNROLL):
                spans[group * UNROLL + inner] = found[inner] - prior
                prior = found[inner]
            return prior

        lax.fori_loop(0, ends.shape[0] // UNROLL, tokens, jnp.where(leading, running[0], -running[total]))
        for at, _, place in lane_blocks(width):
            pooled[:, at : at + 128] = (spans[:, place, :] * shares[...]).astype(pooled.dtype)


def chars_back(blocks, opening, closing, *refs):
    rows_f, rows_b, owners_f, owners_b, letters, before = refs[:6]
    rest = list(refs[6:])
    take = lambda count: [rest.pop(0) for _ in range(count)]
    if opening:
        upstream, shares = take(2)
    else:
        spread, carry_in, *sums_in = take(6)
    if closing:
        position, table, w_gru = take(3)
    if opening:
        (spread,) = take(1)
    if closing:
        grad_gru, grad_table = take(2)
    else:
        carry_out, *sums_out = take(5)
    *sums, carry = take(5)
    if closing:
        (full,) = take(1)
    sums_f, sums_b, more_f, more_b = sums
    step_number = pl.program_id(0)
    block = blocks[0] - 1 - step_number
    width = 384

    @pl.when(step_number == 0)
    def start():
        if opening:
            for held in sums:
                held[...] = jnp.zeros_like(held)
            carry[...] = jnp.zeros_like(carry)
            for at, _, place in lane_blocks(width):
                spread[:, place, :] = upstream[:, at : at + 128] * shares[...]
            for place in (3, 7):
                spread[:, place, :] = jnp.zeros((spread.shape[0], 128), jnp.float32)
        else:
            for held, given in zip(sums, sums_in):
                held[...] = given[...]
            carry[...] = carry_in[...]

    leading = lax.broadcasted_iota(jnp.int32, (8, 128), 0) < 4

    def several(group, passed):
        steps = [STEP_ROWS - 1 - group * UNROLL - inner for inner in range(UNROLL)]
        kept, given, priors, owned = [], [], [], []
        for step in steps:
            place = block * STEP_ROWS + step
            id_f, id_b = rows_f[place], rows_b[place]
            owned.append((id_f, id_b))
            kept.append(jnp.where(leading, letters[id_f, 0:8], letters[id_b, 0:8]))
            given.append(jnp.where(leading, spread[owners_f[place]], spread[owners_b[place]]))
            priors.append(before[step])
        for inner in range(UNROLL):
            carried = given[inner] + passed
            passed = kept[inner] * carried
            moved = carried * priors[inner]
            id_f, id_b = owned[inner]
            for held, row, value in (
                (
                    (sums_f, more_f)[inner % 2],
                    id_f,
                    jnp.where(leading, carried, pltpu.roll(moved, 4, 0)),
                ),
                (
                    (sums_b, more_b)[inner % 2],
                    id_b,
                    jnp.where(leading, pltpu.roll(carried, 4, 0), moved),
                ),
            ):
                held[row] += value
        return passed

    carry[...] = lax.fori_loop(0, STEP_ROWS // UNROLL, several, carry[...])

    @pl.when(step_number == pl.num_programs(0) - 1)
    def finish():
        if not closing:
            carry_out[...] = carry[...]
            for held, given in zip(sums, sums_out):
                given[...] = held[...]
            return
        sums_f[...] += more_f[...]
        sums_b[...] += more_b[...]
        for _, left, place in lane_blocks(width):
            found = sums_f if place < 4 else sums_b
            lane = place % 4
            kept = letters[:, place, :]
            update = 1.0 - kept
            total = found[:, lane, :]
            full[:, left : left + 128] = kept * (
                letters[:, 8 + place, :] * total - update * found[:, 4 + lane, :]
            )
            full[:, left + width : left + width + 128] = update * total
        found = full[...].astype(jnp.bfloat16)
        whole_gru = contract(table[...], found, 0, 0)
        whole_table = contract(found, w_gru[...], 1, 1)
        if grad_gru.shape[0] == whole_gru.shape[0]:
            grad_gru[...] = whole_gru.astype(grad_gru.dtype)
            grad_table[...] = whole_table.astype(grad_table.dtype)
            return
        pairs = grad_gru.shape[0]
        high, low = whole_gru.shape[0] // (2 * pairs), whole_table.shape[0] // (2 * pairs)
        core = position[0] & 1
        for pair in range(pairs):
            halves = []
            for side in range(2):
                at = 2 * pair + side
                rows = whole_gru[at * high : at * high + high]
                halves.append(
                    jnp.concatenate(
                        [rows[:, :D], rows[:, D:], whole_table[at * low : at * low + low]], 0
                    )
                )
            there = pair ^ (position[0] >> 1)
            grad_gru[there] = jnp.where(core == 0, halves[0], halves[1]).astype(grad_gru.dtype)
            grad_table[there] = jnp.where(core == 0, halves[1], halves[0]).astype(grad_table.dtype)


def whole(array):
    return pl.BlockSpec(array.shape, lambda block: (0,) * len(array.shape))


def scalars():
    return pl.BlockSpec(memory_space=pltpu.SMEM)


def run_chars(ids, ends, table, w_gru, shares):
    total, count = ids.shape[0], shares.shape[0]
    f32 = jnp.float32
    outs = (
        jax.ShapeDtypeStruct((table.shape[0], 16, 128), f32),
        jax.ShapeDtypeStruct((total, 8, 128), f32),
        jax.ShapeDtypeStruct((count, w_gru.shape[1] // 2), jnp.bfloat16),
    )
    return pl.pallas_call(
        chars_ahead,
        grid=(total // STEP_ROWS,),
        in_specs=[scalars(), scalars(), scalars(), whole(table), whole(w_gru), whole(shares)],
        out_specs=[
            whole(outs[0]),
            pl.BlockSpec((STEP_ROWS, 8, 128), lambda block: (block, 0, 0)),
            whole(outs[2]),
        ],
        out_shape=outs,
        scratch_shapes=[
            pltpu.VMEM((total + 1, 8, 128), f32),
            pltpu.VMEM((count, 8, 128), f32),
            pltpu.VMEM((2, 8, 128), f32),
        ],
        compiler_params=pltpu.CompilerParams(vmem_limit_bytes=44 << 20),
        cost_estimate=spent(24),
    )(ids, jnp.flip(ids), ends, table, w_gru, shares)


def letter_shapes(ends, parts):
    return [(ends[1].shape[0] // parts, ends[1].shape[1] // D), (ends[0].shape[0] // parts, 1)]


def run_chars_back(last, count, ids, owners, letters, before, *, upstream=None, held=None, ends=None):
    f32 = jnp.float32
    tile = jax.ShapeDtypeStruct((letters.shape[0], 8, 128), f32)
    flat = jax.ShapeDtypeStruct((8, 128), f32)
    inputs = [ids, jnp.flip(ids), owners, jnp.flip(owners), letters, before]
    blocks = [scalars()] * 4 + [
        whole(letters),
        pl.BlockSpec((STEP_ROWS, 8, 128), lambda block: (last - 1 - block, 0, 0)),
    ]
    outs = []
    if upstream is not None:
        inputs += upstream
        outs.append(jax.ShapeDtypeStruct((upstream[0].shape[0], 8, 128), f32))
    else:
        inputs += held
    if ends is not None:
        inputs += [my_place()] + ends
        parts = lax.axis_size("dp") * lax.axis_size("stream")
        if in_pairs(letter_shapes(ends, parts)):
            high = sum(rows * side for rows, side in letter_shapes(ends, parts))
            outs += [jax.ShapeDtypeStruct((parts // 2, high, D), jnp.bfloat16)] * 2
        else:
            outs += [jax.ShapeDtypeStruct(array.shape, jnp.bfloat16) for array in ends[::-1]]
    else:
        outs += [flat] + [tile] * 4
    blocks += [scalars() if array.shape == (1,) else whole(array) for array in inputs[6:]]
    scratch = [pltpu.VMEM(tile.shape, f32)] * 4 + [pltpu.VMEM(flat.shape, f32)]
    if ends is not None:
        scratch.append(pltpu.VMEM((ends[0].shape[0], ends[1].shape[1]), f32))
    return pl.pallas_call(
        functools.partial(chars_back, (last,), upstream is not None, ends is not None),
        grid=(count,),
        in_specs=blocks,
        out_specs=[whole(out) for out in outs],
        out_shape=outs,
        scratch_shapes=scratch,
        compiler_params=pltpu.CompilerParams(vmem_limit_bytes=40 << 20),
        cost_estimate=spent(1),
    )(*inputs)


def attend(queries, key_rows, value_rows, context, logsum):
    size = key_rows.shape[1] // 2
    lanes = lax.broadcasted_iota(jnp.int32, (1, 2 * size), 1)
    scale = size ** (-0.5)
    parts = []
    sums = []
    for head in range(2):
        own = (lanes < size) if head == 0 else (lanes >= size)
        scores = contract(jnp.where(own, queries[...], 0) * scale, key_rows[...], 1, 1)
        row_max = jnp.max(scores, axis=-1, keepdims=True)
        exponent = jnp.exp(scores - row_max)
        row_total = jnp.sum(exponent, axis=-1, keepdims=True)
        parts.append(
            contract(exponent.astype(jnp.bfloat16), value_rows[...], 1, 0) * (1.0 / row_total)
        )
        sums.append(row_max + jnp.log(row_total))
    context[...] = jnp.where(lanes < size, parts[0], parts[1]).astype(context.dtype)
    turned = jnp.transpose(jnp.where(lanes < size, sums[0], sums[1]))
    logsum[0:8, :] = turned[0:8]
    logsum[8:16, :] = turned[size : size + 8]


def attend_back(queries, key_rows, value_rows, logsum, grads, qkv_grad):
    size = key_rows.shape[1] // 2
    lanes = lax.broadcasted_iota(jnp.int32, (1, 2 * size), 1)
    scale = size ** (-0.5)
    parts = []
    key_sum, value_sum = 0.0, 0.0
    for head in range(2):
        own = (lanes < size) if head == 0 else (lanes >= size)
        own_rows = jnp.where(own, queries[...], 0) * scale
        own_grads = jnp.where(own, grads[...], 0)
        scores = contract(key_rows[...], own_rows, 1, 1)
        probs = jnp.exp(scores - logsum[8 * head : 8 * head + 1, :])
        value_sum = value_sum + contract(probs.astype(jnp.bfloat16), own_grads, 1, 0)
        prob_grad = contract(value_rows[...], own_grads, 1, 1)
        center = jnp.sum(prob_grad * probs, axis=0, keepdims=True)
        score_grad = (probs * (prob_grad - center)).astype(jnp.bfloat16)
        key_sum = key_sum + contract(score_grad, own_rows, 1, 0)
        parts.append(contract(score_grad, key_rows[...], 0, 0))
    query_sum = jnp.where(lanes < size, parts[0], parts[1]) * scale
    for number, total in enumerate((query_sum, key_sum, value_sum)):
        at = number * (qkv_grad.shape[1] // 3) + pl.program_id(0) * 2 * size
        qkv_grad[:, pl.ds(pl.multiple_of(at, 2 * size), 2 * size)] = total.astype(qkv_grad.dtype)


def column(rows, width, offset):
    return pl.BlockSpec((rows, width), lambda pair: (0, offset + pair))


def run_attend(qkv, first, pairs):
    length, across = qkv.shape
    every = across // 384
    return pl.pallas_call(
        attend,
        grid=(pairs,),
        in_specs=[column(length, 128, every * part + first) for part in range(3)],
        out_specs=[column(length, 128, 0), pl.BlockSpec((16, length), lambda pair: (pair, 0))],
        out_shape=(
            jax.ShapeDtypeStruct((length, 128 * pairs), jnp.bfloat16),
            jax.ShapeDtypeStruct((16 * pairs, length), jnp.float32),
        ),
        compiler_params=pltpu.CompilerParams(vmem_limit_bytes=28 << 20),
        cost_estimate=spent(5 * pairs),
    )(qkv, qkv, qkv)


def run_attend_back(qkv, logsum, grads, first):
    length, across = qkv.shape
    pairs = across // 384
    return pl.pallas_call(
        attend_back,
        grid=(pairs,),
        in_specs=[column(length, 128, pairs * part) for part in range(3)]
        + [pl.BlockSpec((16, length), lambda pair: (pair, 0)), column(length, 128, first)],
        out_specs=pl.BlockSpec((length, across), lambda pair: (0, 0)),
        out_shape=jax.ShapeDtypeStruct((length, across), jnp.bfloat16),
        compiler_params=pltpu.CompilerParams(vmem_limit_bytes=30 << 20),
        cost_estimate=spent(1),
    )(qkv, qkv, qkv, logsum, grads)


CHUNK = 512
SLOPE = 0.7978845608028654


def gelu_pair(values):
    square = values * values
    curve = jnp.tanh(SLOPE * values * (1.0 + 0.044715 * square))
    half = 0.5 * (1.0 + curve)
    slope = half + (0.5 * SLOPE) * values * (1.0 - curve * curve) * (1.0 + 3 * 0.044715 * square)
    return values * half, slope


def unit(values):
    center = jnp.mean(values, axis=-1, keepdims=True)
    shifted = values - center
    spread = jnp.mean(shifted * shifted, axis=-1, keepdims=True)
    root = lax.rsqrt(spread + 1e-05)
    return shifted * root, root


def unit_back(normal, root, given):
    return (
        given
        - jnp.mean(given, axis=-1, keepdims=True)
        - normal * jnp.mean(given * normal, axis=-1, keepdims=True)
    ) * root


def column_sum(values):
    return jnp.sum(values.reshape(-1, 8, values.shape[1]), axis=0)


def feed_ahead(mixed, gains, up, down, summed, feature):
    normal, _ = unit(mixed[...])
    normed = normal * gains[0:1]
    hidden = contract(normed.astype(jnp.bfloat16), up[...], 1, 0)
    active, _ = gelu_pair(hidden)
    total = normed + contract(active.astype(jnp.bfloat16), down[...], 1, 0)
    summed[...] = total
    normal, _ = unit(total)
    feature[...] = (normal * gains[1:2]).astype(feature.dtype)


def feed_back(
    mixed, summed, feature_grad, gains, up, down, out,
    active_out, hidden_grad, ffn_out, normed_out, mixed_grad, attended, context_grad, gain_sums
):
    @pl.when(pl.program_id(0) == 0)
    def start():
        gain_sums[...] = jnp.zeros_like(gain_sums)

    normal, root = unit(summed[...])
    given = feature_grad[...].astype(jnp.float32)
    gain_sums[8:16] += column_sum(given * normal)
    summed_grad = unit_back(normal, root, given * gains[1:2])
    ffn_grad = summed_grad.astype(jnp.bfloat16)
    ffn_out[...] = ffn_grad
    normal, root = unit(mixed[...])
    normed = (normal * gains[0:1]).astype(jnp.bfloat16)
    normed_out[...] = normed
    hidden = contract(normed, up[...], 1, 0)
    active, slope = gelu_pair(hidden)
    active_out[...] = active.astype(jnp.bfloat16)
    hidden_grad[...] = (slope * contract(ffn_grad, down[...], 1, 1)).astype(jnp.bfloat16)
    normed_grad = summed_grad + contract(hidden_grad[...], up[...], 1, 1)
    gain_sums[0:8] += column_sum(normed_grad * normal)
    total = unit_back(normal, root, normed_grad * gains[0:1])
    mixed_grad[...] = total
    attended[...] = total.astype(jnp.bfloat16)
    context_grad[...] = contract(attended[...], out[...], 1, 1).astype(jnp.bfloat16)


def blend_both(
    order, feature, pooled, mine, theirs, gains, blend,
    result, feature_grad, state_grad, grads, gain_sum, early, middle, late, spread, total
):
    length = feature.shape[0]
    pair = 2 * D
    rows = 128
    chunks = [slice(at, at + rows) for at in range(0, length, rows)]

    def ahead(number):
        return contract(feature[...], blend[number * pair : number * pair + D, :], 1, 0) + contract(
            pooled[...], blend[number * pair + D : number * pair + pair, :], 1, 0
        )

    edge = jnp.zeros((8, D), jnp.float32)
    early[0:8] = edge
    late[length : length + 8] = edge
    spread[0:8] = edge
    spread[length + 8 : length + 16] = edge
    early[8 : length + 8] = ahead(0)
    middle[...] = ahead(1)
    late[0:length] = ahead(2)
    gain_sum[...] = jnp.zeros_like(gain_sum)
    for chunk in chunks:
        before = slice(chunk.start + 7, chunk.stop + 7)
        after = slice(chunk.start + 1, chunk.stop + 1)
        blended, slope = gelu_pair(middle[chunk] + early[before] + late[after])
        normal, root = unit(feature[chunk].astype(jnp.float32) + blended)
        result[chunk] = (normal * gains[2:3]).astype(result.dtype)
        half = length // 2
        within = slice(chunk.start % half, chunk.start % half + rows)
        given = jnp.where(
            order[0] == chunk.start // half,
            mine[within].astype(jnp.float32),
            theirs[within].astype(jnp.float32),
        )
        gain_sum[...] += column_sum(given * normal)
        whole_grad = unit_back(normal, root, given * gains[2:3])
        total[chunk] = whole_grad
        spread[slice(chunk.start + 8, chunk.stop + 8)] = whole_grad * slope
    for chunk in chunks:
        for number, offset in ((0, 9), (1, 8), (2, 7)):
            grads[chunk, number * D : number * D + D] = spread[
                slice(chunk.start + offset, chunk.stop + offset)
            ].astype(jnp.bfloat16)

    def back(left):
        return sum(
            contract(
                grads[:, number * D : number * D + D],
                blend[number * pair + left : number * pair + left + D, :],
                1,
                1,
            )
            for number in range(3)
        )

    feature_grad[...] = (total[...] + back(0)).astype(feature_grad.dtype)
    state_grad[...] = back(D)


def params(size):
    return pltpu.CompilerParams(vmem_limit_bytes=size << 20)


def rows_block(width):
    return pl.BlockSpec((CHUNK, width), lambda step: (step, 0))


def fixed(*shape):
    return pl.BlockSpec(shape, lambda step: (0,) * len(shape), pipeline_mode=pl.Buffered(1))


def run_feed(mixed, gains, up, down):
    length = mixed.shape[0]
    wide = up.shape[1]
    return pl.pallas_call(
        feed_ahead,
        grid=(length // CHUNK,),
        in_specs=[rows_block(D), fixed(3, D), fixed(D, wide), fixed(wide, D)],
        out_specs=[rows_block(D), rows_block(D)],
        out_shape=[
            jax.ShapeDtypeStruct((length, D), jnp.float32),
            jax.ShapeDtypeStruct((length, D), jnp.bfloat16),
        ],
        compiler_params=params(56),
        cost_estimate=spent(18),
    )(mixed, gains, up, down)


def run_feed_back(mixed, summed, feature_grad, gains, up, down, out):
    length = mixed.shape[0]
    wide = up.shape[1]
    bf = jnp.bfloat16
    f32 = jnp.float32
    widths = [(wide, bf), (wide, bf), (D, bf), (D, bf), (D, f32), (D, bf), (D, bf)]
    return pl.pallas_call(
        feed_back,
        grid=(length // CHUNK,),
        in_specs=[rows_block(D)] * 3 + [fixed(3, D), fixed(D, wide), fixed(wide, D), fixed(D, D)],
        out_specs=[rows_block(width) for width, _ in widths] + [fixed(16, D)],
        out_shape=[jax.ShapeDtypeStruct((length, width), kind) for width, kind in widths]
        + [jax.ShapeDtypeStruct((16, D), f32)],
        compiler_params=params(60),
        cost_estimate=spent(32),
    )(mixed, summed, feature_grad, gains, up, down, out)


def run_blend(order, feature, pooled, mine, theirs, gains, blend):
    length = feature.shape[0]
    bf = jnp.bfloat16
    f32 = jnp.float32
    return pl.pallas_call(
        blend_both,
        in_specs=[scalars()] + [pl.BlockSpec(memory_space=pltpu.VMEM)] * 6,
        out_shape=[
            jax.ShapeDtypeStruct((length, D), bf),
            jax.ShapeDtypeStruct((length, D), bf),
            jax.ShapeDtypeStruct((length, D), f32),
            jax.ShapeDtypeStruct((length, 3 * D), bf),
            jax.ShapeDtypeStruct((8, D), f32),
        ],
        scratch_shapes=[
            pltpu.VMEM((length + 8, D), f32),
            pltpu.VMEM((length, D), f32),
            pltpu.VMEM((length + 8, D), f32),
            pltpu.VMEM((length + 16, D), f32),
            pltpu.VMEM((length, D), f32),
        ],
        compiler_params=params(60),
        cost_estimate=spent(26),
    )(order, feature, pooled, mine, theirs, gains, blend)


def blend_weight_grad(feature, pooled, grads, out):
    out[0:D, :] = contract(feature[...], grads[...], 0, 0).astype(out.dtype)
    out[D : 2 * D, :] = contract(pooled[...], grads[...], 0, 0).astype(out.dtype)


def run_blend_grad(feature, pooled, grads):
    length = feature.shape[0]
    return pl.pallas_call(
        blend_weight_grad,
        grid=(3,),
        in_specs=[
            fixed(length, D),
            fixed(length, D),
            pl.BlockSpec((length, D), lambda third: (0, third)),
        ],
        out_specs=pl.BlockSpec((2 * D, D), lambda third: (third, 0)),
        out_shape=jax.ShapeDtypeStruct((6 * D, D), jnp.bfloat16),
        compiler_params=params(48),
        cost_estimate=spent(12),
    )(feature, pooled, grads)


def group_grads(
    place, tokens, first, second, third, context, attended, gains, mixed, early, middle, late,
    keep, send, tokens_grad, held
):
    total = mixed[...]
    for grads, weight in ((first, early), (second, middle), (third, late)):
        total = total + contract(grads[...], weight[...], 1, 1)
    tokens_grad[...] = total.astype(tokens_grad.dtype)
    pairs, high, _ = keep.shape
    rows = D // (2 * pairs)
    pieces = [(tokens, first), (tokens, second), (tokens, third), (context, attended)]
    for number, (former, latter) in enumerate(pieces):
        whole_grad = contract(former[...], latter[...], 0, 0)
        held[:, number * rows : number * rows + rows] = whole_grad.reshape(2 * pairs, rows, D)
    held[:, 4 * rows :] = jnp.broadcast_to(gains[...][None], (2 * pairs, 8, D))
    core = place[0] & 1
    for pair in range(pairs):
        there = pair ^ (place[0] >> 1)
        former, latter = held[2 * pair], held[2 * pair + 1]
        keep[there] = jnp.where(core == 0, former, latter).astype(keep.dtype)
        send[there] = jnp.where(core == 0, latter, former).astype(send.dtype)


def run_group_grads(tokens, qkv_grads, context, attended, gains, mixed, weights):
    parts = lax.axis_size("dp") * lax.axis_size("stream")
    high = 4 * (D // parts) + 8
    half = jax.ShapeDtypeStruct((parts // 2, high, D), jnp.bfloat16)
    inputs = (tokens, *qkv_grads, context, attended, gains, mixed, *weights)
    return pl.pallas_call(
        group_grads,
        grid=(1,),
        in_specs=[scalars()] + [fixed(*array.shape) for array in inputs],
        out_specs=[fixed(*half.shape)] * 2 + [fixed(*tokens.shape)],
        out_shape=[half, half, jax.ShapeDtypeStruct(tokens.shape, jnp.bfloat16)],
        scratch_shapes=[pltpu.VMEM((parts, high, D), jnp.float32)],
        compiler_params=params(60),
        cost_estimate=spent(1),
    )(my_place(), *inputs)


def on_device(
    tokens_in,
    char_ids,
    char_lengths,
    out_grad,
    w_qkv,
    first_qkv,
    second_qkv,
    w_out,
    first_out,
    second_out,
    w_up,
    first_up,
    second_up,
    w_down,
    first_down,
    second_down,
    w_gru,
    first_gru,
    second_gru,
    w_blend,
    first_blend,
    second_blend,
    char_table,
    first_table,
    second_table,
    gains,
    first_gains,
    second_gains,
):
    masters = (w_qkv, w_out, w_up, w_down, w_gru, w_blend, char_table, gains)
    firsts = (
        first_qkv,
        first_out,
        first_up,
        first_down,
        first_gru,
        first_blend,
        first_table,
        first_gains,
    )
    seconds = (
        second_qkv,
        second_out,
        second_up,
        second_down,
        second_gru,
        second_blend,
        second_table,
        second_gains,
    )
    parts = lax.axis_size("stream") * lax.axis_size("dp")
    on_first = lax.axis_index("stream") == 0
    half_len = tokens_in.shape[1]
    flow = Flow()

    def both_halves(pair, got):
        kept = jnp.where(on_first, pair[0], pair[1])
        return jnp.where(
            on_first, jnp.concatenate([kept, got], 0), jnp.concatenate([got, kept], 0)
        )

    ids_row = jnp.where(on_first, char_ids[0], char_ids[1])
    lengths_row = jnp.where(on_first, char_lengths[0], char_lengths[1])

    queries = HEADS // 2
    groups = 3
    pairs = queries // groups
    wide = 128 * pairs
    everyone = ("stream", "dp")
    by_group = w_qkv.reshape(w_qkv.shape[0], 3, groups, -1).transpose(0, 2, 1, 3)
    by_group = by_group.reshape(w_qkv.shape[0], groups, -1)
    flow.begin("tokens", swap_chain(jnp.where(on_first, tokens_in[1], tokens_in[0])), [4])
    flow.begin("group0", gather_steps([by_group[:, 0]], False))
    flow.begin("group1", gather_steps([by_group[:, 1]], True))
    flow.slot(())
    flow.slot(())
    flow.begin("group2", gather_steps([by_group[:, 2], w_out], True))
    flow.begin("up", gather_steps([w_up], True), [0, 1, 0, 1, 0])
    flow.slot(())
    shards = flow.slot((char_table, w_gru, gains_rows(gains), w_blend))
    shapes = shapes_of(shards[:3], 1)
    packed = jnp.concatenate([to_rows(shard, 1)[0] for shard in shards[:3]], 0)
    rest = lax.all_gather(packed, everyone, axis=0, tiled=False)
    blend_all = lax.all_gather(
        shards[3].astype(jnp.bfloat16), everyone, axis=0, tiled=True
    )
    flow.begin("down", gather_steps([w_down], True), [0, 0, 1, 0, 0])
    flow.slot(())
    tokens = both_halves(tokens_in, flow.end("tokens"))
    weights, parts_qkv, contexts, logsums = [], [], [], []
    for number in range(groups):
        w_group, *w_more = flow.end("group%d" % number)
        if number == 2:
            shares = 1.0 / lengths_row.astype(jnp.float32)[:, None]
            ends = jnp.cumsum(lengths_row)
            segment = char_segments(ends, ids_row.shape[0])
            lengths_row = (segment, shares, ends)
        qkv = product(tokens, w_group).astype(jnp.bfloat16)
        context, logsum = run_attend(qkv, 0, pairs)
        qkv, context, logsum, tokens, lengths_row = flow.slot(
            (qkv, context, logsum, tokens, lengths_row)
        )
        weights.append(w_group)
        parts_qkv.append(qkv)
        contexts.append(context)
        logsums.append(logsum)
    (out_all,) = w_more
    segment, shares, ends = lengths_row
    context = jnp.concatenate(contexts, 1)
    table_all, gru_all, gain_all = unpack_rows(rest, shapes)
    gain_all = jnp.sum(gain_all.reshape(parts, 8, D)[:, :3].astype(jnp.float32), 0)
    letters, before, pooled = run_chars(ids_row, ends, table_all, gru_all, shares)
    letters, before, pooled, context, tokens = flow.slot((letters, before, pooled, context, tokens))
    mixed_sum = tokens.astype(jnp.float32) + product(context, out_all)
    mixed_sum, gain_all = flow.slot((mixed_sum, gain_all))
    flow.begin("out_grad", swap_chain(jnp.where(on_first, out_grad[1], out_grad[0])))
    (up_all,) = flow.end("up")
    (down_all,) = flow.end("down")
    summed, feature = run_feed(mixed_sum, gain_all, up_all, down_all)
    summed, feature, blend_all = flow.slot((summed, feature, blend_all))
    result, feature_grad, state_grad, blend_grads, gain_blend = run_blend(
        lax.axis_index("stream").reshape(1),
        feature,
        pooled,
        jnp.where(on_first, out_grad[0], out_grad[1]),
        flow.end("out_grad"),
        gain_all,
        blend_all,
    )
    grad_blend = run_blend_grad(feature, pooled, blend_grads)
    result, grad_blend, feature_grad = flow.slot((result, grad_blend, feature_grad))
    (blend_sum,) = scatter_whole([grad_blend])
    flow.begin("result", swap_chain(jnp.where(on_first, result[half_len:], result[:half_len])))
    active, hidden_grad, ffn_grad, normed, mixed_grad, attended_grad, context_grad, gain_sums = (
        run_feed_back(mixed_sum, summed, feature_grad, gain_all, up_all, down_all, out_all)
    )
    gain_grads = jnp.concatenate(
        [jnp.sum(sums, 0, keepdims=True) for sums in (gain_sums[:8], gain_sums[8:], gain_blend)], 0
    )
    gain_grads = jnp.pad(gain_grads, ((0, 5), (0, 0)))
    if in_pairs([(w_down.shape[0], 1), (w_up.shape[0], 4)]):
        feed_grad = run_feed_grads(active, ffn_grad, normed, hidden_grad)
    else:
        feed_grad = [
            inner_rows(active, ffn_grad).astype(jnp.bfloat16),
            inner_rows(normed, hidden_grad).astype(jnp.bfloat16),
        ]
    feed_grad, state_grad, context_grad, gain_grads = flow.slot(
        (feed_grad, state_grad, context_grad, gain_grads)
    )
    flow.begin(
        "feed",
        feed_chain(feed_grad, [(w_down.shape[0], 1), (w_up.shape[0], 4)], True, True),
        [0, 0, 0, 0, 1],
    )
    qkv_grads = []
    for number in range(groups):
        qkv_grad = run_attend_back(
            parts_qkv[number], logsums[number], context_grad, pairs * number
        )
        if number == 0:
            qkv_grad, context_grad, state_grad = flow.slot((qkv_grad, context_grad, state_grad))
        qkv_grads.append(qkv_grad)
    qkv_shapes = [(w_qkv.shape[0], 1)] * 3 + [(w_out.shape[0], 1), (8, 1)]
    if in_pairs(qkv_shapes):
        *qkv_halves, tokens_grad = run_group_grads(
            tokens, qkv_grads, context, attended_grad, gain_grads, mixed_grad, weights
        )
    else:
        tokens_grad = mixed_grad + sum(
            inner_cols(grad, weight) for grad, weight in zip(qkv_grads, weights)
        )
        tokens_grad = tokens_grad.astype(jnp.bfloat16)
        qkv_halves = [inner_rows(tokens, grad).astype(jnp.bfloat16) for grad in qkv_grads]
        qkv_halves.append(inner_rows(context, attended_grad).astype(jnp.bfloat16))
        gain_rows = jnp.broadcast_to(gain_grads[None], (parts, 8, D)).astype(jnp.bfloat16)
        qkv_halves.append(gain_rows.reshape(8 * parts, D))
    qkv_halves, tokens_grad = flow.slot((qkv_halves, tokens_grad))
    flow.begin("qkv", feed_chain(qkv_halves, qkv_shapes, False, True), [0, 0, 1, 0])
    blocks = ids_row.shape[0] // STEP_ROWS
    spread, *held = run_chars_back(
        blocks, blocks // 2, ids_row, segment, letters, before, upstream=[state_grad, shares]
    )
    spread, held, blend_sum = flow.slot((spread, held, blend_sum))
    grad_gru, grad_table = run_chars_back(
        blocks // 2,
        blocks // 2,
        ids_row,
        segment,
        letters,
        before,
        held=[spread, *held],
        ends=[table_all, gru_all],
    )
    grad_gru, grad_table, tokens_grad = flow.slot((grad_gru, grad_table, tokens_grad))
    flow.begin(
        "letters",
        feed_chain([grad_gru, grad_table], letter_shapes([table_all, gru_all], parts), False, False),
    )
    flow.begin(
        "tokens",
        swap_chain(jnp.where(on_first, tokens_grad[half_len:], tokens_grad[:half_len])),
        [1],
    )
    while flow.live:
        flow.slot(())
    own_result = jnp.where(on_first, result[:half_len], result[half_len:])
    own_grad = jnp.where(on_first, tokens_grad[:half_len], tokens_grad[half_len:])
    back_result, back_grad = flow.end("result"), flow.end("tokens")
    block_parts = [
        jnp.where(on_first, own_result, back_result),
        jnp.where(on_first, back_result, own_result),
    ]
    grad_parts = [
        jnp.where(on_first, own_grad, back_grad),
        jnp.where(on_first, back_grad, own_grad),
    ]
    *group_sums, out_sum, gain_sum = flow.end("qkv")
    group_sums = jnp.stack(group_sums, 1)
    qkv_sum = group_sums.reshape(w_qkv.shape[0], groups, 3, -1).transpose(0, 2, 1, 3)
    letter_sums = flow.end("letters")
    feed_sums = flow.end("feed")
    sums = (
        qkv_sum.reshape(w_qkv.shape),
        out_sum,
        feed_sums[1],
        feed_sums[0],
        letter_sums[0],
        blend_sum,
        letter_sums[1],
        lax.dynamic_slice(
            gain_sum, (0, my_place()[0] * gains.shape[1]), gains.shape
        ),
    )
    rates = step_rates()
    results = [
        adamw(masters[number], firsts[number], seconds[number], sums[number], rates[number])
        for number in range(8)
    ]
    return (
        jnp.stack(block_parts),
        jnp.stack(grad_parts),
        results[0][0],
        results[0][1],
        results[0][2],
        results[1][0],
        results[1][1],
        results[1][2],
        results[2][0],
        results[2][1],
        results[2][2],
        results[3][0],
        results[3][1],
        results[3][2],
        results[4][0],
        results[4][1],
        results[4][2],
        results[5][0],
        results[5][1],
        results[5][2],
        results[6][0],
        results[6][1],
        results[6][2],
        results[7][0],
        results[7][1],
        results[7][2],
    )


def solution(mesh):
    in_specs = (
        P("dp", "stream", None),
        P("dp", None),
        P("dp", None),
        P("dp", "stream", None),
        P(("stream", "dp"), None),
        P(("stream", "dp"), None),
        P(("stream", "dp"), None),
        P(("stream", "dp"), None),
        P(("stream", "dp"), None),
        P(("stream", "dp"), None),
        P(("stream", "dp"), None),
        P(("stream", "dp"), None),
        P(("stream", "dp"), None),
        P(("stream", "dp"), None),
        P(("stream", "dp"), None),
        P(("stream", "dp"), None),
        P(("stream", "dp"), None),
        P(("stream", "dp"), None),
        P(("stream", "dp"), None),
        P(("stream", "dp"), None),
        P(("stream", "dp"), None),
        P(("stream", "dp"), None),
        P(("stream", "dp"), None),
        P(("stream", "dp"), None),
        P(("stream", "dp"), None),
        P(None, ("stream", "dp")),
        P(None, ("stream", "dp")),
        P(None, ("stream", "dp")),
    )
    out_specs = (
        P("dp", "stream", None),
        P("dp", "stream", None),
        P(("stream", "dp"), None),
        P(("stream", "dp"), None),
        P(("stream", "dp"), None),
        P(("stream", "dp"), None),
        P(("stream", "dp"), None),
        P(("stream", "dp"), None),
        P(("stream", "dp"), None),
        P(("stream", "dp"), None),
        P(("stream", "dp"), None),
        P(("stream", "dp"), None),
        P(("stream", "dp"), None),
        P(("stream", "dp"), None),
        P(("stream", "dp"), None),
        P(("stream", "dp"), None),
        P(("stream", "dp"), None),
        P(("stream", "dp"), None),
        P(("stream", "dp"), None),
        P(("stream", "dp"), None),
        P(("stream", "dp"), None),
        P(("stream", "dp"), None),
        P(("stream", "dp"), None),
        P(None, ("stream", "dp")),
        P(None, ("stream", "dp")),
        P(None, ("stream", "dp")),
    )
    return jax.shard_map(
        on_device, mesh=mesh, in_specs=in_specs, out_specs=out_specs, check_vma=False
    )
```
